128 devices in a mesh: lat: 4 (over y_hi, core), lon: 32 (over x, z, y_lo).
Axes of the slice: x: 4, y: 4 (y_hi: 2, y_lo: 2; y = y_hi * 2 + y_lo), z: 4, core: 2. Of those that a mesh axis runs over, the one named last changes fastest.
Arguments:
- node_latents: bfloat16 [8, 96, 64, 512], P('lat', 'lon'), may hold values from -6 to 6
- edge_latents: bfloat16 [4, 32, 3072, 512], P('lat', 'lon'), may hold values from -6 to 6
- senders: int32 [4, 32, 3072], P('lat', 'lon'), may hold values from 0 to 3327, as said below
- receivers: int32 [4, 32, 3072], P('lat', 'lon'), may hold values from 0 to 383
- edge_count: int32 [4, 32], P('lat', 'lon'), may hold values from 1536 to 3072, as said below
- edge_self_w: bfloat16 [512, 512], replicated, may hold values from -0.25 to 0.25
- edge_send_w: bfloat16 [512, 512], replicated, may hold values from -0.25 to 0.25
- edge_recv_w: bfloat16 [512, 512], replicated, may hold values from -0.25 to 0.25
- edge_out_w: bfloat16 [512, 512], replicated, may hold values from -0.25 to 0.25
- node_self_w: bfloat16 [512, 512], replicated, may hold values from -0.25 to 0.25
- node_aggr_w: bfloat16 [512, 512], replicated, may hold values from -0.25 to 0.25
- node_out_w: bfloat16 [512, 512], replicated, may hold values from -0.25 to 0.25
- edge_gain: float32 [512], replicated, may hold values from 0.1 to 1.9
- node_gain: float32 [512], replicated, may hold values from 0.1 to 1.9
- node_upstream: bfloat16 [8, 96, 64, 512], P('lat', 'lon'), may hold values from -6 to 6
- edge_upstream: bfloat16 [4, 32, 3072, 512], P('lat', 'lon'), may hold values from -6 to 6
Outputs:
- node_update: bfloat16 [8, 96, 64, 512], P('lat', 'lon')
- edge_update: bfloat16 [4, 32, 3072, 512], P('lat', 'lon')
- node_grads: float32 [8, 96, 64, 512], P('lat', 'lon')
- edge_grads: float32 [4, 32, 3072, 512], P('lat', 'lon')
The draws below stay inside these ranges and needn't reach their ends.
Inputs may be any that keep to these rules, and one draw needn't show every extreme that they name: A sender below 1280 lies in the receiver's block or one of the eight blocks around it, never in a block row outside the grid; a sender of 1280 or more names coarse node senders - 1280. Exactly 768 slots of each tile name coarse nodes, and at most 6 slots of one tile name coarse nodes of any one tile. `edge_count`: the tiles of the first and last latitude band have all 3072 slots live.
All inputs are finite; a program needn't handle non-finite values.
Results may differ from the reference program's by a relative error of at most 0.013.
Values may be sent and summed in bfloat16 or wider, within the bound.
A program may use at most 192 MiB of HBM per device.

```python
import jax
import jax.numpy as jnp
from jax import lax

D = 512
BLOCK = 64
BLAT = 2
BLON = 3
EDGE_DEV = 3072
COARSE_DEV = 16
BANDS = 4
SECTORS = 32
NODE_DEV = 384
EXT_ROWS = 1280
COARSE_ALL = 2048


def edge_lists(key):
    key = jax.random.fold_in(key, 11)
    keys = jax.random.split(key, 7)
    shape = (BANDS, SECTORS, EDGE_DEV)
    tile_count = BANDS * SECTORS
    receiver_ids = jax.random.randint(keys[0], shape, 0, BLAT * BLON * BLOCK)
    first_slot = jnp.arange(tile_count * EDGE_DEV).reshape(shape) == 0
    receiver_ids = jnp.where(first_slot, BLAT * BLON * BLOCK - 1, receiver_ids)
    block_index = receiver_ids // BLOCK
    block_row = block_index // BLON
    block_col = block_index % BLON
    row_step = jax.random.randint(keys[1], shape, -1, 2)
    col_step = jax.random.randint(keys[2], shape, -1, 2)
    band_index = jnp.arange(BANDS)[:, None, None]
    global_row = band_index * BLAT + block_row + row_step
    outside = jnp.logical_or(global_row < 0, global_row >= BANDS * BLAT)
    row_step = jnp.where(outside, 0, row_step)
    member = jax.random.randint(keys[3], shape, 0, BLOCK)
    near_ids = ((block_row + 1 + row_step) * (BLON + 2) + (block_col + 1 + col_step)) * BLOCK + member
    tile_keys = jax.random.split(keys[4], tile_count)
    rank = jax.vmap(lambda one: jax.random.permutation(one, EDGE_DEV))(tile_keys).reshape(shape)
    long_edge = rank < EDGE_DEV // 4
    tile_zero = (jnp.arange(tile_count) == 0).reshape(BANDS, SECTORS, 1)
    shift = jax.random.randint(keys[5], (BANDS, SECTORS, 1), 0, tile_count)
    shift = jnp.where(tile_zero, tile_count - 1, shift)
    owner = (rank + shift) % tile_count
    coarse_member = jax.random.randint(keys[6], shape, 0, COARSE_DEV)
    top_slot = jnp.logical_and(tile_zero, rank == 0)
    coarse_member = jnp.where(top_slot, COARSE_DEV - 1, coarse_member)
    far_ids = EXT_ROWS + owner * COARSE_DEV + coarse_member
    sender_ids = jnp.where(long_edge, far_ids, near_ids)
    return (sender_ids.astype(jnp.int32), receiver_ids.astype(jnp.int32))


def draw_senders(key, part):
    return edge_lists(key)[0]


def draw_receivers(key, part):
    return edge_lists(key)[1]


def draw_edge_count(key, part):
    key = jax.random.fold_in(key, 5)
    counts = jax.random.randint(key, (BANDS, SECTORS), EDGE_DEV // 2, EDGE_DEV + 1)
    band_index = jnp.arange(BANDS)[:, None]
    polar = jnp.logical_or(band_index == 0, band_index == BANDS - 1)
    return jnp.where(polar, EDGE_DEV, counts).astype(jnp.int32)


def shard_levels(key, extent, shards, low, high):
    def one(axis_at, parts):
        heights = jax.random.uniform(jax.random.fold_in(jax.random.fold_in(key, 6), axis_at), (parts,), jnp.float32, low / len(shards), high / len(shards))
        return jnp.repeat(jnp.exp(heights), extent[axis_at] // parts).reshape((-1,) + (1,) * (len(extent) - axis_at - 1))

    gain = one(*shards[0])
    for cut in shards[1:]:
        gain = gain * one(*cut)
    return gain


def gaussian(rng, dims, spread, limit, pieces=(), held_as=jnp.bfloat16):
    entries = spread * jax.random.normal(rng, dims, jnp.float32)
    if pieces:
        entries = entries * shard_levels(rng, dims, pieces, -0.22, 0.18)
    return jnp.clip(entries, -limit, limit).astype(held_as)


def setup_inputs(seed: int = 0) -> dict:
    streams_of = jax.random.split(jax.random.key(seed), 17)
    node_latents = gaussian(streams_of[0], (BANDS * BLAT, SECTORS * BLON, BLOCK, D), 1.0, 6.0, ((0, 4), (1, 32)))
    edge_latents = gaussian(streams_of[1], (BANDS, SECTORS, EDGE_DEV, D), 1.0, 6.0, ((0, 4), (1, 32)))
    senders = draw_senders(jax.random.fold_in(streams_of[16], 71), 0)
    receivers = draw_receivers(jax.random.fold_in(streams_of[16], 71), 0)
    edge_count = draw_edge_count(jax.random.fold_in(streams_of[16], 71), 0)
    edge_self_w = gaussian(streams_of[5], (D, D), D ** -0.5, 0.25)
    edge_send_w = gaussian(streams_of[6], (D, D), D ** -0.5, 0.25)
    edge_recv_w = gaussian(streams_of[7], (D, D), D ** -0.5, 0.25)
    edge_out_w = gaussian(streams_of[8], (D, D), D ** -0.5, 0.25)
    node_self_w = gaussian(streams_of[9], (D, D), D ** -0.5, 0.25)
    node_aggr_w = gaussian(streams_of[10], (D, D), D ** -0.5, 0.25)
    node_out_w = gaussian(streams_of[11], (D, D), D ** -0.5, 0.25)
    edge_gain = jnp.clip(1.0 + 0.18 * jax.random.normal(streams_of[12], (D,), jnp.float32), 0.1, 1.9)
    node_gain = jnp.clip(1.0 + 0.18 * jax.random.normal(streams_of[13], (D,), jnp.float32), 0.1, 1.9)
    node_upstream = gaussian(streams_of[14], (BANDS * BLAT, SECTORS * BLON, BLOCK, D), 1.0, 6.0, ((0, 4), (1, 32)))
    edge_upstream = gaussian(streams_of[15], (BANDS, SECTORS, EDGE_DEV, D), 1.0, 6.0, ((0, 4), (1, 32)))
    return {"node_latents": node_latents, "edge_latents": edge_latents, "senders": senders, "receivers": receivers, "edge_count": edge_count, "edge_self_w": edge_self_w, "edge_send_w": edge_send_w, "edge_recv_w": edge_recv_w, "edge_out_w": edge_out_w, "node_self_w": node_self_w, "node_aggr_w": node_aggr_w, "node_out_w": node_out_w, "edge_gain": edge_gain, "node_gain": node_gain, "node_upstream": node_upstream, "edge_upstream": edge_upstream}


EPSILON = 1e-05

def matmul(left, right):
    return jnp.dot(left, right, preferred_element_type=jnp.float32)

def layer_norm(hidden):
    center = hidden - lax.optimization_barrier(jnp.mean(hidden, -1, keepdims=True))
    inv_std = lax.rsqrt(lax.optimization_barrier(jnp.mean(center * center, -1, keepdims=True)) + EPSILON)
    return (center * inv_std, inv_std)

def norm_back(grad_out, normed, inv_std):
    mean_grad = lax.optimization_barrier(jnp.mean(grad_out, -1, keepdims=True))
    mean_cross = lax.optimization_barrier(jnp.mean(grad_out * normed, -1, keepdims=True))
    return inv_std * (grad_out - mean_grad - normed * mean_cross)

def silu_grad(pre_act):
    sigmoid = jax.nn.sigmoid(pre_act)
    return sigmoid * (1.0 + pre_act * (1.0 - sigmoid))

def local_pass(edge_rows, sender_term, recv_rows, live_mask, flat_nodes, receiver_ids, up_nodes, up_edges, weights, gains):
    self_w, recv_w, out_w, node_w, aggr_w, node_out = weights
    edge_gain, node_gain = gains
    edge_pre = matmul(edge_rows, self_w) + sender_term + matmul(recv_rows, recv_w)
    edge_act = jax.nn.silu(edge_pre).astype(jnp.bfloat16)
    edge_normed, edge_rstd = layer_norm(matmul(edge_act, out_w))
    message = (live_mask * edge_normed * edge_gain).astype(jnp.bfloat16)
    edge_new = (edge_rows.astype(jnp.float32) + message.astype(jnp.float32)).astype(jnp.bfloat16)
    aggregate = jnp.zeros(flat_nodes.shape, jnp.float32).at[receiver_ids].add(message.astype(jnp.float32)).astype(jnp.bfloat16)
    node_pre = matmul(flat_nodes, node_w) + matmul(aggregate, aggr_w)
    node_act = jax.nn.silu(node_pre).astype(jnp.bfloat16)
    node_normed, node_rstd = layer_norm(matmul(node_act, node_out))
    node_new = (flat_nodes.astype(jnp.float32) + node_normed * node_gain).astype(jnp.bfloat16)
    up_node32 = up_nodes.astype(jnp.float32)
    up_edge32 = up_edges.astype(jnp.float32)
    node_hidden_grad = norm_back(up_node32 * node_gain, node_normed, node_rstd).astype(jnp.bfloat16)
    node_pre_grad = (matmul(node_hidden_grad, node_out.T) * silu_grad(node_pre)).astype(jnp.bfloat16)
    node_grad = up_node32 + matmul(node_pre_grad, node_w.T)
    aggregate_grad = matmul(node_pre_grad, aggr_w.T)
    message_grad = live_mask * (up_edge32 + aggregate_grad[receiver_ids])
    edge_hidden_grad = norm_back(message_grad * edge_gain, edge_normed, edge_rstd).astype(jnp.bfloat16)
    pre_grad = (matmul(edge_hidden_grad, out_w.T) * silu_grad(edge_pre)).astype(jnp.bfloat16)
    edge_grad = up_edge32 + matmul(pre_grad, self_w.T)
    node_grad = node_grad.at[receiver_ids].add(matmul(pre_grad, recv_w.T))
    return (edge_new, node_new, edge_grad, node_grad, pre_grad)

def reference(node_latents, edge_latents, senders, receivers, edge_count, edge_self_w, edge_send_w, edge_recv_w, edge_out_w, node_self_w, node_aggr_w, node_out_w, edge_gain, node_gain, node_upstream, edge_upstream):
    weights = (edge_self_w, edge_recv_w, edge_out_w, node_self_w, node_aggr_w, node_out_w)
    gains = (edge_gain, node_gain)
    node_grid = node_latents.reshape(BANDS, BLAT, SECTORS, BLON, BLOCK, D)
    coarse = node_grid[:, 0, :, 0, :COARSE_DEV].reshape(COARSE_ALL, D)
    wrapped = jnp.concatenate([node_latents[:, -1:], node_latents, node_latents[:, :1]], axis=1)
    padded = jnp.pad(wrapped, ((1, 1), (0, 0), (0, 0), (0, 0)))
    tile_count = BANDS * SECTORS

    def to_tiles(grid_array):
        return grid_array.reshape(BANDS, BLAT, SECTORS, BLON, BLOCK, D).transpose(0, 2, 1, 3, 4, 5).reshape(tile_count, NODE_DEV, D)

    def from_tiles(tile_array):
        return tile_array.reshape(BANDS, SECTORS, BLAT, BLON, BLOCK, D).transpose(0, 2, 1, 3, 4, 5).reshape(BANDS * BLAT, SECTORS * BLON, BLOCK, D)
    zero = jnp.zeros((), jnp.int32)
    tile_ids = jnp.arange(tile_count, dtype=jnp.int32)

    def tile_step(totals, inputs):
        grad_pad, grad_far = totals
        tile_index, flat_nodes, edge_rows, sender_ids, receiver_ids, count, up_nodes, up_edges = inputs
        band_row = tile_index // SECTORS * BLAT
        sector_col = tile_index % SECTORS * BLON
        corner = (band_row.astype(jnp.int32), sector_col.astype(jnp.int32), zero, zero)
        window = (BLAT + 2, BLON + 2, BLOCK, D)
        extended = lax.dynamic_slice(padded, corner, window)
        sender_table = jnp.concatenate([extended.reshape(EXT_ROWS, D), coarse], 0)
        sender_term = matmul(sender_table[sender_ids], edge_send_w)
        recv_rows = flat_nodes[receiver_ids]
        live_mask = (jnp.arange(EDGE_DEV) < count).astype(jnp.float32)[:, None]
        edge_new, node_new, edge_grad, node_grad, pre_grad = local_pass(edge_rows, sender_term, recv_rows, live_mask, flat_nodes, receiver_ids, up_nodes, up_edges, weights, gains)
        sender_grad = matmul(pre_grad, edge_send_w.T)
        table_grad = jnp.zeros((EXT_ROWS + COARSE_ALL, D), jnp.float32).at[sender_ids].add(sender_grad)
        rim_grad = table_grad[:EXT_ROWS].reshape(window)
        grad_pad = lax.dynamic_update_slice(grad_pad, lax.dynamic_slice(grad_pad, corner, window) + rim_grad, corner)
        grad_far = grad_far + table_grad[EXT_ROWS:]
        return ((grad_pad, grad_far), (node_new, edge_new, node_grad, edge_grad))
    inputs = (tile_ids, to_tiles(node_latents), edge_latents.reshape(tile_count, EDGE_DEV, D), senders.reshape(tile_count, EDGE_DEV), receivers.reshape(tile_count, EDGE_DEV), edge_count.reshape(tile_count), to_tiles(node_upstream), edge_upstream.reshape(tile_count, EDGE_DEV, D))
    start_totals = (jnp.zeros(padded.shape, jnp.float32), jnp.zeros((COARSE_ALL, D), jnp.float32))
    (grad_pad, grad_far), stacked = lax.scan(tile_step, start_totals, inputs)
    node_new, edge_new, node_grad, edge_grad = stacked
    inner_grad = grad_pad[1:-1]
    core_grad = inner_grad[:, 1:-1]
    core_grad = core_grad.at[:, -1].add(inner_grad[:, 0]).at[:, 0].add(inner_grad[:, -1])
    core_grad = core_grad.reshape(BANDS, BLAT, SECTORS, BLON, BLOCK, D)
    core_grad = core_grad.at[:, 0, :, 0, :COARSE_DEV].add(grad_far.reshape(BANDS, SECTORS, COARSE_DEV, D))
    node_grads = from_tiles(node_grad) + core_grad.reshape(BANDS * BLAT, SECTORS * BLON, BLOCK, D)
    node_update = from_tiles(node_new)
    edge_update = edge_new.reshape(BANDS, SECTORS, EDGE_DEV, D)
    edge_grads = edge_grad.reshape(BANDS, SECTORS, EDGE_DEV, D)
    return (node_update, edge_update, node_grads, edge_grads)
```

```python
import jax
import jax.numpy as jnp
from jax import lax
from jax.experimental import pallas as pl
from jax.experimental.pallas import tpu as pltpu
from jax.sharding import PartitionSpec as P

MESH = pl.DeviceIdType.MESH
F32 = jnp.float32
BF16 = jnp.bfloat16
EPSILON = 1e-05

D = 512
BLOCK = 64
SLOTS = 3072
NODES = 384
EXT = 1280
OWNERS = 128
MEMBERS = 16
COARSE = OWNERS * MEMBERS
PER_OWNER = 8
PACKED = OWNERS * PER_OWNER
RECV_AT = EXT + PACKED
TABLE = RECV_AT + NODES
STEP = 256
STEPS = SLOTS // STEP
LANES = 128
GROUP = 16
GROUPS = OWNERS // GROUP
LONS = 32
CHUNK = 8
VMEM_BYTES = 60 * 1024 * 1024


def dot(left, right):
    return jnp.dot(left, right, preferred_element_type=F32)


def dot_t(left, right):
    return lax.dot_general(left, right, (((1,), (1,)), ((), ())), preferred_element_type=F32)


def t_dot(left, right):
    return lax.dot_general(left, right, (((0,), (0,)), ((), ())), preferred_element_type=F32)


def onehot(mask):
    return jnp.where(mask, 1.0, 0.0).astype(BF16)


def mean(rows):
    return jnp.sum(rows, -1, keepdims=True) * (1.0 / D)


def sigmoid(pre):
    return 0.5 * jnp.tanh(0.5 * pre) + 0.5


def places():
    lat = lax.axis_index("lat")
    lon = lax.axis_index("lon")
    return lat, lon, lat % 2, lat // 2


def shifted(lat, lon, row, col):
    return {"lat": lax.rem(lat + row + 4, 4), "lon": lax.rem(lon + col + LONS, LONS)}


def greet(lat, lon, core, half):
    barrier = pltpu.get_barrier_semaphore()
    for row in (-1, 1):
        for col in (-1, 0, 1):
            pl.semaphore_signal(barrier, inc=1, device_id=shifted(lat, lon, row, col), device_id_type=MESH)

    def one(step, carry):
        peer = {
            "lat": lax.rem(half + step // LONS, 2) * 2 + core,
            "lon": lax.rem(lon + step, LONS),
        }
        pl.semaphore_signal(barrier, inc=1, device_id=peer, device_id_type=MESH)
        return carry

    lax.fori_loop(1, 2 * LONS, one, 0)
    pl.semaphore_wait(barrier, 6 + 2 * LONS - 1)


HALO = (
    ((-1, 0), (0, 1), (0, 3), (3, 1), (1, 3)),
    ((1, 0), (1, 1), (0, 3), (0, 1), (1, 3)),
    ((0, -1), (0, 2), (0, 1), (1, 2), (4, 1)),
    ((0, 1), (0, 2), (2, 1), (1, 2), (0, 1)),
    ((-1, -1), (0, 1), (0, 1), (3, 1), (4, 1)),
    ((-1, 1), (0, 1), (2, 1), (3, 1), (0, 1)),
    ((1, -1), (1, 1), (0, 1), (0, 1), (4, 1)),
    ((1, 1), (1, 1), (2, 1), (0, 1), (0, 1)),
)


def spread_kernel(nodes, ext, coarse, own_sem, halo_send, halo_recv, far_send, far_recv, pass_send, pass_recv):
    lat, lon, core, half = places()
    greet(lat, lon, core, half)
    mine = lat * LONS + lon
    first = nodes.at[0, 0, pl.ds(0, MEMBERS)]

    own = pltpu.make_async_copy(nodes, ext.at[pl.ds(1, 2), pl.ds(1, 3)], own_sem)
    own.start()
    kept = pltpu.make_async_copy(first, coarse.at[mine], far_recv.at[half, lon // CHUNK])
    kept.start()

    def far_copy(step):
        peer = {
            "lat": lax.rem(half + step // LONS, 2) * 2 + core,
            "lon": lax.rem(lon + step, LONS),
        }
        return pltpu.make_async_remote_copy(
            src_ref=first,
            dst_ref=coarse.at[mine],
            send_sem=far_send,
            recv_sem=far_recv.at[half, lon // CHUNK],
            device_id=peer,
            device_id_type=MESH,
        )

    def far_one(step, carry):
        far_copy(step).start()
        return carry

    lax.fori_loop(1, 2 * LONS, far_one, 0)

    halos = []
    for at, ((row, col), (r0, rn), (c0, cn), (er, ern), (ec, ecn)) in enumerate(HALO):
        copy = pltpu.make_async_remote_copy(
            src_ref=nodes.at[pl.ds(r0, rn), pl.ds(c0, cn)],
            dst_ref=ext.at[pl.ds(er, ern), pl.ds(ec, ecn)],
            send_sem=halo_send.at[at],
            recv_sem=halo_recv.at[at],
            device_id=shifted(lat, lon, row, col),
            device_id_type=MESH,
        )
        copy.start()
        halos.append(copy)

    partner = {"lat": half * 2 + 1 - core, "lon": lon}
    passes = []
    for far in range(2):
        for part in range(LONS // CHUNK):
            at = (far * 2 + core) * LONS + part * CHUNK
            block = coarse.at[pl.ds(at, CHUNK)]
            pltpu.make_async_copy(block, block, far_recv.at[far, part]).wait()
            copy = pltpu.make_async_remote_copy(
                src_ref=block,
                dst_ref=block,
                send_sem=pass_send.at[far, part],
                recv_sem=pass_recv.at[far, part],
                device_id=partner,
                device_id_type=MESH,
            )
            copy.start()
            passes.append(copy)
    own.wait()
    for copy in halos:
        copy.wait()
    for copy in passes:
        copy.wait()
    sent = coarse.at[pl.ds(0, 2 * LONS - 1)]
    pltpu.make_async_copy(sent, sent, far_send).wait()


def spread(nodes):
    return pl.pallas_call(
        spread_kernel,
        out_shape=(
            jax.ShapeDtypeStruct((4, 5, BLOCK, D), BF16),
            jax.ShapeDtypeStruct((OWNERS, MEMBERS, D), BF16),
        ),
        in_specs=[pl.BlockSpec(memory_space=pl.ANY)],
        out_specs=(pl.BlockSpec(memory_space=pl.ANY),) * 2,
        scratch_shapes=[
            pltpu.SemaphoreType.DMA,
            pltpu.SemaphoreType.DMA((8,)),
            pltpu.SemaphoreType.DMA((8,)),
            pltpu.SemaphoreType.DMA,
            pltpu.SemaphoreType.DMA((2, LONS // CHUNK)),
            pltpu.SemaphoreType.DMA((2, LONS // CHUNK)),
            pltpu.SemaphoreType.DMA((2, LONS // CHUNK)),
        ],
        compiler_params=pltpu.CompilerParams(collective_id=0, has_side_effects=True),
        name="spread",
    )(nodes)


BACK = (
    ((-1, 0), (0, 1), (1, 3)),
    ((1, 0), (3, 1), (1, 3)),
    ((0, -1), (1, 2), (0, 1)),
    ((0, 1), (1, 2), (4, 1)),
    ((-1, -1), (0, 1), (0, 1)),
    ((-1, 1), (0, 1), (4, 1)),
    ((1, -1), (3, 1), (0, 1)),
    ((1, 1), (3, 1), (4, 1)),
)


def collect_kernel(
    rim, far_grad, part, send_w, out,
    paired, summed, landed, rows_in, cols_in, corners_in, total,
    halo_send, halo_recv, pair_send, pair_recv, far_send, far_recv,
):
    lat, lon, core, half = places()
    greet(lat, lon, core, half)
    mine = half * LONS + lon
    partner = {"lat": half * 2 + 1 - core, "lon": lon}
    parts = LONS // CHUNK

    pairs = []
    for hop in range(2):
        for step in range(parts):
            far = lax.rem(half + hop, 2)
            group = lax.rem(lon // CHUNK + step, parts)
            at = (far * 2 + 1 - core) * LONS + group * CHUNK
            copy = pltpu.make_async_remote_copy(
                src_ref=far_grad.at[pl.ds(at, CHUNK)],
                dst_ref=paired.at[hop, step],
                send_sem=pair_send.at[hop, step],
                recv_sem=pair_recv.at[hop, step],
                device_id=partner,
                device_id_type=MESH,
            )
            copy.start()
            pairs.append((copy, hop, step, far, group))

    targets = [
        rows_in.at[pl.ds(1, 1)], rows_in.at[pl.ds(0, 1)],
        cols_in.at[1], cols_in.at[0],
        corners_in.at[3], corners_in.at[2], corners_in.at[1], corners_in.at[0],
    ]
    halos = []
    for at, ((row, col), (er, ern), (ec, ecn)) in enumerate(BACK):
        copy = pltpu.make_async_remote_copy(
            src_ref=rim.at[pl.ds(er, ern), pl.ds(ec, ecn)],
            dst_ref=targets[at],
            send_sem=halo_send.at[at],
            recv_sem=halo_recv.at[at],
            device_id=shifted(lat, lon, row, col),
            device_id_type=MESH,
        )
        copy.start()
        halos.append(copy)

    for copy, hop, step, far, group in pairs:
        copy.wait_recv()
        at = (far * 2 + core) * LONS + group * CHUNK
        summed[hop, step] = (
            far_grad[pl.ds(at, CHUNK)].astype(F32) + paired[hop, step].astype(F32)
        ).astype(BF16)
        for turn in range(CHUNK):
            place = lax.rem(lon + turn, CHUNK)
            to_lon = group * CHUNK + place
            source = summed.at[hop, step, place]

            def stay():
                pltpu.make_async_copy(source, landed.at[mine], far_recv).start()

            def go():
                pltpu.make_async_remote_copy(
                    src_ref=source,
                    dst_ref=landed.at[mine],
                    send_sem=far_send,
                    recv_sem=far_recv,
                    device_id={"lat": far * 2 + core, "lon": to_lon},
                    device_id_type=MESH,
                ).start()

            if hop == 0 and step == 0 and turn == 0:
                stay()
            else:
                go()

    total[...] = rim[1:3, 1:4].astype(F32)
    for copy in halos:
        copy.wait_recv()
    total[...] += rows_in[...].astype(F32)
    total[:, 0] += cols_in[0][:, 0].astype(F32)
    total[:, 2] += cols_in[1][:, 0].astype(F32)
    total[0, 0] += corners_in[0][0, 0].astype(F32)
    total[0, 2] += corners_in[1][0, 0].astype(F32)
    total[1, 0] += corners_in[2][0, 0].astype(F32)
    total[1, 2] += corners_in[3][0, 0].astype(F32)

    pltpu.make_async_copy(landed, landed, far_recv).wait()

    def add(at, acc):
        return acc + landed[at].astype(F32)

    total[0, 0, :MEMBERS] += lax.fori_loop(0, 2 * LONS, add, jnp.zeros((MEMBERS, D), F32))
    for row in range(2):
        for col in range(3):
            at = (row * 3 + col) * BLOCK
            out[at : at + BLOCK] = part[at : at + BLOCK] + dot_t(total[row, col].astype(BF16), send_w[...])

    for copy in halos:
        copy.wait_send()
    for copy, *_ in pairs:
        copy.wait_send()
    sent = landed.at[pl.ds(0, 2 * LONS - 1)]
    pltpu.make_async_copy(sent, sent, far_send).wait()


def collect(rim, far_grad, part, send_w):
    parts = LONS // CHUNK
    vmem = pl.BlockSpec(memory_space=pltpu.VMEM)
    return pl.pallas_call(
        collect_kernel,
        out_shape=jax.ShapeDtypeStruct((NODES, D), F32),
        in_specs=[vmem] * 4,
        out_specs=vmem,
        scratch_shapes=[
            pltpu.VMEM((2, parts, CHUNK, MEMBERS, D), BF16),
            pltpu.VMEM((2, parts, CHUNK, MEMBERS, D), BF16),
            pltpu.VMEM((2 * LONS, MEMBERS, D), BF16),
            pltpu.VMEM((2, 3, BLOCK, D), BF16),
            pltpu.VMEM((2, 2, 1, BLOCK, D), BF16),
            pltpu.VMEM((4, 1, 1, BLOCK, D), BF16),
            pltpu.VMEM((2, 3, BLOCK, D), F32),
            pltpu.SemaphoreType.DMA((8,)),
            pltpu.SemaphoreType.DMA((8,)),
            pltpu.SemaphoreType.DMA((2, parts)),
            pltpu.SemaphoreType.DMA((2, parts)),
            pltpu.SemaphoreType.DMA,
            pltpu.SemaphoreType.DMA,
        ],
        compiler_params=pltpu.CompilerParams(
            collective_id=1, has_side_effects=True, vmem_limit_bytes=VMEM_BYTES
        ),
        name="collect",
    )(rim, far_grad, part, send_w)


def layer_norm(hidden):
    center = hidden - mean(hidden)
    inv_std = lax.rsqrt(mean(center * center) + EPSILON)
    return center * inv_std, inv_std


def norm_back(grad_out, normed, inv_std):
    return inv_std * (grad_out - mean(grad_out) - normed * mean(grad_out * normed))


def layer_kernel(
    count, senders, receivers, ext, coarse, nodes, node_up, edges, edge_up,
    self_w, send_w, recv_w, out_w, node_w, aggr_w, node_out, edge_gain, node_gain,
    node_new, edge_new, node_grad, edge_grad, rim, far_grad,
    edges_v, up_v, new_v, grad_v, table, hot, packed, picks, requests, slot_of, normed_v, slope_v, rstd_v, pre_grad_v, aggr, aggr_grad,
    edges_sem, up_sem, new_sem, grad_sem,
):
    def rows_of(step):
        return pl.ds(pl.multiple_of(step * STEP, STEP), STEP)

    loads = []
    for step in range(STEPS):
        at = pl.ds(step * STEP, STEP)
        pltpu.make_async_copy(edges.at[at], edges_v.at[at], edges_sem.at[step]).start()
    for step in range(STEPS):
        at = pl.ds(step * STEP, STEP)
        pltpu.make_async_copy(edge_up.at[at], up_v.at[at], up_sem.at[step]).start()

    earlier = onehot(
        lax.broadcasted_iota(jnp.int32, (STEP, STEP), 0) < lax.broadcasted_iota(jnp.int32, (STEP, STEP), 1)
    )
    down = lax.broadcasted_iota(jnp.int32, (OWNERS, STEP), 0)
    requests[...] = jnp.zeros_like(requests)

    def rank_step(step, seen):
        at = rows_of(step)
        ids = senders[:, at]
        far = ids - EXT
        owner = jnp.right_shift(far, 4)
        mask = jnp.broadcast_to(owner, (OWNERS, STEP)) == down
        flags = jnp.where(mask, 1.0, 0.0)
        flags_16 = flags.astype(BF16)
        before = dot(flags_16, earlier) + seen
        rank = jnp.sum(flags * before, 0, keepdims=True).astype(jnp.int32)
        slot_of[0:1, at] = jnp.where(far >= 0, EXT + owner * PER_OWNER + rank, ids)
        member = jnp.where(far >= 0, jnp.bitwise_and(far, MEMBERS - 1) + 1, 0).astype(F32)
        chosen = jnp.where(jnp.broadcast_to(rank, (OWNERS, STEP)) == down, jnp.broadcast_to(member, (OWNERS, STEP)), 0.0)
        requests[...] += dot_t(flags_16, chosen.astype(BF16))
        return seen + jnp.sum(flags, 1, keepdims=True)

    lax.fori_loop(0, STEPS, rank_step, jnp.zeros((OWNERS, 1), F32))

    wide = jnp.broadcast_to(requests[...][:, None, :], (OWNERS, PER_OWNER, LANES)).reshape(PACKED, LANES)
    at_row = jnp.bitwise_and(lax.broadcasted_iota(jnp.int32, (PACKED, LANES), 0), PER_OWNER - 1)
    at_lane = lax.broadcasted_iota(jnp.int32, (PACKED, LANES), 1)
    wanted = jnp.sum(jnp.where(at_row == at_lane, wide, 0.0), 1, keepdims=True).astype(jnp.int32)
    span = GROUP * MEMBERS
    rows_in = lax.broadcasted_iota(jnp.int32, (PACKED, span), 0)
    cols_in = lax.broadcasted_iota(jnp.int32, (PACKED, span), 1)
    same = jnp.bitwise_and(jnp.right_shift(rows_in, 3), GROUP - 1) == jnp.right_shift(cols_in, 4)
    named = wanted == jnp.bitwise_and(cols_in, MEMBERS - 1) + 1
    picks[...] = onehot(jnp.logical_and(same, named))

    for at in range(0, EXT, STEP):
        table[at : at + STEP] = dot(ext[at : at + STEP], send_w[...]).astype(BF16)
    for at in range(0, NODES, LANES):
        table[RECV_AT + at : RECV_AT + at + LANES] = dot(nodes[at : at + LANES], recv_w[...]).astype(BF16)
    for group in range(GROUPS):
        at, span = group * GROUP * PER_OWNER, GROUP * MEMBERS
        packed[at : at + LANES] = dot(
            picks[at : at + LANES], coarse[group * span : (group + 1) * span]
        ).astype(BF16)
    for at in range(0, PACKED, STEP):
        table[EXT + at : EXT + at + STEP] = dot(packed[at : at + STEP], send_w[...]).astype(BF16)

    lane = lax.broadcasted_iota(jnp.int32, (STEP, LANES), 1)
    node_row = lax.broadcasted_iota(jnp.int32, (NODES, STEP), 0)
    slot_row = lax.broadcasted_iota(jnp.int32, (STEP, 1), 0)
    aggr[...] = jnp.zeros_like(aggr)

    def column(ids):
        return jnp.transpose(jnp.broadcast_to(ids, (LANES, STEP)))

    def live_of(step):
        return (slot_row + step * STEP < count[0, 0]).astype(F32)

    def forward(step, carry):
        at = rows_of(step)
        from_col = column(slot_of[0:1, at])
        to_col = column(receivers[:, at])
        for base in range(0, RECV_AT, LANES):
            hot[:, base : base + LANES] = onehot(from_col == lane + base)
        for base in range(0, NODES, LANES):
            hot[:, RECV_AT + base : RECV_AT + base + LANES] = onehot(to_col == lane + base)
        pltpu.make_async_copy(edges.at[at], edges_v.at[at], edges_sem.at[step]).wait()
        rows = edges_v[at]
        pre = dot(rows, self_w[...]) + dot(hot[...], table[...])
        gate = sigmoid(pre)
        act = pre * gate
        slope_v[at] = (gate + act * (1.0 - gate)).astype(BF16)
        normed, rstd = layer_norm(dot(act.astype(BF16), out_w[...]))
        normed_v[at] = normed.astype(BF16)
        rstd_v[at] = jnp.broadcast_to(rstd, (STEP, LANES))
        message = (live_of(step) * normed * edge_gain[...]).astype(BF16)
        new_v[at] = (rows.astype(F32) + message.astype(F32)).astype(BF16)
        pltpu.make_async_copy(new_v.at[at], edge_new.at[at], new_sem.at[step]).start()
        to_hot = onehot(jnp.broadcast_to(receivers[:, at], (NODES, STEP)) == node_row)
        aggr[...] += dot(to_hot, message)
        return carry

    lax.fori_loop(0, STEPS, forward, 0)

    node_rows = nodes[...]
    node_pre = dot(node_rows, node_w[...]) + dot(aggr[...].astype(BF16), aggr_w[...])
    gate = sigmoid(node_pre)
    act = node_pre * gate
    slope = gate + act * (1.0 - gate)
    normed, rstd = layer_norm(dot(act.astype(BF16), node_out[...]))
    node_new[...] = (node_rows.astype(F32) + normed * node_gain[...]).astype(BF16)
    up = node_up[...].astype(F32)
    hidden_grad = norm_back(up * node_gain[...], normed, rstd).astype(BF16)
    pre_grad = (dot_t(hidden_grad, node_out[...]) * slope).astype(BF16)
    node_grad[...] = up + dot_t(pre_grad, node_w[...])
    aggr_grad[...] = dot_t(pre_grad, aggr_w[...]).astype(BF16)

    def backward(step, carry):
        at = rows_of(step)
        to_col = column(receivers[:, at])
        for base in range(0, NODES, LANES):
            hot[:, base : base + LANES] = onehot(to_col == lane + base)
        pltpu.make_async_copy(edge_up.at[at], up_v.at[at], up_sem.at[step]).wait()
        upstream = up_v[at].astype(F32)
        grad = live_of(step) * (upstream + dot(hot[:, :NODES], aggr_grad[...])) * edge_gain[...]
        normed = normed_v[at].astype(F32)
        hidden_grad = norm_back(grad, normed, rstd_v[at][:, :1]).astype(BF16)
        pre_grad = (dot_t(hidden_grad, out_w[...]) * slope_v[at].astype(F32)).astype(BF16)
        pre_grad_v[at] = pre_grad
        grad_v[at] = upstream + dot_t(pre_grad, self_w[...])
        pltpu.make_async_copy(grad_v.at[at], edge_grad.at[at], grad_sem.at[step]).start()
        return carry

    lax.fori_loop(0, STEPS, backward, 0)

    def summed(ids, base, size):
        mask = jnp.broadcast_to(ids, (size, SLOTS)) == lax.broadcasted_iota(jnp.int32, (size, SLOTS), 0) + base
        return dot(onehot(mask), pre_grad_v[...])

    def rim_step(step, carry):
        at = rows_of(step)
        rim[at] = summed(slot_of[0:1, :], step * STEP, STEP).astype(BF16)
        return carry

    def far_step(step, carry):
        at = rows_of(step)
        packed[at] = summed(slot_of[0:1, :], EXT + step * STEP, STEP).astype(BF16)
        return carry

    lax.fori_loop(0, EXT // STEP, rim_step, 0)
    lax.fori_loop(0, PACKED // STEP, far_step, 0)
    for group in range(GROUPS):
        at, span = group * GROUP * PER_OWNER, GROUP * MEMBERS
        far_grad[group * span : (group + 1) * span] = t_dot(
            picks[at : at + LANES], packed[at : at + LANES]
        ).astype(BF16)

    def recv_step(step, carry):
        at = pl.ds(pl.multiple_of(step * LANES, LANES), LANES)
        got = summed(receivers[...], step * LANES, LANES).astype(BF16)
        node_grad[at] += dot_t(got, recv_w[...])
        return carry

    lax.fori_loop(0, NODES // LANES, recv_step, 0)

    for step in range(STEPS):
        at = pl.ds(step * STEP, STEP)
        pltpu.make_async_copy(new_v.at[at], edge_new.at[at], new_sem.at[step]).wait()
        pltpu.make_async_copy(grad_v.at[at], edge_grad.at[at], grad_sem.at[step]).wait()


def layer(count, senders, receivers, ext, coarse, nodes, node_up, edges, edge_up, weights, gains):
    vmem = pl.BlockSpec(memory_space=pltpu.VMEM)
    smem = pl.BlockSpec(memory_space=pltpu.SMEM)
    far = pl.BlockSpec(memory_space=pl.ANY)
    return pl.pallas_call(
        layer_kernel,
        out_shape=(
            jax.ShapeDtypeStruct((NODES, D), BF16),
            jax.ShapeDtypeStruct((SLOTS, D), BF16),
            jax.ShapeDtypeStruct((NODES, D), F32),
            jax.ShapeDtypeStruct((SLOTS, D), F32),
            jax.ShapeDtypeStruct((EXT, D), BF16),
            jax.ShapeDtypeStruct((COARSE, D), BF16),
        ),
        in_specs=[smem, vmem, vmem, vmem, vmem, vmem, vmem, far, far] + [vmem] * 9,
        out_specs=(vmem, far, vmem, far, vmem, vmem),
        scratch_shapes=[
            pltpu.VMEM((SLOTS, D), BF16),
            pltpu.VMEM((SLOTS, D), BF16),
            pltpu.VMEM((SLOTS, D), BF16),
            pltpu.VMEM((SLOTS, D), F32),
            pltpu.VMEM((TABLE, D), BF16),
            pltpu.VMEM((STEP, TABLE), BF16),
            pltpu.VMEM((PACKED, D), BF16),
            pltpu.VMEM((PACKED, GROUP * MEMBERS), BF16),
            pltpu.VMEM((OWNERS, LANES), F32),
            pltpu.VMEM((8, SLOTS), jnp.int32),
            pltpu.VMEM((SLOTS, D), BF16),
            pltpu.VMEM((SLOTS, D), BF16),
            pltpu.VMEM((SLOTS, LANES), F32),
            pltpu.VMEM((SLOTS, D), BF16),
            pltpu.VMEM((NODES, D), F32),
            pltpu.VMEM((NODES, D), BF16),
            pltpu.SemaphoreType.DMA((STEPS,)),
            pltpu.SemaphoreType.DMA((STEPS,)),
            pltpu.SemaphoreType.DMA((STEPS,)),
            pltpu.SemaphoreType.DMA((STEPS,)),
        ],
        compiler_params=pltpu.CompilerParams(vmem_limit_bytes=VMEM_BYTES),
        name="layer",
    )(count, senders, receivers, ext, coarse, nodes, node_up, edges, edge_up, *weights, *gains)


def body(
    node_latents,
    edge_latents,
    senders,
    receivers,
    edge_count,
    edge_self_w,
    edge_send_w,
    edge_recv_w,
    edge_out_w,
    node_self_w,
    node_aggr_w,
    node_out_w,
    edge_gain,
    node_gain,
    node_upstream,
    edge_upstream,
):
    ext, coarse = spread(node_latents)
    weights = (edge_self_w, edge_send_w, edge_recv_w, edge_out_w, node_self_w, node_aggr_w, node_out_w)
    gains = (edge_gain.reshape(1, D), node_gain.reshape(1, D))
    node_new, edge_new, node_grad, edge_grad, rim, far_grad = layer(
        edge_count,
        senders.reshape(1, SLOTS),
        receivers.reshape(1, SLOTS),
        ext.reshape(EXT, D),
        coarse.reshape(COARSE, D),
        node_latents.reshape(NODES, D),
        node_upstream.reshape(NODES, D),
        edge_latents.reshape(SLOTS, D),
        edge_upstream.reshape(SLOTS, D),
        weights,
        gains,
    )
    node_grads = collect(
        rim.reshape(4, 5, BLOCK, D), far_grad.reshape(OWNERS, MEMBERS, D), node_grad, edge_send_w
    )
    grid = node_latents.shape
    return (
        node_new.reshape(grid),
        edge_new.reshape(edge_latents.shape),
        node_grads.reshape(grid),
        edge_grad.reshape(edge_latents.shape),
    )


def solution(mesh):
    tiles = P("lat", "lon", None, None)
    lists = P("lat", "lon", None)
    return jax.shard_map(
        body,
        mesh=mesh,
        in_specs=(tiles, tiles, lists, lists, P("lat", "lon")) + (P(),) * 9 + (tiles, tiles),
        out_specs=(tiles,) * 4,
        check_vma=False,
    )
```

```python
import jax
import jax.numpy as jnp
from jax import lax
from jax.experimental import pallas as pl
from jax.experimental.pallas import tpu as pltpu
from jax.sharding import PartitionSpec as P

MESH = pl.DeviceIdType.MESH
F32 = jnp.float32
BF16 = jnp.bfloat16
EPSILON = 1e-05

D = 512
BLOCK = 64
SLOTS = 3072
NODES = 384
EXT = 1280
OWNERS = 128
MEMBERS = 16
COARSE = OWNERS * MEMBERS
PER_OWNER = 8
PACKED = OWNERS * PER_OWNER
STEP = 256
STEPS = SLOTS // STEP
LANES = 128
GROUP = 16
GROUPS = OWNERS // GROUP
LONS = 32
SAME_CORE = 64
RIM = 14 * BLOCK
VMEM_BYTES = 60 * 1024 * 1024


def dot(left, right):
    return jnp.dot(left, right, preferred_element_type=F32)


def dot_t(left, right):
    return lax.dot_general(left, right, (((1,), (1,)), ((), ())), preferred_element_type=F32)


def t_dot(left, right):
    return lax.dot_general(left, right, (((0,), (0,)), ((), ())), preferred_element_type=F32)


def onehot(mask):
    return jnp.where(mask, 1.0, 0.0).astype(BF16)


def mean(rows):
    return jnp.sum(rows, -1, keepdims=True) * (1.0 / D)


def sigmoid(pre):
    return 0.5 * jnp.tanh(0.5 * pre) + 0.5


def places():
    lat = lax.axis_index("lat")
    lon = lax.axis_index("lon")
    return lat, lon


def shifted(lat, lon, row, col):
    return {"lat": lax.rem(lat + row + 4, 4), "lon": lax.rem(lon + col + LONS, LONS)}


def rings(lat, lon):
    core, x, z = lat % 2, lon // 8, lon // 2 % 4
    y = lat // 2 * 2 + lon % 2
    near = z + core * (x - z)
    far = x + core * (z - x)

    def device(y_step, near_step, far_step):
        y_at = lax.rem(y + y_step, 4)
        x_at = lax.rem(x + far_step + core * (near_step - far_step), 4)
        z_at = lax.rem(z + near_step + core * (far_step - near_step), 4)
        return {"lat": y_at // 2 * 2 + core, "lon": x_at * 8 + z_at * 2 + y_at % 2}

    return core, y, near, far, device


def greet(lat, lon, device):
    peers = [shifted(lat, lon, row, col) for row in (-1, 0, 1) for col in (-1, 0, 1) if row or col]
    for step in (1, 2, 3):
        peers += [device(step, 0, 0), device(0, step, 0), device(0, 0, step)]
    for peer in peers:
        pl.semaphore_signal(pltpu.get_barrier_semaphore(), inc=1, device_id=peer, device_id_type=MESH)
    return len(peers)


def reaches(lat, row):
    return jnp.logical_and(lat + row >= 0, lat + row < 4)


RIM_BASES = (0, 64, 128, 192, 256, 960, 1024, 1088, 1152, 1216, 320, 640, 576, 896)
CORE_BASES = (384, 448, 512, 704, 768, 832)
HALO = (
    ((-1, 0), (0, (0, 3)), (6, 3)),
    ((1, 0), (1, (0, 3)), (1, 3)),
    ((0, -1), (None, 0), (12, 2)),
    ((0, 1), (None, 2), (10, 2)),
    ((-1, -1), (0, (0, 1)), (9, 1)),
    ((-1, 1), (0, (2, 1)), (5, 1)),
    ((1, -1), (1, (0, 1)), (4, 1)),
    ((1, 1), (1, (2, 1)), (0, 1)),
)
BACK = (
    ((-1, 0), (1, 3), (3, 3)),
    ((1, 0), (6, 3), (0, 3)),
    ((0, -1), (10, 2), (8, 2)),
    ((0, 1), (12, 2), (6, 2)),
    ((-1, -1), (0, 1), (13, 1)),
    ((-1, 1), (4, 1), (12, 1)),
    ((1, -1), (5, 1), (11, 1)),
    ((1, 1), (9, 1), (10, 1)),
)


def place_of(owner):
    core = jnp.bitwise_and(jnp.right_shift(owner, 5), 1)
    y = jnp.right_shift(owner, 6) * 2 + jnp.bitwise_and(owner, 1)
    x = jnp.bitwise_and(jnp.right_shift(owner, 3), 3)
    z = jnp.bitwise_and(jnp.right_shift(owner, 1), 3)
    place = jnp.where(core == 0, x * 16 + z * 4, SAME_CORE + z * 16 + x * 4) + y
    return jnp.where(owner < 0, owner, place)


def rows_of(step, size=STEP):
    return pl.ds(pl.multiple_of(step * size, size), size)


def column(ids):
    return jnp.transpose(jnp.broadcast_to(ids, (LANES, STEP)))


def lane_ids(first, second):
    lane = lax.broadcasted_iota(jnp.int32, (STEP, LANES), 1)
    return lane + jnp.where(lane < BLOCK, first, second - BLOCK)


def row_ids(bases):
    row = lax.broadcasted_iota(jnp.int32, (len(bases) * BLOCK, 1), 0)
    block = jnp.right_shift(row, 6)
    start = jnp.zeros_like(row)
    for at, base in enumerate(bases):
        start = jnp.where(block == at, base - at * BLOCK, start)
    return row + start


def rank_slots(senders, slot_of, requests, picks):
    earlier = onehot(
        lax.broadcasted_iota(jnp.int32, (STEP, STEP), 0) < lax.broadcasted_iota(jnp.int32, (STEP, STEP), 1)
    )
    down = lax.broadcasted_iota(jnp.int32, (OWNERS, STEP), 0)
    requests[...] = jnp.zeros_like(requests)

    def rank_step(step, seen):
        at = rows_of(step)
        ids = senders[:, at]
        far = ids - EXT
        owner = place_of(jnp.right_shift(far, 4))
        flags = jnp.where(jnp.broadcast_to(owner, (OWNERS, STEP)) == down, 1.0, 0.0)
        flags_16 = flags.astype(BF16)
        before = dot(flags_16, earlier) + seen
        rank = jnp.sum(flags * before, 0, keepdims=True).astype(jnp.int32)
        slot_of[0:1, at] = jnp.where(far >= 0, EXT + owner * PER_OWNER + rank, ids)
        member = jnp.where(far >= 0, jnp.bitwise_and(far, MEMBERS - 1) + 1, 0).astype(F32)
        chosen = jnp.where(jnp.broadcast_to(rank, (OWNERS, STEP)) == down, jnp.broadcast_to(member, (OWNERS, STEP)), 0.0)
        requests[...] += dot_t(flags_16, chosen.astype(BF16))
        return seen + jnp.sum(flags, 1, keepdims=True)

    lax.fori_loop(0, STEPS, rank_step, jnp.zeros((OWNERS, 1), F32))
    wide = jnp.broadcast_to(requests[...][:, None, :], (OWNERS, PER_OWNER, LANES)).reshape(PACKED, LANES)
    at_row = jnp.bitwise_and(lax.broadcasted_iota(jnp.int32, (PACKED, LANES), 0), PER_OWNER - 1)
    at_lane = lax.broadcasted_iota(jnp.int32, (PACKED, LANES), 1)
    wanted = jnp.sum(jnp.where(at_row == at_lane, wide, 0.0), 1, keepdims=True).astype(jnp.int32)
    span = GROUP * MEMBERS
    rows_in = lax.broadcasted_iota(jnp.int32, (PACKED, span), 0)
    cols_in = lax.broadcasted_iota(jnp.int32, (PACKED, span), 1)
    same = jnp.bitwise_and(jnp.right_shift(rows_in, 3), GROUP - 1) == jnp.right_shift(cols_in, 4)
    named = wanted == jnp.bitwise_and(cols_in, MEMBERS - 1) + 1
    picks[...] = onehot(jnp.logical_and(same, named))


def spread_kernel(
    nodes, senders, receivers, node_rows, edges, self_w, send_w, recv_w,
    pre, slot_of, picks,
    coarse, rim, edges_v, pre_v, weights_v, table, hot, packed, requests,
    load_sem, edges_sem, pre_sem, kept_sem, halo_send, halo_recv,
    y_send, y_recv, near_send, near_recv, far_send, far_recv, pass_send, pass_recv,
):
    lat, lon = places()
    core, y, near, far, device = rings(lat, lon)
    met = greet(lat, lon, device)
    loads = []
    for at, source in enumerate((recv_w, send_w, self_w)):
        copy = pltpu.make_async_copy(source, weights_v.at[at], load_sem.at[at])
        copy.start()
        loads.append(copy)
    for step in range(STEPS):
        at = pl.ds(step * STEP, STEP)
        pltpu.make_async_copy(edges.at[at], edges_v.at[at], edges_sem.at[step]).start()

    base = core * SAME_CORE
    mine = base + far * 16 + near * 4 + y
    first = nodes.at[0, 0, pl.ds(0, MEMBERS)]
    kept = pltpu.make_async_copy(first, coarse.at[mine], kept_sem)
    kept.start()
    rank_slots(senders, slot_of, requests, picks)
    pl.semaphore_wait(pltpu.get_barrier_semaphore(), met)

    def remote(source, target, sems, at, peer):
        return pltpu.make_async_remote_copy(
            src_ref=source,
            dst_ref=target,
            send_sem=sems[0].at[at],
            recv_sem=sems[1].at[at],
            device_id=peer,
            device_id_type=MESH,
        )

    y_copies = [remote(first, coarse.at[mine], (y_send, y_recv), step - 1, device(step, 0, 0)) for step in (1, 2, 3)]
    for copy in y_copies:
        copy.start()
    halos = []
    for at, ((row, col), (r, c), (to, size)) in enumerate(HALO):
        source = nodes.at[pl.ds(0, 2), c] if r is None else nodes.at[r, pl.ds(*c)]
        copy = remote(source, rim.at[pl.ds(to, size)], (halo_send, halo_recv), at, shifted(lat, lon, row, col))
        if row:
            pl.when(reaches(lat, row))(copy.start)
        else:
            copy.start()
        halos.append((row, copy))

    @pl.when(lat == 0)
    def _():
        rim[0:5] = jnp.zeros((5, BLOCK, D), BF16)

    @pl.when(lat == 3)
    def _():
        rim[5:10] = jnp.zeros((5, BLOCK, D), BF16)

    for copy in loads:
        copy.wait()
    table[0:NODES] = dot(node_rows[...], weights_v[0]).astype(BF16)
    table[NODES : 2 * NODES] = dot(node_rows[...], weights_v[1]).astype(BF16)
    core_ids = [lane_ids(CORE_BASES[at], CORE_BASES[at + 1]) for at in (0, 2, 4)]
    own_ids = [lane_ids(at * LANES, at * LANES + BLOCK) for at in range(3)]
    rim_ids = [lane_ids(RIM_BASES[at], RIM_BASES[at + 1]) for at in range(0, 14, 2)]
    far_ids = [lane_ids(EXT + at * LANES, EXT + at * LANES + BLOCK) for at in range(PACKED // LANES)]

    def own_step(step, carry):
        at = rows_of(step)
        from_col = column(slot_of[0:1, at])
        to_col = column(receivers[:, at])
        for group in range(3):
            hot[:, group * LANES : (group + 1) * LANES] = onehot(to_col == own_ids[group])
            hot[:, NODES + group * LANES : NODES + (group + 1) * LANES] = onehot(from_col == core_ids[group])
        pltpu.make_async_copy(edges.at[at], edges_v.at[at], edges_sem.at[step]).wait()
        pre_v[at] = dot(edges_v[at], weights_v[2]) + dot(hot[:, : 2 * NODES], table[: 2 * NODES])
        return carry

    def rim_step(step, carry):
        at = rows_of(step)
        from_col = column(slot_of[0:1, at])
        for group in range(RIM // LANES):
            hot[:, group * LANES : (group + 1) * LANES] = onehot(from_col == rim_ids[group])
        pre_v[at] += dot(hot[:, :RIM], table[:RIM])
        return carry

    def far_step(step, carry):
        at = rows_of(step)
        from_col = column(slot_of[0:1, at])
        for group in range(PACKED // LANES):
            hot[:, group * LANES : (group + 1) * LANES] = onehot(from_col == far_ids[group])
        pre_v[at] += dot(hot[...], table[...])
        pltpu.make_async_copy(pre_v.at[at], pre.at[at], pre_sem.at[step]).start()
        return carry

    lax.fori_loop(0, 4, own_step, 0)
    kept.wait()
    for copy in y_copies:
        copy.wait_recv()

    def piece(step):
        return coarse.at[pl.ds(base + far * 16 + lax.rem(near + 4 - step, 4) * 4, 4)]

    near_copies = [remote(piece(0), piece(0), (near_send, near_recv), step - 1, device(0, step, 0)) for step in (1, 3, 2)]
    for copy in near_copies:
        copy.start()
    far_copies = {}

    def send_far(part):
        for step in (1, 3, 2):
            copy = remote(piece(part), piece(part), (far_send, far_recv), part * 3 + step - 1, device(0, 0, step))
            copy.start()
            far_copies[part, step] = copy

    send_far(0)
    lax.fori_loop(4, 8, own_step, 0)
    for part, copy in zip((1, 3, 2), near_copies):
        copy.wait_recv()
        send_far(part)
    partner = shifted(lat, lon, 1 - 2 * core, 0)
    passes = []

    def hand_over(step):
        block = coarse.at[pl.ds(base + lax.rem(far + 4 - step, 4) * 16, 16)]
        copy = remote(block, block, (pass_send, pass_recv), step, partner)
        copy.start()
        passes.append(copy)

    hand_over(0)
    lax.fori_loop(8, STEPS, own_step, 0)
    for row, copy in halos:
        if row:
            pl.when(reaches(lat, -row))(copy.wait_recv)
        else:
            copy.wait_recv()
    table[:RIM] = dot(rim[...].reshape(RIM, D), weights_v[1]).astype(BF16)
    lax.fori_loop(0, STEPS // 2, rim_step, 0)
    for part in range(4):
        far_copies[part, 1].wait_recv()
    hand_over(1)
    lax.fori_loop(STEPS // 2, STEPS, rim_step, 0)
    for step in (3, 2):
        for part in range(4):
            far_copies[part, step].wait_recv()
        hand_over(step)
    for copy in passes:
        copy.wait_recv()
    for group in range(GROUPS):
        at, span = group * LANES, GROUP
        packed[at : at + LANES] = dot(
            picks[at : at + LANES], coarse[group * span : (group + 1) * span].reshape(GROUP * MEMBERS, D)
        ).astype(BF16)
    table[...] = dot(packed[...], weights_v[1]).astype(BF16)
    lax.fori_loop(0, STEPS, far_step, 0)
    for step in range(STEPS):
        at = pl.ds(step * STEP, STEP)
        pltpu.make_async_copy(pre_v.at[at], pre.at[at], pre_sem.at[step]).wait()
    for row, copy in halos:
        if row:
            pl.when(reaches(lat, row))(copy.wait_send)
        else:
            copy.wait_send()
    for copy in y_copies + near_copies + list(far_copies.values()) + passes:
        copy.wait_send()


def spread(nodes, senders, receivers, node_rows, edges, self_w, send_w, recv_w):
    vmem = pl.BlockSpec(memory_space=pltpu.VMEM)
    hbm = pl.BlockSpec(memory_space=pl.ANY)
    dma = pltpu.SemaphoreType.DMA
    return pl.pallas_call(
        spread_kernel,
        out_shape=(
            jax.ShapeDtypeStruct((SLOTS, D), F32),
            jax.ShapeDtypeStruct((8, SLOTS), jnp.int32),
            jax.ShapeDtypeStruct((PACKED, GROUP * MEMBERS), BF16),
        ),
        in_specs=[hbm, vmem, vmem, vmem, hbm, hbm, hbm, hbm],
        out_specs=(hbm, vmem, vmem),
        scratch_shapes=[
            pltpu.VMEM((OWNERS, MEMBERS, D), BF16),
            pltpu.VMEM((14, BLOCK, D), BF16),
            pltpu.VMEM((SLOTS, D), BF16),
            pltpu.VMEM((SLOTS, D), F32),
            pltpu.VMEM((3, D, D), BF16),
            pltpu.VMEM((PACKED, D), BF16),
            pltpu.VMEM((STEP, PACKED), BF16),
            pltpu.VMEM((PACKED, D), BF16),
            pltpu.VMEM((OWNERS, LANES), F32),
            dma((3,)), dma((STEPS,)), dma((STEPS,)), dma, dma((8,)), dma((8,)),
            dma((3,)), dma((3,)), dma((3,)), dma((3,)), dma((12,)), dma((12,)), dma((4,)), dma((4,)),
        ],
        compiler_params=pltpu.CompilerParams(
            collective_id=0, has_side_effects=True, vmem_limit_bytes=VMEM_BYTES
        ),
        name="spread",
    )(nodes, senders, receivers, node_rows, edges, self_w, send_w, recv_w)


def collect_kernel(
    far_grad, slot_of, receivers, pre_grad, send_w, recv_w, out,
    pre_grad_v, own_far, paired, summed, far_in, near_sum, near_in, y_sum, y_in, rim, rim_in, total,
    load_sem, halo_send, halo_recv, pair_send, pair_recv, far_send, far_recv, near_send, near_recv, y_send, y_recv,
):
    lat, lon = places()
    core, y, near, far, device = rings(lat, lon)
    met = greet(lat, lon, device)
    partner = shifted(lat, lon, 1 - 2 * core, 0)
    load = pltpu.make_async_copy(pre_grad, pre_grad_v, load_sem.at[0])
    load.start()
    load_far = pltpu.make_async_copy(far_grad.at[pl.ds(core * SAME_CORE, SAME_CORE)], own_far, load_sem.at[1])
    load_far.start()

    def remote(source, target, sems, at, peer):
        return pltpu.make_async_remote_copy(
            src_ref=source,
            dst_ref=target,
            send_sem=sems[0].at[at],
            recv_sem=sems[1].at[at],
            device_id=peer,
            device_id_type=MESH,
        )

    @pl.when(lat == 0)
    def _():
        rim_in[0:3] = jnp.zeros((3, BLOCK, D), BF16)
        rim_in[10:12] = jnp.zeros((2, BLOCK, D), BF16)

    @pl.when(lat == 3)
    def _():
        rim_in[3:6] = jnp.zeros((3, BLOCK, D), BF16)
        rim_in[12:14] = jnp.zeros((2, BLOCK, D), BF16)

    pl.semaphore_wait(pltpu.get_barrier_semaphore(), met)
    pairs = []
    for step in (1, 3, 2, 0):
        at = lax.rem(near + step, 4) * 16
        copy = remote(
            far_grad.at[pl.ds((1 - core) * SAME_CORE + at, 16)], paired.at[pl.ds(at, 16)], (pair_send, pair_recv), step, partner
        )
        copy.start()
        pairs.append((step, copy))

    def gathered(ids, bases):
        rows = row_ids(bases)
        mask = jnp.broadcast_to(ids, (rows.shape[0], SLOTS)) == rows
        return dot(onehot(mask), pre_grad_v[...])

    load.wait()
    slots = slot_of[0:1, :]
    rim[0:5] = gathered(slots, RIM_BASES[0:5]).astype(BF16).reshape(5, BLOCK, D)
    rim[5:10] = gathered(slots, RIM_BASES[5:10]).astype(BF16).reshape(5, BLOCK, D)
    rim[10:14] = gathered(slots, RIM_BASES[10:14]).astype(BF16).reshape(4, BLOCK, D)
    halos = []
    for at, ((row, col), (start, size), (to, _)) in enumerate(BACK):
        copy = remote(
            rim.at[pl.ds(start, size)], rim_in.at[pl.ds(to, size)], (halo_send, halo_recv), at, shifted(lat, lon, row, col)
        )
        if row:
            pl.when(reaches(lat, row))(copy.start)
        else:
            copy.start()
        halos.append((row, copy))

    load_far.wait()
    copies = []
    for step, copy in pairs:
        copy.wait_recv()
        at = lax.rem(far + step, 4) * 16
        for row in range(16):
            summed[at + row] = (own_far[at + row].astype(F32) + paired[at + row].astype(F32)).astype(BF16)
        if step:
            sent = remote(
                summed.at[pl.ds(at, 16)], far_in.at[step - 1], (far_send, far_recv), step - 1, device(0, 0, step)
            )
            sent.start()
            copies.append(sent)

    total[...] = gathered(slots, CORE_BASES)
    got = gathered(receivers[...], tuple(range(0, NODES, BLOCK))).astype(BF16)
    out[...] = dot_t(got, recv_w[...])

    for copy in copies:
        copy.wait_recv()
    waiting = list(copies)
    copies = []
    for step in (1, 3, 2, 0):
        at = lax.rem(near + step, 4) * 4
        for row in range(4):
            acc = summed[far * 16 + at + row].astype(F32)
            for peer in range(3):
                acc += far_in[peer, at + row].astype(F32)
            near_sum[at + row] = acc.astype(BF16)
        if step:
            sent = remote(
                near_sum.at[pl.ds(at, 4)], near_in.at[step - 1], (near_send, near_recv), step - 1, device(0, step, 0)
            )
            sent.start()
            copies.append(sent)

    for row, copy in halos:
        if row:
            pl.when(reaches(lat, -row))(copy.wait_recv)
        else:
            copy.wait_recv()

    def add(at, block):
        total[at * BLOCK : (at + 1) * BLOCK] += rim_in[block].astype(F32)

    for block in range(6):
        add(block, block)
    for at, block in ((0, 6), (3, 7), (2, 8), (5, 9), (0, 10), (2, 11), (3, 12), (5, 13)):
        add(at, block)
    out[BLOCK:] += dot_t(total[BLOCK:].astype(BF16), send_w[...])

    for copy in copies:
        copy.wait_recv()
    waiting += copies
    copies = []
    for step in (1, 3, 2, 0):
        at = lax.rem(y + step, 4)
        acc = near_sum[near * 4 + at].astype(F32)
        for peer in range(3):
            acc += near_in[peer, at].astype(F32)
        if step:
            y_sum[at] = acc.astype(BF16)
            sent = remote(y_sum.at[at], y_in.at[step - 1], (y_send, y_recv), step - 1, device(step, 0, 0))
            sent.start()
            copies.append(sent)
    for copy in copies:
        copy.wait_recv()
    waiting += copies
    for peer in range(3):
        acc += y_in[peer].astype(F32)
    total[:MEMBERS] += acc
    out[:BLOCK] += dot_t(total[:BLOCK].astype(BF16), send_w[...])
    for row, copy in halos:
        if row:
            pl.when(reaches(lat, row))(copy.wait_send)
        else:
            copy.wait_send()
    for copy in waiting + [copy for _, copy in pairs]:
        copy.wait_send()


def collect(far_grad, slot_of, receivers, pre_grad, send_w, recv_w):
    vmem = pl.BlockSpec(memory_space=pltpu.VMEM)
    hbm = pl.BlockSpec(memory_space=pl.ANY)
    dma = pltpu.SemaphoreType.DMA
    return pl.pallas_call(
        collect_kernel,
        out_shape=jax.ShapeDtypeStruct((NODES, D), F32),
        in_specs=[hbm, vmem, vmem, hbm, vmem, vmem],
        out_specs=vmem,
        scratch_shapes=[
            pltpu.VMEM((SLOTS, D), BF16),
            pltpu.VMEM((SAME_CORE, MEMBERS, D), BF16),
            pltpu.VMEM((SAME_CORE, MEMBERS, D), BF16),
            pltpu.VMEM((SAME_CORE, MEMBERS, D), BF16),
            pltpu.VMEM((3, 16, MEMBERS, D), BF16),
            pltpu.VMEM((16, MEMBERS, D), BF16),
            pltpu.VMEM((3, 4, MEMBERS, D), BF16),
            pltpu.VMEM((4, MEMBERS, D), BF16),
            pltpu.VMEM((3, MEMBERS, D), BF16),
            pltpu.VMEM((14, BLOCK, D), BF16),
            pltpu.VMEM((14, BLOCK, D), BF16),
            pltpu.VMEM((NODES, D), F32),
            dma((2,)), dma((8,)), dma((8,)), dma((4,)), dma((4,)),
            dma((3,)), dma((3,)), dma((3,)), dma((3,)), dma((3,)), dma((3,)),
        ],
        compiler_params=pltpu.CompilerParams(
            collective_id=1, has_side_effects=True, vmem_limit_bytes=VMEM_BYTES
        ),
        name="collect",
    )(far_grad, slot_of, receivers, pre_grad, send_w, recv_w)


def layer_norm(hidden):
    center = hidden - mean(hidden)
    inv_std = lax.rsqrt(mean(center * center) + EPSILON)
    return center * inv_std, inv_std


def norm_back(grad_out, normed, inv_std):
    return inv_std * (grad_out - mean(grad_out) - normed * mean(grad_out * normed))


def layer_kernel(
    count, slot_of, receivers, picks, nodes, node_up, pre, edges, edge_up,
    out_w, self_w, node_w, aggr_w, node_out, edge_gain, node_gain,
    node_new, edge_new, node_grad, edge_grad, pre_grad, far_grad,
    pre_v, edges_v, up_v, new_v, grad_v, packed, normed_v, slope_v, rstd_v, pre_grad_v, aggr, aggr_grad,
    pre_sem, edges_sem, up_sem, new_sem, grad_sem, pre_grad_sem,
):
    for step in range(STEPS):
        at = pl.ds(step * STEP, STEP)
        pltpu.make_async_copy(pre.at[at], pre_v.at[at], pre_sem.at[step]).start()
        pltpu.make_async_copy(edges.at[at], edges_v.at[at], edges_sem.at[step]).start()
    for step in range(STEPS):
        at = pl.ds(step * STEP, STEP)
        pltpu.make_async_copy(edge_up.at[at], up_v.at[at], up_sem.at[step]).start()

    node_row = lax.broadcasted_iota(jnp.int32, (NODES, STEP), 0)
    slot_row = lax.broadcasted_iota(jnp.int32, (STEP, 1), 0)
    own_ids = [lane_ids(at * LANES, at * LANES + BLOCK) for at in range(3)]
    aggr[...] = jnp.zeros_like(aggr)

    def live_of(step):
        return (slot_row + step * STEP < count[0, 0]).astype(F32)

    def forward(step, carry):
        at = rows_of(step)
        pltpu.make_async_copy(pre.at[at], pre_v.at[at], pre_sem.at[step]).wait()
        pltpu.make_async_copy(edges.at[at], edges_v.at[at], edges_sem.at[step]).wait()
        before = pre_v[at]
        gate = sigmoid(before)
        act = before * gate
        slope_v[at] = (gate + act * (1.0 - gate)).astype(BF16)
        normed, rstd = layer_norm(dot(act.astype(BF16), out_w[...]))
        normed_v[at] = normed.astype(BF16)
        rstd_v[at] = jnp.broadcast_to(rstd, (STEP, LANES))
        message = (live_of(step) * normed * edge_gain[...]).astype(BF16)
        new_v[at] = (edges_v[at].astype(F32) + message.astype(F32)).astype(BF16)
        pltpu.make_async_copy(new_v.at[at], edge_new.at[at], new_sem.at[step]).start()
        to_hot = onehot(jnp.broadcast_to(receivers[:, at], (NODES, STEP)) == node_row)
        aggr[...] += dot(to_hot, message)
        return carry

    lax.fori_loop(0, STEPS, forward, 0, unroll=2)

    node_rows = nodes[...]
    node_pre = dot(node_rows, node_w[...]) + dot(aggr[...].astype(BF16), aggr_w[...])
    gate = sigmoid(node_pre)
    act = node_pre * gate
    slope = gate + act * (1.0 - gate)
    normed, rstd = layer_norm(dot(act.astype(BF16), node_out[...]))
    node_new[...] = (node_rows.astype(F32) + normed * node_gain[...]).astype(BF16)
    up = node_up[...].astype(F32)
    hidden_grad = norm_back(up * node_gain[...], normed, rstd).astype(BF16)
    node_pre_grad = (dot_t(hidden_grad, node_out[...]) * slope).astype(BF16)
    node_grad[...] = up + dot_t(node_pre_grad, node_w[...])
    aggr_grad[...] = dot_t(node_pre_grad, aggr_w[...]).astype(BF16)

    def backward(step, carry):
        at = rows_of(step)
        to_col = column(receivers[:, at])
        to_hot = jnp.concatenate([onehot(to_col == ids) for ids in own_ids], axis=1)
        pltpu.make_async_copy(edge_up.at[at], up_v.at[at], up_sem.at[step]).wait()
        upstream = up_v[at].astype(F32)
        grad = live_of(step) * (upstream + dot(to_hot, aggr_grad[...])) * edge_gain[...]
        normed = normed_v[at].astype(F32)
        hidden_grad = norm_back(grad, normed, rstd_v[at][:, :1]).astype(BF16)
        gone = (dot_t(hidden_grad, out_w[...]) * slope_v[at].astype(F32)).astype(BF16)
        pre_grad_v[at] = gone
        pltpu.make_async_copy(pre_grad_v.at[at], pre_grad.at[at], pre_grad_sem.at[step]).start()
        grad_v[at] = upstream + dot_t(gone, self_w[...])
        pltpu.make_async_copy(grad_v.at[at], edge_grad.at[at], grad_sem.at[step]).start()
        return carry

    lax.fori_loop(0, STEPS, backward, 0, unroll=2)

    def far_step(step, carry):
        base = EXT + step * STEP
        mask = jnp.broadcast_to(slot_of[0:1, :], (STEP, SLOTS)) == lax.broadcasted_iota(jnp.int32, (STEP, SLOTS), 0) + base
        packed[rows_of(step)] = dot(onehot(mask), pre_grad_v[...]).astype(BF16)
        return carry

    lax.fori_loop(0, PACKED // STEP, far_step, 0)
    for group in range(GROUPS):
        at, span = group * LANES, GROUP * MEMBERS
        far_grad[group * span : (group + 1) * span] = t_dot(
            picks[at : at + LANES], packed[at : at + LANES]
        ).astype(BF16)

    for step in range(STEPS):
        at = pl.ds(step * STEP, STEP)
        pltpu.make_async_copy(new_v.at[at], edge_new.at[at], new_sem.at[step]).wait()
        pltpu.make_async_copy(pre_grad_v.at[at], pre_grad.at[at], pre_grad_sem.at[step]).wait()
        pltpu.make_async_copy(grad_v.at[at], edge_grad.at[at], grad_sem.at[step]).wait()


def layer(count, slot_of, receivers, picks, nodes, node_up, pre, edges, edge_up, weights, gains):
    vmem = pl.BlockSpec(memory_space=pltpu.VMEM)
    smem = pl.BlockSpec(memory_space=pltpu.SMEM)
    hbm = pl.BlockSpec(memory_space=pl.ANY)
    dma = pltpu.SemaphoreType.DMA
    return pl.pallas_call(
        layer_kernel,
        out_shape=(
            jax.ShapeDtypeStruct((NODES, D), BF16),
            jax.ShapeDtypeStruct((SLOTS, D), BF16),
            jax.ShapeDtypeStruct((NODES, D), F32),
            jax.ShapeDtypeStruct((SLOTS, D), F32),
            jax.ShapeDtypeStruct((SLOTS, D), BF16),
            jax.ShapeDtypeStruct((COARSE, D), BF16),
        ),
        in_specs=[smem] + [vmem] * 5 + [hbm] * 3 + [vmem] * 7,
        out_specs=(vmem, hbm, vmem, hbm, hbm, vmem),
        scratch_shapes=[
            pltpu.VMEM((SLOTS, D), F32),
            pltpu.VMEM((SLOTS, D), BF16),
            pltpu.VMEM((SLOTS, D), BF16),
            pltpu.VMEM((SLOTS, D), BF16),
            pltpu.VMEM((SLOTS, D), F32),
            pltpu.VMEM((PACKED, D), BF16),
            pltpu.VMEM((SLOTS, D), BF16),
            pltpu.VMEM((SLOTS, D), BF16),
            pltpu.VMEM((SLOTS, LANES), F32),
            pltpu.VMEM((SLOTS, D), BF16),
            pltpu.VMEM((NODES, D), F32),
            pltpu.VMEM((NODES, D), BF16),
        ]
        + [dma((STEPS,))] * 6,
        compiler_params=pltpu.CompilerParams(vmem_limit_bytes=VMEM_BYTES),
        name="layer",
    )(count, slot_of, receivers, picks, nodes, node_up, pre, edges, edge_up, *weights, *gains)


def body(
    node_latents,
    edge_latents,
    senders,
    receivers,
    edge_count,
    edge_self_w,
    edge_send_w,
    edge_recv_w,
    edge_out_w,
    node_self_w,
    node_aggr_w,
    node_out_w,
    edge_gain,
    node_gain,
    node_upstream,
    edge_upstream,
):
    grid = node_latents.shape
    node_rows = node_latents.reshape(NODES, D)
    edges = edge_latents.reshape(SLOTS, D)
    to = receivers.reshape(1, SLOTS)
    pre, slot_of, picks = spread(
        node_latents, senders.reshape(1, SLOTS), to, node_rows, edges, edge_self_w, edge_send_w, edge_recv_w
    )
    node_new, edge_new, node_grad, edge_grad, pre_grad, far_grad = layer(
        edge_count,
        slot_of,
        to,
        picks,
        node_rows,
        node_upstream.reshape(NODES, D),
        pre,
        edges,
        edge_upstream.reshape(SLOTS, D),
        (edge_out_w, edge_self_w, node_self_w, node_aggr_w, node_out_w),
        (edge_gain.reshape(1, D), node_gain.reshape(1, D)),
    )
    returned = collect(far_grad.reshape(OWNERS, MEMBERS, D), slot_of, to, pre_grad, edge_send_w, edge_recv_w)
    return (
        node_new.reshape(grid),
        edge_new.reshape(edge_latents.shape),
        (node_grad + returned).reshape(grid),
        edge_grad.reshape(edge_latents.shape),
    )


def solution(mesh):
    tiles = P("lat", "lon", None, None)
    lists = P("lat", "lon", None)
    return jax.shard_map(
        body,
        mesh=mesh,
        in_specs=(tiles, tiles, lists, lists, P("lat", "lon")) + (P(),) * 9 + (tiles, tiles),
        out_specs=(tiles,) * 4,
        check_vma=False,
    )
```

```python
import jax
import jax.numpy as jnp
from jax import lax
from jax.experimental import pallas as pl
from jax.experimental.pallas import tpu as pltpu
from jax.sharding import PartitionSpec as P

MESH = pl.DeviceIdType.MESH
F32 = jnp.float32
BF16 = jnp.bfloat16
EPSILON = 1e-05

D = 512
BLOCK = 64
SLOTS = 3072
NODES = 384
EXT = 1280
OWNERS = 128
MEMBERS = 16
COARSE = OWNERS * MEMBERS
PER_OWNER = 8
PACKED = OWNERS * PER_OWNER
STEP = 512
STEPS = SLOTS // STEP
TURN = 2
TURNS = STEPS // TURN
WIDE = STEP * TURN
LANES = 128
GROUP = 16
GROUPS = OWNERS // GROUP
LONS = 32
SAME_CORE = 64
RIM = 14 * BLOCK
VMEM_BYTES = 60 * 1024 * 1024


def dot(left, right):
    return jnp.dot(left, right, preferred_element_type=F32)


def dot_t(left, right):
    return lax.dot_general(left, right, (((1,), (1,)), ((), ())), preferred_element_type=F32)


def t_dot(left, right):
    return lax.dot_general(left, right, (((0,), (0,)), ((), ())), preferred_element_type=F32)


def onehot(mask):
    return jnp.where(mask, 1.0, 0.0).astype(BF16)


def mean(rows):
    return jnp.sum(rows, -1, keepdims=True) * (1.0 / D)


def sigmoid(pre):
    return 0.5 * jnp.tanh(0.5 * pre) + 0.5


def places():
    lat = lax.axis_index("lat")
    lon = lax.axis_index("lon")
    return lat, lon


def shifted(lat, lon, row, col):
    return {"lat": lax.rem(lat + row + 4, 4), "lon": lax.rem(lon + col + LONS, LONS)}


def rings(lat, lon):
    core, x, z = lat % 2, lon // 8, lon // 2 % 4
    y = lat // 2 * 2 + lon % 2
    near = z + core * (x - z)
    far = x + core * (z - x)

    def device(y_step, near_step, far_step):
        y_at = lax.rem(y + y_step, 4)
        x_at = lax.rem(x + far_step + core * (near_step - far_step), 4)
        z_at = lax.rem(z + near_step + core * (far_step - near_step), 4)
        return {"lat": y_at // 2 * 2 + core, "lon": x_at * 8 + z_at * 2 + y_at % 2}

    return core, y, near, far, device


PLANE = tuple((near, y) for near in (0, 1, 3, 2) for y in (0, 1, 3, 2) if near or y)


def greet(lat, lon, device):
    peers = [shifted(lat, lon, row, col) for row in (-1, 0, 1) for col in (-1, 0, 1) if row or col]
    peers += [device(y_step, near_step, 0) for near_step, y_step in PLANE]
    peers += [device(0, 0, step) for step in (1, 2, 3)]
    for peer in peers:
        pl.semaphore_signal(pltpu.get_barrier_semaphore(), inc=1, device_id=peer, device_id_type=MESH)
    return len(peers)


def reaches(lat, row):
    return jnp.logical_and(lat + row >= 0, lat + row < 4)


RIM_BASES = (0, 64, 128, 192, 256, 960, 1024, 1088, 1152, 1216, 320, 640, 576, 896)
CORE_BASES = (384, 448, 512, 704, 768, 832)
HALO = (
    ((-1, 0), (0, (0, 3)), (6, 3)),
    ((1, 0), (1, (0, 3)), (1, 3)),
    ((0, -1), (None, 0), (12, 2)),
    ((0, 1), (None, 2), (10, 2)),
    ((-1, -1), (0, (0, 1)), (9, 1)),
    ((-1, 1), (0, (2, 1)), (5, 1)),
    ((1, -1), (1, (0, 1)), (4, 1)),
    ((1, 1), (1, (2, 1)), (0, 1)),
)
BACK = (
    ((-1, 0), (1, 3), (3, 3)),
    ((1, 0), (6, 3), (0, 3)),
    ((0, -1), (10, 2), (8, 2)),
    ((0, 1), (12, 2), (6, 2)),
    ((-1, -1), (0, 1), (13, 1)),
    ((-1, 1), (4, 1), (12, 1)),
    ((1, -1), (5, 1), (11, 1)),
    ((1, 1), (9, 1), (10, 1)),
)


def place_of(owner):
    core = jnp.bitwise_and(jnp.right_shift(owner, 5), 1)
    y = jnp.right_shift(owner, 6) * 2 + jnp.bitwise_and(owner, 1)
    x = jnp.bitwise_and(jnp.right_shift(owner, 3), 3)
    z = jnp.bitwise_and(jnp.right_shift(owner, 1), 3)
    place = jnp.where(core == 0, x * 16 + z * 4, SAME_CORE + z * 16 + x * 4) + y
    return jnp.where(owner < 0, owner, place)


def rows_of(step, size=STEP):
    return pl.ds(pl.multiple_of(step * size, size), size)


def turn_of(turn):
    return rows_of(turn, WIDE)


def steps_of(turn):
    return [rows_of(turn * TURN + step) for step in range(TURN)]


def hot_rows(col, groups):
    return jnp.concatenate([onehot(col == ids) for ids in groups], axis=1)


def column(ids):
    return jnp.transpose(jnp.broadcast_to(ids, (LANES, STEP)))


def lane_ids(first, second):
    lane = lax.broadcasted_iota(jnp.int32, (STEP, LANES), 1)
    return lane + jnp.where(lane < BLOCK, first, second - BLOCK)


def row_ids(bases):
    row = lax.broadcasted_iota(jnp.int32, (len(bases) * BLOCK, 1), 0)
    block = jnp.right_shift(row, 6)
    start = jnp.zeros_like(row)
    for at, base in enumerate(bases):
        start = jnp.where(block == at, base - at * BLOCK, start)
    return row + start


def rank_slots(senders, slot_of, requests, picks):
    earlier = onehot(
        lax.broadcasted_iota(jnp.int32, (STEP, STEP), 0) < lax.broadcasted_iota(jnp.int32, (STEP, STEP), 1)
    )
    down = lax.broadcasted_iota(jnp.int32, (OWNERS, STEP), 0)
    requests[...] = jnp.zeros_like(requests)

    def rank_step(step, seen):
        at = rows_of(step)
        ids = senders[:, at]
        far = ids - EXT
        owner = place_of(jnp.right_shift(far, 4))
        flags = jnp.where(jnp.broadcast_to(owner, (OWNERS, STEP)) == down, 1.0, 0.0)
        flags_16 = flags.astype(BF16)
        before = dot(flags_16, earlier) + seen
        rank = jnp.sum(flags * before, 0, keepdims=True).astype(jnp.int32)
        slot_of[0:1, at] = jnp.where(far >= 0, EXT + owner * PER_OWNER + rank, ids)
        member = jnp.where(far >= 0, jnp.bitwise_and(far, MEMBERS - 1) + 1, 0).astype(F32)
        chosen = jnp.where(jnp.broadcast_to(rank, (OWNERS, STEP)) == down, jnp.broadcast_to(member, (OWNERS, STEP)), 0.0)
        requests[...] += dot_t(flags_16, chosen.astype(BF16))
        return seen + jnp.sum(flags, 1, keepdims=True)

    lax.fori_loop(0, STEPS, rank_step, jnp.zeros((OWNERS, 1), F32))
    wide = jnp.broadcast_to(requests[...][:, None, :], (OWNERS, PER_OWNER, LANES)).reshape(PACKED, LANES)
    at_row = jnp.bitwise_and(lax.broadcasted_iota(jnp.int32, (PACKED, LANES), 0), PER_OWNER - 1)
    at_lane = lax.broadcasted_iota(jnp.int32, (PACKED, LANES), 1)
    wanted = jnp.sum(jnp.where(at_row == at_lane, wide, 0.0), 1, keepdims=True).astype(jnp.int32)
    span = GROUP * MEMBERS
    rows_in = lax.broadcasted_iota(jnp.int32, (PACKED, span), 0)
    cols_in = lax.broadcasted_iota(jnp.int32, (PACKED, span), 1)
    same = jnp.bitwise_and(jnp.right_shift(rows_in, 3), GROUP - 1) == jnp.right_shift(cols_in, 4)
    named = wanted == jnp.bitwise_and(cols_in, MEMBERS - 1) + 1
    picks[...] = onehot(jnp.logical_and(same, named))


def spread_kernel(
    nodes, senders_in, receivers_in, node_rows_in, edges, self_w, send_w, recv_w,
    pre, slot_out, picks_out, table_out,
    coarse, rim, edges_v, pre_v, weights_v, table, packed, requests, senders, receivers, node_rows, slot_of, picks,
    load_sem, out_sem, edges_sem, pre_sem, halo_send, halo_recv,
    plane_send, plane_recv, far_send, far_recv, pass_send, pass_recv,
):
    lat, lon = places()
    core, y, near, far, device = rings(lat, lon)
    met = greet(lat, lon, device)
    loads = []
    sources = (
        (senders_in, senders), (receivers_in, receivers), (node_rows_in, node_rows),
        (recv_w, weights_v.at[0]), (send_w, weights_v.at[1]), (self_w, weights_v.at[2]),
    )
    for at, (source, target) in enumerate(sources):
        copy = pltpu.make_async_copy(source, target, load_sem.at[at])
        copy.start()
        loads.append(copy)
    for turn in range(TURNS):
        at = turn_of(turn)
        pltpu.make_async_copy(edges.at[at], edges_v.at[at], edges_sem.at[turn]).start()

    base = core * SAME_CORE
    mine = base + far * 16 + near * 4 + y
    first = nodes.at[0, 0, pl.ds(0, MEMBERS)]
    kept = pltpu.make_async_copy(first, coarse.at[mine], load_sem.at[6])
    kept.start()
    pl.semaphore_wait(pltpu.get_barrier_semaphore(), met)

    def remote(source, target, sems, at, peer):
        return pltpu.make_async_remote_copy(
            src_ref=source,
            dst_ref=target,
            send_sem=sems[0].at[at],
            recv_sem=sems[1].at[at],
            device_id=peer,
            device_id_type=MESH,
        )

    plane = {}
    for near_step, y_step in PLANE:
        copy = remote(
            first, coarse.at[mine], (plane_send, plane_recv), near_step * 4 + y_step, device(y_step, near_step, 0)
        )
        copy.start()
        plane[near_step, y_step] = copy
    halos = []
    for at, ((row, col), (r, c), (to, size)) in enumerate(HALO):
        source = nodes.at[pl.ds(0, 2), c] if r is None else nodes.at[r, pl.ds(*c)]
        copy = remote(source, rim.at[pl.ds(to, size)], (halo_send, halo_recv), at, shifted(lat, lon, row, col))
        if row:
            pl.when(reaches(lat, row))(copy.start)
        else:
            copy.start()
        halos.append((row, copy))

    @pl.when(lat == 0)
    def _():
        rim[0:5] = jnp.zeros((5, BLOCK, D), BF16)

    @pl.when(lat == 3)
    def _():
        rim[5:10] = jnp.zeros((5, BLOCK, D), BF16)

    for copy in loads:
        copy.wait()
    rank_slots(senders, slot_of, requests, picks)
    outs = [
        pltpu.make_async_copy(slot_of, slot_out, out_sem.at[0]),
        pltpu.make_async_copy(picks, picks_out, out_sem.at[1]),
    ]
    for copy in outs:
        copy.start()
    table[0:NODES] = dot(node_rows[...], weights_v[0]).astype(BF16)
    table[NODES : 2 * NODES] = dot(node_rows[...], weights_v[1]).astype(BF16)
    core_ids = [lane_ids(CORE_BASES[at], CORE_BASES[at + 1]) for at in (0, 2, 4)]
    own_ids = [lane_ids(at * LANES, at * LANES + BLOCK) for at in range(3)]
    rim_ids = [lane_ids(RIM_BASES[at], RIM_BASES[at + 1]) for at in range(0, 14, 2)]

    def own_turn(turn, carry):
        whole = turn_of(turn)
        pltpu.make_async_copy(edges.at[whole], edges_v.at[whole], edges_sem.at[turn]).wait()
        for at in steps_of(turn):
            hot = jnp.concatenate(
                [hot_rows(column(receivers[:, at]), own_ids), hot_rows(column(slot_of[0:1, at]), core_ids)], axis=1
            )
            pre_v[at] = dot(edges_v[at], weights_v[2]) + dot(hot, table[: 2 * NODES])
        return carry

    def rim_turn(turn, carry):
        whole = turn_of(turn)
        for at in steps_of(turn):
            pre_v[at] += dot(hot_rows(column(slot_of[0:1, at]), rim_ids), table[:RIM])
        pltpu.make_async_copy(pre_v.at[whole], pre.at[whole], pre_sem.at[turn]).start()
        return carry

    def piece(step):
        return coarse.at[pl.ds(base + far * 16 + lax.rem(near + 4 - step, 4) * 4, 4)]

    far_copies = {}

    def send_far(part):
        for y_step in range(4):
            if (part, y_step) in plane:
                plane[part, y_step].wait_recv()
        for step in (1, 3, 2):
            copy = remote(piece(part), piece(part), (far_send, far_recv), part * 3 + step - 1, device(0, 0, step))
            copy.start()
            far_copies[part, step] = copy

    partner = shifted(lat, lon, 1 - 2 * core, 0)
    passes = []

    def hand_over(step):
        if step:
            for part in range(4):
                far_copies[part, step].wait_recv()
        block = coarse.at[pl.ds(base + lax.rem(far + 4 - step, 4) * 16, 16)]
        copy = remote(block, block, (pass_send, pass_recv), step, partner)
        copy.start()
        passes.append(copy)

    def pack(group):
        at = pl.ds(pl.multiple_of(group * LANES, LANES), LANES)
        rows = dot(picks[at], coarse[pl.ds(group * GROUP, GROUP)].reshape(GROUP * MEMBERS, D)).astype(BF16)
        packed[at] = dot(rows, weights_v[1]).astype(BF16)

    kept.wait()
    send_far(0)
    for part in (1, 3, 2):
        send_far(part)
    hand_over(0)
    lax.fori_loop(0, TURNS, own_turn, 0)
    for row, copy in halos:
        if row:
            pl.when(reaches(lat, -row))(copy.wait_recv)
        else:
            copy.wait_recv()
    table[...] = dot(rim[...].reshape(RIM, D), weights_v[1]).astype(BF16)
    lax.fori_loop(0, 1, rim_turn, 0)
    hand_over(1)
    lax.fori_loop(1, TURNS, rim_turn, 0)
    for step in (3, 2):
        hand_over(step)
    for step in range(4):
        pack(core * 4 + step)
    for copy in passes:
        copy.wait_recv()
    for step in range(4):
        pack(4 - core * 4 + step)
    copy = pltpu.make_async_copy(packed, table_out, out_sem.at[2])
    copy.start()
    for turn in range(TURNS):
        at = turn_of(turn)
        pltpu.make_async_copy(pre_v.at[at], pre.at[at], pre_sem.at[turn]).wait()
    for copy in outs + [copy]:
        copy.wait()
    for row, copy in halos:
        if row:
            pl.when(reaches(lat, row))(copy.wait_send)
        else:
            copy.wait_send()
    for copy in list(plane.values()) + list(far_copies.values()) + passes:
        copy.wait_send()


def spread(nodes, senders, receivers, node_rows, edges, self_w, send_w, recv_w):
    hbm = pl.BlockSpec(memory_space=pl.ANY)
    dma = pltpu.SemaphoreType.DMA
    return pl.pallas_call(
        spread_kernel,
        out_shape=(
            jax.ShapeDtypeStruct((SLOTS, D), F32),
            jax.ShapeDtypeStruct((8, SLOTS), jnp.int32),
            jax.ShapeDtypeStruct((PACKED, GROUP * MEMBERS), BF16),
            jax.ShapeDtypeStruct((PACKED, D), BF16),
        ),
        in_specs=[hbm] * 8,
        out_specs=(hbm,) * 4,
        scratch_shapes=[
            pltpu.VMEM((OWNERS, MEMBERS, D), BF16),
            pltpu.VMEM((14, BLOCK, D), BF16),
            pltpu.VMEM((SLOTS, D), BF16),
            pltpu.VMEM((SLOTS, D), F32),
            pltpu.VMEM((3, D, D), BF16),
            pltpu.VMEM((RIM, D), BF16),
            pltpu.VMEM((PACKED, D), BF16),
            pltpu.VMEM((OWNERS, LANES), F32),
            pltpu.VMEM((1, SLOTS), jnp.int32),
            pltpu.VMEM((1, SLOTS), jnp.int32),
            pltpu.VMEM((NODES, D), BF16),
            pltpu.VMEM((8, SLOTS), jnp.int32),
            pltpu.VMEM((PACKED, GROUP * MEMBERS), BF16),
            dma((7,)), dma((3,)), dma((TURNS,)), dma((TURNS,)), dma((8,)), dma((8,)),
            dma((16,)), dma((16,)), dma((12,)), dma((12,)), dma((4,)), dma((4,)),
        ],
        compiler_params=pltpu.CompilerParams(
            collective_id=0, has_side_effects=True, vmem_limit_bytes=VMEM_BYTES
        ),
        name="spread",
    )(nodes, senders, receivers, node_rows, edges, self_w, send_w, recv_w)


def collect_kernel(
    far_grad, slot_in, receivers_in, pre_grad, send_in, recv_in, out,
    pre_grad_v, own_far, paired, summed, far_in, plane_sum, plane_in, rim, rim_in, total,
    slot_of, receivers, send_w, recv_w,
    load_sem, halo_send, halo_recv, pair_send, pair_recv, far_send, far_recv, plane_send, plane_recv,
):
    lat, lon = places()
    core, y, near, far, device = rings(lat, lon)
    met = greet(lat, lon, device)
    partner = shifted(lat, lon, 1 - 2 * core, 0)
    loads = []
    sources = (
        (slot_in, slot_of), (pre_grad, pre_grad_v), (far_grad.at[pl.ds(core * SAME_CORE, SAME_CORE)], own_far),
        (receivers_in, receivers), (recv_in, recv_w), (send_in, send_w),
    )
    for at, (source, target) in enumerate(sources):
        copy = pltpu.make_async_copy(source, target, load_sem.at[at])
        copy.start()
        loads.append(copy)

    def remote(source, target, sems, at, peer):
        return pltpu.make_async_remote_copy(
            src_ref=source,
            dst_ref=target,
            send_sem=sems[0].at[at],
            recv_sem=sems[1].at[at],
            device_id=peer,
            device_id_type=MESH,
        )

    @pl.when(lat == 0)
    def _():
        rim_in[0:3] = jnp.zeros((3, BLOCK, D), BF16)
        rim_in[10:12] = jnp.zeros((2, BLOCK, D), BF16)

    @pl.when(lat == 3)
    def _():
        rim_in[3:6] = jnp.zeros((3, BLOCK, D), BF16)
        rim_in[12:14] = jnp.zeros((2, BLOCK, D), BF16)

    pl.semaphore_wait(pltpu.get_barrier_semaphore(), met)
    pairs = []
    for step in (1, 3, 2, 0):
        at = lax.rem(near + step, 4) * 16
        copy = remote(
            far_grad.at[pl.ds((1 - core) * SAME_CORE + at, 16)], paired.at[pl.ds(at, 16)], (pair_send, pair_recv), step, partner
        )
        copy.start()
        pairs.append((step, copy))

    def gathered(ids, bases):
        rows = row_ids(bases)
        mask = jnp.broadcast_to(ids, (rows.shape[0], SLOTS)) == rows
        return dot(onehot(mask), pre_grad_v[...])

    for copy in loads:
        copy.wait()
    slots = slot_of[0:1, :]
    rim[0:5] = gathered(slots, RIM_BASES[0:5]).astype(BF16).reshape(5, BLOCK, D)
    rim[5:10] = gathered(slots, RIM_BASES[5:10]).astype(BF16).reshape(5, BLOCK, D)
    rim[10:14] = gathered(slots, RIM_BASES[10:14]).astype(BF16).reshape(4, BLOCK, D)
    halos = []
    for at, ((row, col), (start, size), (to, _)) in enumerate(BACK):
        copy = remote(
            rim.at[pl.ds(start, size)], rim_in.at[pl.ds(to, size)], (halo_send, halo_recv), at, shifted(lat, lon, row, col)
        )
        if row:
            pl.when(reaches(lat, row))(copy.start)
        else:
            copy.start()
        halos.append((row, copy))

    copies = []
    for step, copy in pairs:
        copy.wait_recv()
        at = lax.rem(far + step, 4) * 16
        for row in range(16):
            summed[at + row] = (own_far[at + row].astype(F32) + paired[at + row].astype(F32)).astype(BF16)
        if step:
            sent = remote(
                summed.at[pl.ds(at, 16)], far_in.at[step - 1], (far_send, far_recv), step - 1, device(0, 0, step)
            )
            sent.start()
            copies.append(sent)

    total[...] = gathered(slots, CORE_BASES)
    got = gathered(receivers[...], tuple(range(0, NODES, BLOCK))).astype(BF16)
    out[...] = dot_t(got, recv_w[...])

    for copy in copies:
        copy.wait_recv()
    plane = []
    for near_step, y_step in PLANE + ((0, 0),):
        at = lax.rem(near + near_step, 4) * 4 + lax.rem(y + y_step, 4)
        acc = summed[far * 16 + at].astype(F32)
        for peer in range(3):
            acc += far_in[peer, at].astype(F32)
        if near_step or y_step:
            plane_sum[at] = acc.astype(BF16)
            slot = near_step * 4 + y_step - 1
            sent = remote(
                plane_sum.at[at], plane_in.at[slot], (plane_send, plane_recv), slot, device(y_step, near_step, 0)
            )
            sent.start()
            plane.append(sent)

    for row, copy in halos:
        if row:
            pl.when(reaches(lat, -row))(copy.wait_recv)
        else:
            copy.wait_recv()

    def add(at, block):
        total[at * BLOCK : (at + 1) * BLOCK] += rim_in[block].astype(F32)

    for block in range(6):
        add(block, block)
    for at, block in ((0, 6), (3, 7), (2, 8), (5, 9), (0, 10), (2, 11), (3, 12), (5, 13)):
        add(at, block)
    out[BLOCK:] += dot_t(total[BLOCK:].astype(BF16), send_w[...])

    for copy in plane:
        copy.wait_recv()
    for slot in range(15):
        acc += plane_in[slot].astype(F32)
    total[:MEMBERS] += acc
    out[:BLOCK] += dot_t(total[:BLOCK].astype(BF16), send_w[...])
    for row, copy in halos:
        if row:
            pl.when(reaches(lat, row))(copy.wait_send)
        else:
            copy.wait_send()
    for copy in copies + plane + [copy for _, copy in pairs]:
        copy.wait_send()


def collect(far_grad, slot_of, receivers, pre_grad, send_w, recv_w):
    vmem = pl.BlockSpec(memory_space=pltpu.VMEM)
    hbm = pl.BlockSpec(memory_space=pl.ANY)
    dma = pltpu.SemaphoreType.DMA
    return pl.pallas_call(
        collect_kernel,
        out_shape=jax.ShapeDtypeStruct((NODES, D), F32),
        in_specs=[hbm] * 6,
        out_specs=vmem,
        scratch_shapes=[
            pltpu.VMEM((SLOTS, D), BF16),
            pltpu.VMEM((SAME_CORE, MEMBERS, D), BF16),
            pltpu.VMEM((SAME_CORE, MEMBERS, D), BF16),
            pltpu.VMEM((SAME_CORE, MEMBERS, D), BF16),
            pltpu.VMEM((3, 16, MEMBERS, D), BF16),
            pltpu.VMEM((16, MEMBERS, D), BF16),
            pltpu.VMEM((15, MEMBERS, D), BF16),
            pltpu.VMEM((14, BLOCK, D), BF16),
            pltpu.VMEM((14, BLOCK, D), BF16),
            pltpu.VMEM((NODES, D), F32),
            pltpu.VMEM((8, SLOTS), jnp.int32),
            pltpu.VMEM((1, SLOTS), jnp.int32),
            pltpu.VMEM((D, D), BF16),
            pltpu.VMEM((D, D), BF16),
            dma((6,)), dma((8,)), dma((8,)), dma((4,)), dma((4,)),
            dma((3,)), dma((3,)), dma((15,)), dma((15,)),
        ],
        compiler_params=pltpu.CompilerParams(
            collective_id=1, has_side_effects=True, vmem_limit_bytes=VMEM_BYTES
        ),
        name="collect",
    )(far_grad, slot_of, receivers, pre_grad, send_w, recv_w)


def centered(weight):
    rows = weight[...].astype(F32)
    return (rows - mean(rows)).astype(BF16)


def layer_norm(hidden):
    center = hidden - mean(hidden)
    inv_std = lax.rsqrt(mean(center * center) + EPSILON)
    return center * inv_std, inv_std


def norm_back(grad_out, normed, inv_std):
    return inv_std * (grad_out - mean(grad_out) - normed * mean(grad_out * normed))


def layer_kernel(
    count, slot_of, receivers, picks, table, nodes, node_up, pre, edges, edge_up,
    out_w, self_w, node_w, aggr_w, node_out, edge_gain, node_gain,
    node_new, edge_new, node_grad, edge_grad, pre_grad, far_grad,
    pre_v, edges_v, up_v, new_v, grad_v, packed, normed_v, slope_v, rstd_v, pre_grad_v, aggr, aggr_grad, out_c,
    pre_sem, edges_sem, up_sem, new_sem, grad_sem, pre_grad_sem,
):
    def loaded(turn):
        at = turn_of(turn)
        return (
            pltpu.make_async_copy(pre.at[at], pre_v.at[at], pre_sem.at[turn]),
            pltpu.make_async_copy(edges.at[at], edges_v.at[at], edges_sem.at[turn]),
        )

    def raised(turn):
        at = turn_of(turn)
        return pltpu.make_async_copy(edge_up.at[at], up_v.at[at], up_sem.at[turn])

    for turn in range(TURNS):
        for copy in loaded(turn):
            copy.start()
    for turn in range(TURNS):
        raised(turn).start()

    out_c[...] = centered(out_w)
    node_row = lax.broadcasted_iota(jnp.int32, (NODES, WIDE), 0)
    slot_row = lax.broadcasted_iota(jnp.int32, (STEP, 1), 0)
    own_ids = [lane_ids(at * LANES, at * LANES + BLOCK) for at in range(3)]
    far_ids = [lane_ids(EXT + at * LANES, EXT + at * LANES + BLOCK) for at in range(PACKED // LANES)]
    aggr[...] = jnp.zeros_like(aggr)

    def live_of(step):
        return (slot_row + step * STEP < count[0, 0]).astype(F32)

    def stored(turn):
        at = turn_of(turn)
        return pltpu.make_async_copy(new_v.at[at], edge_new.at[at], new_sem.at[turn])

    def returned(turn):
        at = turn_of(turn)
        return (
            pltpu.make_async_copy(pre_grad_v.at[at], pre_grad.at[at], pre_grad_sem.at[turn]),
            pltpu.make_async_copy(grad_v.at[at], edge_grad.at[at], grad_sem.at[turn]),
        )

    def forward(turn, carry):
        for copy in loaded(turn):
            copy.wait()
        messages = []
        for step, at in enumerate(steps_of(turn)):
            before = pre_v[at] + dot(hot_rows(column(slot_of[0:1, at]), far_ids), table[...])
            gate = sigmoid(before)
            act = before * gate
            slope_v[at] = (gate + act * (1.0 - gate)).astype(BF16)
            center = dot(act.astype(BF16), out_c[...])
            rstd = live_of(turn * TURN + step) * lax.rsqrt(mean(center * center) + EPSILON)
            normed = center * rstd
            normed_v[at] = normed.astype(BF16)
            rstd_v[at] = jnp.broadcast_to(rstd, (STEP, LANES))
            message = (normed * edge_gain[...]).astype(BF16)
            new_v[at] = edges_v[at] + message
            messages.append(message)
        to_hot = onehot(jnp.broadcast_to(receivers[:, turn_of(turn)], (NODES, WIDE)) == node_row)
        aggr[...] += dot(to_hot, jnp.concatenate(messages, axis=0))
        stored(turn).start()
        return carry

    lax.fori_loop(0, TURNS, forward, 0)

    node_rows = nodes[...]
    node_pre = dot(node_rows, node_w[...]) + dot(aggr[...].astype(BF16), aggr_w[...])
    gate = sigmoid(node_pre)
    act = node_pre * gate
    slope = gate + act * (1.0 - gate)
    normed, rstd = layer_norm(dot(act.astype(BF16), node_out[...]))
    node_new[...] = (node_rows.astype(F32) + normed * node_gain[...]).astype(BF16)
    up = node_up[...].astype(F32)
    hidden_grad = norm_back(up * node_gain[...], normed, rstd).astype(BF16)
    node_pre_grad = (dot_t(hidden_grad, node_out[...]) * slope).astype(BF16)
    node_grad[...] = up + dot_t(node_pre_grad, node_w[...])
    aggr_grad[...] = dot_t(node_pre_grad, aggr_w[...]).astype(BF16)

    def backward(turn, carry):
        raised(turn).wait()
        for step, at in enumerate(steps_of(turn)):
            upstream = up_v[at].astype(F32)
            to_hot = hot_rows(column(receivers[:, at]), own_ids)
            grad = (upstream + dot(to_hot, aggr_grad[...])) * edge_gain[...]
            normed = normed_v[at].astype(F32)
            hidden_grad = (rstd_v[at][:, :1] * (grad - normed * mean(grad * normed))).astype(BF16)
            gone = dot_t(hidden_grad, out_c[...]).astype(BF16) * slope_v[at]
            pre_grad_v[at] = gone
            grad_v[at] = upstream + dot_t(gone, self_w[...])
        for copy in returned(turn):
            copy.start()
        return carry

    lax.fori_loop(0, TURNS, backward, 0)

    def far_step(step, carry):
        base = EXT + step * STEP
        mask = jnp.broadcast_to(slot_of[0:1, :], (STEP, SLOTS)) == lax.broadcasted_iota(jnp.int32, (STEP, SLOTS), 0) + base
        packed[rows_of(step)] = dot(onehot(mask), pre_grad_v[...]).astype(BF16)
        return carry

    lax.fori_loop(0, PACKED // STEP, far_step, 0)
    for group in range(GROUPS):
        at, span = group * LANES, GROUP * MEMBERS
        far_grad[group * span : (group + 1) * span] = t_dot(
            picks[at : at + LANES], packed[at : at + LANES]
        ).astype(BF16)

    for turn in range(TURNS):
        stored(turn).wait()
        for copy in returned(turn):
            copy.wait()


def layer(count, slot_of, receivers, picks, table, nodes, node_up, pre, edges, edge_up, weights, gains):
    vmem = pl.BlockSpec(memory_space=pltpu.VMEM)
    smem = pl.BlockSpec(memory_space=pltpu.SMEM)
    hbm = pl.BlockSpec(memory_space=pl.ANY)
    dma = pltpu.SemaphoreType.DMA
    return pl.pallas_call(
        layer_kernel,
        out_shape=(
            jax.ShapeDtypeStruct((NODES, D), BF16),
            jax.ShapeDtypeStruct((SLOTS, D), BF16),
            jax.ShapeDtypeStruct((NODES, D), F32),
            jax.ShapeDtypeStruct((SLOTS, D), F32),
            jax.ShapeDtypeStruct((SLOTS, D), BF16),
            jax.ShapeDtypeStruct((COARSE, D), BF16),
        ),
        in_specs=[smem] + [vmem] * 6 + [hbm] * 3 + [vmem] * 7,
        out_specs=(vmem, hbm, vmem, hbm, hbm, vmem),
        scratch_shapes=[
            pltpu.VMEM((SLOTS, D), F32),
            pltpu.VMEM((SLOTS, D), BF16),
            pltpu.VMEM((SLOTS, D), BF16),
            pltpu.VMEM((SLOTS, D), BF16),
            pltpu.VMEM((SLOTS, D), F32),
            pltpu.VMEM((PACKED, D), BF16),
            pltpu.VMEM((SLOTS, D), BF16),
            pltpu.VMEM((SLOTS, D), BF16),
            pltpu.VMEM((SLOTS, LANES), F32),
            pltpu.VMEM((SLOTS, D), BF16),
            pltpu.VMEM((NODES, D), F32),
            pltpu.VMEM((NODES, D), BF16),
            pltpu.VMEM((D, D), BF16),
        ]
        + [dma((TURNS,))] * 6,
        compiler_params=pltpu.CompilerParams(vmem_limit_bytes=VMEM_BYTES),
        name="layer",
    )(count, slot_of, receivers, picks, table, nodes, node_up, pre, edges, edge_up, *weights, *gains)


def body(
    node_latents,
    edge_latents,
    senders,
    receivers,
    edge_count,
    edge_self_w,
    edge_send_w,
    edge_recv_w,
    edge_out_w,
    node_self_w,
    node_aggr_w,
    node_out_w,
    edge_gain,
    node_gain,
    node_upstream,
    edge_upstream,
):
    grid = node_latents.shape
    node_rows = node_latents.reshape(NODES, D)
    edges = edge_latents.reshape(SLOTS, D)
    to = receivers.reshape(1, SLOTS)
    pre, slot_of, picks, table = spread(
        node_latents, senders.reshape(1, SLOTS), to, node_rows, edges, edge_self_w, edge_send_w, edge_recv_w
    )
    node_new, edge_new, node_grad, edge_grad, pre_grad, far_grad = layer(
        edge_count,
        slot_of,
        to,
        picks,
        table,
        node_rows,
        node_upstream.reshape(NODES, D),
        pre,
        edges,
        edge_upstream.reshape(SLOTS, D),
        (edge_out_w, edge_self_w, node_self_w, node_aggr_w, node_out_w),
        (edge_gain.reshape(1, D), node_gain.reshape(1, D)),
    )
    returned = collect(far_grad.reshape(OWNERS, MEMBERS, D), slot_of, to, pre_grad, edge_send_w, edge_recv_w)
    return (
        node_new.reshape(grid),
        edge_new.reshape(edge_latents.shape),
        (node_grad + returned).reshape(grid),
        edge_grad.reshape(edge_latents.shape),
    )


def solution(mesh):
    tiles = P("lat", "lon", None, None)
    lists = P("lat", "lon", None)
    return jax.shard_map(
        body,
        mesh=mesh,
        in_specs=(tiles, tiles, lists, lists, P("lat", "lon")) + (P(),) * 9 + (tiles, tiles),
        out_specs=(tiles,) * 4,
        check_vma=False,
    )
```

```python
import jax
import jax.numpy as jnp
from jax import lax
from jax.experimental import pallas as pl
from jax.experimental.pallas import tpu as pltpu
from jax.sharding import PartitionSpec as P

MESH = pl.DeviceIdType.MESH
F32 = jnp.float32
BF16 = jnp.bfloat16
EPSILON = 1e-05

D = 512
BLOCK = 64
SLOTS = 3072
NODES = 384
EXT = 1280
OWNERS = 128
MEMBERS = 16
COARSE = OWNERS * MEMBERS
PER_OWNER = 8
PACKED = OWNERS * PER_OWNER
STEP = 512
STEPS = SLOTS // STEP
TURN = 2
TURNS = STEPS // TURN
WIDE = STEP * TURN
LANES = 128
GROUP = 16
GROUPS = OWNERS // GROUP
LONS = 32
SAME_CORE = 64
RIM = 14 * BLOCK
VMEM_BYTES = 60 * 1024 * 1024


def dot(left, right):
    return jnp.dot(left, right, preferred_element_type=F32)


def dot_t(left, right):
    return lax.dot_general(left, right, (((1,), (1,)), ((), ())), preferred_element_type=F32)


def t_dot(left, right):
    return lax.dot_general(left, right, (((0,), (0,)), ((), ())), preferred_element_type=F32)


def onehot(mask):
    return jnp.where(mask, 1.0, 0.0).astype(BF16)


def mean(rows):
    return jnp.sum(rows, -1, keepdims=True) * (1.0 / D)


def sigmoid(pre):
    return 0.5 * jnp.tanh(0.5 * pre) + 0.5


def places():
    lat = lax.axis_index("lat")
    lon = lax.axis_index("lon")
    return lat, lon


def shifted(lat, lon, row, col):
    return {"lat": lax.rem(lat + row + 4, 4), "lon": lax.rem(lon + col + LONS, LONS)}


def rings(lat, lon):
    core, x, z = lat % 2, lon // 8, lon // 2 % 4
    y = lat // 2 * 2 + lon % 2
    near = z + core * (x - z)
    far = x + core * (z - x)

    def device(y_step, near_step, far_step):
        y_at = lax.rem(y + y_step, 4)
        x_at = lax.rem(x + far_step + core * (near_step - far_step), 4)
        z_at = lax.rem(z + near_step + core * (far_step - near_step), 4)
        return {"lat": y_at // 2 * 2 + core, "lon": x_at * 8 + z_at * 2 + y_at % 2}

    return core, y, near, far, device


PLANE = tuple((near, y) for near in (0, 1, 3, 2) for y in (0, 1, 3, 2) if near or y)


def greet(lat, lon, device):
    peers = [shifted(lat, lon, row, col) for row in (-1, 0, 1) for col in (-1, 0, 1) if row or col]
    peers += [device(y_step, near_step, 0) for near_step, y_step in PLANE]
    peers += [device(0, 0, step) for step in (1, 2, 3)]
    for peer in peers:
        pl.semaphore_signal(pltpu.get_barrier_semaphore(), inc=1, device_id=peer, device_id_type=MESH)
    return len(peers)


def reaches(lat, row):
    return jnp.logical_and(lat + row >= 0, lat + row < 4)


RIM_BASES = (0, 64, 128, 192, 256, 960, 1024, 1088, 1152, 1216, 320, 640, 576, 896)
CORE_BASES = (384, 448, 512, 704, 768, 832)
HALO = (
    ((-1, 0), (0, (0, 3)), (6, 3)),
    ((1, 0), (1, (0, 3)), (1, 3)),
    ((0, -1), (None, 0), (12, 2)),
    ((0, 1), (None, 2), (10, 2)),
    ((-1, -1), (0, (0, 1)), (9, 1)),
    ((-1, 1), (0, (2, 1)), (5, 1)),
    ((1, -1), (1, (0, 1)), (4, 1)),
    ((1, 1), (1, (2, 1)), (0, 1)),
)
BACK = (
    ((-1, 0), (1, 3), (3, 3)),
    ((1, 0), (6, 3), (0, 3)),
    ((0, -1), (10, 2), (8, 2)),
    ((0, 1), (12, 2), (6, 2)),
    ((-1, -1), (0, 1), (13, 1)),
    ((-1, 1), (4, 1), (12, 1)),
    ((1, -1), (5, 1), (11, 1)),
    ((1, 1), (9, 1), (10, 1)),
)


def place_of(owner):
    core = jnp.bitwise_and(jnp.right_shift(owner, 5), 1)
    y = jnp.right_shift(owner, 6) * 2 + jnp.bitwise_and(owner, 1)
    x = jnp.bitwise_and(jnp.right_shift(owner, 3), 3)
    z = jnp.bitwise_and(jnp.right_shift(owner, 1), 3)
    place = jnp.where(core == 0, x * 16 + z * 4, SAME_CORE + z * 16 + x * 4) + y
    return jnp.where(owner < 0, owner, place)


def rows_of(step, size=STEP):
    return pl.ds(pl.multiple_of(step * size, size), size)


def turn_of(turn):
    return rows_of(turn, WIDE)


def steps_of(turn):
    return [rows_of(turn * TURN + step) for step in range(TURN)]


def hot_rows(col, groups):
    return jnp.concatenate([onehot(col == ids) for ids in groups], axis=1)


def column(ids):
    return jnp.transpose(jnp.broadcast_to(ids, (LANES, STEP)))


def lane_ids(first, second):
    lane = lax.broadcasted_iota(jnp.int32, (STEP, LANES), 1)
    return lane + jnp.where(lane < BLOCK, first, second - BLOCK)


def row_ids(bases):
    row = lax.broadcasted_iota(jnp.int32, (len(bases) * BLOCK, 1), 0)
    block = jnp.right_shift(row, 6)
    start = jnp.zeros_like(row)
    for at, base in enumerate(bases):
        start = jnp.where(block == at, base - at * BLOCK, start)
    return row + start


def rank_slots(senders, slot_of, requests, picks):
    earlier = onehot(
        lax.broadcasted_iota(jnp.int32, (STEP, STEP), 0) < lax.broadcasted_iota(jnp.int32, (STEP, STEP), 1)
    )
    down = lax.broadcasted_iota(jnp.int32, (OWNERS, STEP), 0)
    requests[...] = jnp.zeros_like(requests)

    def rank_step(step, seen):
        at = rows_of(step)
        ids = senders[:, at]
        far = ids - EXT
        owner = place_of(jnp.right_shift(far, 4))
        flags = jnp.where(jnp.broadcast_to(owner, (OWNERS, STEP)) == down, 1.0, 0.0)
        flags_16 = flags.astype(BF16)
        before = dot(flags_16, earlier) + seen
        rank = jnp.sum(flags * before, 0, keepdims=True).astype(jnp.int32)
        slot_of[0:1, at] = jnp.where(far >= 0, EXT + owner * PER_OWNER + rank, ids)
        member = jnp.where(far >= 0, jnp.bitwise_and(far, MEMBERS - 1) + 1, 0).astype(F32)
        chosen = jnp.where(jnp.broadcast_to(rank, (OWNERS, STEP)) == down, jnp.broadcast_to(member, (OWNERS, STEP)), 0.0)
        requests[...] += dot_t(flags_16, chosen.astype(BF16))
        return seen + jnp.sum(flags, 1, keepdims=True)

    lax.fori_loop(0, STEPS, rank_step, jnp.zeros((OWNERS, 1), F32))
    wide = jnp.broadcast_to(requests[...][:, None, :], (OWNERS, PER_OWNER, LANES)).reshape(PACKED, LANES)
    at_row = jnp.bitwise_and(lax.broadcasted_iota(jnp.int32, (PACKED, LANES), 0), PER_OWNER - 1)
    at_lane = lax.broadcasted_iota(jnp.int32, (PACKED, LANES), 1)
    wanted = jnp.sum(jnp.where(at_row == at_lane, wide, 0.0), 1, keepdims=True).astype(jnp.int32)
    span = GROUP * MEMBERS
    rows_in = lax.broadcasted_iota(jnp.int32, (PACKED, span), 0)
    cols_in = lax.broadcasted_iota(jnp.int32, (PACKED, span), 1)
    same = jnp.bitwise_and(jnp.right_shift(rows_in, 3), GROUP - 1) == jnp.right_shift(cols_in, 4)
    named = wanted == jnp.bitwise_and(cols_in, MEMBERS - 1) + 1
    picks[...] = onehot(jnp.logical_and(same, named))


def spread_kernel(
    nodes, senders_in, receivers_in, node_rows_in, edges, self_w, send_w, recv_w,
    pre, slot_out, picks_out, table_out,
    coarse, rim, edges_v, pre_v, pre_out, weights_v, table, packed, requests, senders, receivers, node_rows, slot_of, picks,
    load_sem, out_sem, edges_sem, pre_sem, halo_send, halo_recv,
    plane_send, plane_recv, far_send, far_recv, pass_send, pass_recv,
):
    lat, lon = places()
    core, y, near, far, device = rings(lat, lon)
    met = greet(lat, lon, device)
    loads = []
    sources = (
        (senders_in, senders), (receivers_in, receivers), (node_rows_in, node_rows),
        (recv_w, weights_v.at[0]), (send_w, weights_v.at[1]), (self_w, weights_v.at[2]),
    )
    for at, (source, target) in enumerate(sources):
        copy = pltpu.make_async_copy(source, target, load_sem.at[at])
        copy.start()
        loads.append(copy)
    for turn in range(TURNS):
        at = turn_of(turn)
        pltpu.make_async_copy(edges.at[at], edges_v.at[at], edges_sem.at[turn]).start()

    base = core * SAME_CORE
    mine = base + far * 16 + near * 4 + y
    first = nodes.at[0, 0, pl.ds(0, MEMBERS)]
    kept = pltpu.make_async_copy(first, coarse.at[mine], load_sem.at[6])
    kept.start()
    loads[0].wait()
    rank_slots(senders, slot_of, requests, picks)
    outs = [
        pltpu.make_async_copy(slot_of, slot_out, out_sem.at[0]),
        pltpu.make_async_copy(picks, picks_out, out_sem.at[1]),
    ]
    for copy in outs:
        copy.start()
    pl.semaphore_wait(pltpu.get_barrier_semaphore(), met)

    def remote(source, target, sems, at, peer):
        return pltpu.make_async_remote_copy(
            src_ref=source,
            dst_ref=target,
            send_sem=sems[0].at[at],
            recv_sem=sems[1].at[at],
            device_id=peer,
            device_id_type=MESH,
        )

    plane = {}
    for near_step, y_step in PLANE:
        copy = remote(
            first, coarse.at[mine], (plane_send, plane_recv), near_step * 4 + y_step, device(y_step, near_step, 0)
        )
        copy.start()
        plane[near_step, y_step] = copy
    @pl.when(lat == 0)
    def _():
        rim[0:5] = jnp.zeros((5, BLOCK, D), BF16)

    @pl.when(lat == 3)
    def _():
        rim[5:10] = jnp.zeros((5, BLOCK, D), BF16)

    for copy in plane.values():
        copy.wait_send()
    halos = []
    for at, ((row, col), (r, c), (to, size)) in enumerate(HALO):
        source = nodes.at[pl.ds(0, 2), c] if r is None else nodes.at[r, pl.ds(*c)]
        copy = remote(source, rim.at[pl.ds(to, size)], (halo_send, halo_recv), at, shifted(lat, lon, row, col))
        if row:
            pl.when(reaches(lat, row))(copy.start)
        else:
            copy.start()
        halos.append((row, copy))

    for copy in loads[1:]:
        copy.wait()
    table[0:NODES] = dot(node_rows[...], weights_v[0]).astype(BF16)
    table[NODES : 2 * NODES] = dot(node_rows[...], weights_v[1]).astype(BF16)
    core_ids = [lane_ids(CORE_BASES[at], CORE_BASES[at + 1]) for at in (0, 2, 4)]
    own_ids = [lane_ids(at * LANES, at * LANES + BLOCK) for at in range(3)]
    rim_ids = [lane_ids(RIM_BASES[at], RIM_BASES[at + 1]) for at in range(0, 14, 2)]

    def own_turn(turn, carry):
        whole = turn_of(turn)
        pltpu.make_async_copy(edges.at[whole], edges_v.at[whole], edges_sem.at[turn]).wait()
        for at in steps_of(turn):
            hot = jnp.concatenate(
                [hot_rows(column(receivers[:, at]), own_ids), hot_rows(column(slot_of[0:1, at]), core_ids)], axis=1
            )
            pre_v[at] = dot(edges_v[at], weights_v[2]) + dot(hot, table[: 2 * NODES])
        return carry

    def rim_turn(turn, carry):
        whole = turn_of(turn)
        for at in steps_of(turn):
            near_rows = dot(hot_rows(column(slot_of[0:1, at]), rim_ids), table[:RIM])
            pre_out[at] = (pre_v[at] + near_rows).astype(BF16)
        pltpu.make_async_copy(pre_out.at[whole], pre.at[whole], pre_sem.at[turn]).start()
        return carry

    def piece(step):
        return coarse.at[pl.ds(base + far * 16 + lax.rem(near + 4 - step, 4) * 4, 4)]

    far_copies = {}

    def send_far(part):
        for y_step in range(4):
            if (part, y_step) in plane:
                plane[part, y_step].wait_recv()
        for step in (1, 3, 2):
            copy = remote(piece(part), piece(part), (far_send, far_recv), part * 3 + step - 1, device(0, 0, step))
            copy.start()
            far_copies[part, step] = copy

    partner = shifted(lat, lon, 1 - 2 * core, 0)
    passes = []

    def hand_over(step):
        if step:
            for part in range(4):
                far_copies[part, step].wait_recv()
        block = coarse.at[pl.ds(base + lax.rem(far + 4 - step, 4) * 16, 16)]
        copy = remote(block, block, (pass_send, pass_recv), step, partner)
        copy.start()
        passes.append(copy)

    def pack(group):
        at = pl.ds(pl.multiple_of(group * LANES, LANES), LANES)
        rows = dot(picks[at], coarse[pl.ds(group * GROUP, GROUP)].reshape(GROUP * MEMBERS, D)).astype(BF16)
        packed[at] = dot(rows, weights_v[1]).astype(BF16)

    lax.fori_loop(0, 1, own_turn, 0)
    kept.wait()
    send_far(0)
    for part in (1, 3, 2):
        send_far(part)
    hand_over(0)
    lax.fori_loop(1, TURNS, own_turn, 0)
    for row, copy in halos:
        if row:
            pl.when(reaches(lat, -row))(copy.wait_recv)
        else:
            copy.wait_recv()
    table[...] = dot(rim[...].reshape(RIM, D), weights_v[1]).astype(BF16)
    hand_over(1)
    lax.fori_loop(0, 1, rim_turn, 0)
    hand_over(3)
    lax.fori_loop(1, 2, rim_turn, 0)
    hand_over(2)
    lax.fori_loop(2, TURNS, rim_turn, 0)
    for step in range(4):
        pack(core * 4 + step)
    for copy in passes:
        copy.wait_recv()
    for step in range(4):
        pack(4 - core * 4 + step)
    copy = pltpu.make_async_copy(packed, table_out, out_sem.at[2])
    copy.start()
    for turn in range(TURNS):
        at = turn_of(turn)
        pltpu.make_async_copy(pre_out.at[at], pre.at[at], pre_sem.at[turn]).wait()
    for copy in outs + [copy]:
        copy.wait()
    for row, copy in halos:
        if row:
            pl.when(reaches(lat, row))(copy.wait_send)
        else:
            copy.wait_send()
    for copy in list(far_copies.values()) + passes:
        copy.wait_send()


def spread(nodes, senders, receivers, node_rows, edges, self_w, send_w, recv_w):
    hbm = pl.BlockSpec(memory_space=pl.ANY)
    dma = pltpu.SemaphoreType.DMA
    return pl.pallas_call(
        spread_kernel,
        out_shape=(
            jax.ShapeDtypeStruct((SLOTS, D), BF16),
            jax.ShapeDtypeStruct((8, SLOTS), jnp.int32),
            jax.ShapeDtypeStruct((PACKED, GROUP * MEMBERS), BF16),
            jax.ShapeDtypeStruct((PACKED, D), BF16),
        ),
        in_specs=[hbm] * 8,
        out_specs=(hbm,) * 4,
        scratch_shapes=[
            pltpu.VMEM((OWNERS, MEMBERS, D), BF16),
            pltpu.VMEM((14, BLOCK, D), BF16),
            pltpu.VMEM((SLOTS, D), BF16),
            pltpu.VMEM((SLOTS, D), F32),
            pltpu.VMEM((SLOTS, D), BF16),
            pltpu.VMEM((3, D, D), BF16),
            pltpu.VMEM((RIM, D), BF16),
            pltpu.VMEM((PACKED, D), BF16),
            pltpu.VMEM((OWNERS, LANES), F32),
            pltpu.VMEM((1, SLOTS), jnp.int32),
            pltpu.VMEM((1, SLOTS), jnp.int32),
            pltpu.VMEM((NODES, D), BF16),
            pltpu.VMEM((8, SLOTS), jnp.int32),
            pltpu.VMEM((PACKED, GROUP * MEMBERS), BF16),
            dma((7,)), dma((3,)), dma((TURNS,)), dma((TURNS,)), dma((8,)), dma((8,)),
            dma((16,)), dma((16,)), dma((12,)), dma((12,)), dma((4,)), dma((4,)),
        ],
        compiler_params=pltpu.CompilerParams(
            collective_id=0, has_side_effects=True, vmem_limit_bytes=VMEM_BYTES
        ),
        name="spread",
    )(nodes, senders, receivers, node_rows, edges, self_w, send_w, recv_w)


def collect_kernel(
    slot_in, receivers_in, picks_in, pre_grad, send_in, recv_in, out,
    pre_grad_v, far_grad, paired, summed, far_in, plane_sum, plane_in, rim, rim_in, total,
    slot_of, receivers, picks, send_w, recv_w,
    load_sem, halo_send, halo_recv, pair_send, pair_recv, far_send, far_recv, plane_send, plane_recv,
):
    lat, lon = places()
    core, y, near, far, device = rings(lat, lon)
    met = greet(lat, lon, device)
    partner = shifted(lat, lon, 1 - 2 * core, 0)
    loads = []
    sources = (
        (slot_in, slot_of), (pre_grad, pre_grad_v), (picks_in, picks),
        (receivers_in, receivers), (recv_in, recv_w), (send_in, send_w),
    )
    for at, (source, target) in enumerate(sources):
        copy = pltpu.make_async_copy(source, target, load_sem.at[at])
        copy.start()
        loads.append(copy)

    def remote(source, target, sems, at, peer):
        return pltpu.make_async_remote_copy(
            src_ref=source,
            dst_ref=target,
            send_sem=sems[0].at[at],
            recv_sem=sems[1].at[at],
            device_id=peer,
            device_id_type=MESH,
        )

    @pl.when(lat == 0)
    def _():
        rim_in[0:3] = jnp.zeros((3, BLOCK, D), BF16)
        rim_in[10:12] = jnp.zeros((2, BLOCK, D), BF16)

    @pl.when(lat == 3)
    def _():
        rim_in[3:6] = jnp.zeros((3, BLOCK, D), BF16)
        rim_in[12:14] = jnp.zeros((2, BLOCK, D), BF16)

    def summed_by(ids, rows):
        mask = jnp.broadcast_to(ids, (rows.shape[0], SLOTS)) == rows
        return dot(onehot(mask), pre_grad_v[...])

    def gathered(ids, bases):
        return summed_by(ids, row_ids(bases))

    half = PACKED // 2

    def far_rows(side):
        rows = lax.broadcasted_iota(jnp.int32, (half, 1), 0) + (EXT + side * half)
        got = summed_by(slot_of[0:1, :], rows).astype(BF16)
        for group in range(4):
            wanted = picks[pl.ds(pl.multiple_of(side * half + group * LANES, LANES), LANES)]
            block = t_dot(wanted, got[group * LANES : (group + 1) * LANES]).astype(BF16)
            far_grad[side, group] = block.reshape(4, 4, MEMBERS, D)

    for copy in loads[:3]:
        copy.wait()
    far_rows(1 - core)
    pl.semaphore_wait(pltpu.get_barrier_semaphore(), met)
    pairs = []
    for part in (1, 3, 2, 0):
        at = lax.rem(far + part, 4)
        copy = remote(far_grad.at[1 - core, :, at], paired.at[:, at], (pair_send, pair_recv), part, partner)
        copy.start()
        pairs.append((part, copy))
    slots = slot_of[0:1, :]
    rim[0:5] = gathered(slots, RIM_BASES[0:5]).astype(BF16).reshape(5, BLOCK, D)
    rim[5:10] = gathered(slots, RIM_BASES[5:10]).astype(BF16).reshape(5, BLOCK, D)
    rim[10:14] = gathered(slots, RIM_BASES[10:14]).astype(BF16).reshape(4, BLOCK, D)
    halos = []
    for at, ((row, col), (start, size), (to, _)) in enumerate(BACK):
        copy = remote(
            rim.at[pl.ds(start, size)], rim_in.at[pl.ds(to, size)], (halo_send, halo_recv), at, shifted(lat, lon, row, col)
        )
        if row:
            pl.when(reaches(lat, row))(copy.start)
        else:
            copy.start()
        halos.append((row, copy))
    far_rows(core)

    copies = {}
    for part, copy in pairs:
        copy.wait_recv()
        at = lax.rem(near + part, 4)
        for step in (1, 3, 2, 0):
            to = lax.rem(far + step, 4)
            summed[to, at] = (far_grad[core, to, at].astype(F32) + paired[to, at].astype(F32)).astype(BF16)
            if step:
                slot = part * 3 + step - 1
                copies[part, step] = remote(
                    summed.at[to, at], far_in.at[slot], (far_send, far_recv), slot, device(0, 0, step)
                )
                copies[part, step].start()

    for copy in loads[3:]:
        copy.wait()
    total[...] = gathered(slots, CORE_BASES)
    got = gathered(receivers[...], tuple(range(0, NODES, BLOCK))).astype(BF16)
    out[...] = dot_t(got, recv_w[...])

    plane = []
    for part in (1, 3, 2, 0):
        for step in (1, 3, 2):
            copies[part, step].wait_recv()
        at = lax.rem(near + part, 4)
        for y_step in (1, 3, 2, 0):
            y_at = lax.rem(y + y_step, 4)
            acc = summed[far, at, y_at].astype(F32)
            for step in range(3):
                acc += far_in[part * 3 + step, y_at].astype(F32)
            if part or y_step:
                slot = part * 4 + y_step - 1
                plane_sum[slot] = acc.astype(BF16)
                sent = remote(
                    plane_sum.at[slot], plane_in.at[slot], (plane_send, plane_recv), slot, device(y_step, part, 0)
                )
                sent.start()
                plane.append(sent)

    for row, copy in halos:
        if row:
            pl.when(reaches(lat, -row))(copy.wait_recv)
        else:
            copy.wait_recv()

    def add(at, block):
        total[at * BLOCK : (at + 1) * BLOCK] += rim_in[block].astype(F32)

    for block in range(6):
        add(block, block)
    for at, block in ((0, 6), (3, 7), (2, 8), (5, 9), (0, 10), (2, 11), (3, 12), (5, 13)):
        add(at, block)
    out[BLOCK:] += dot_t(total[BLOCK:].astype(BF16), send_w[...])

    for copy in plane:
        copy.wait_recv()
    for slot in range(15):
        acc += plane_in[slot].astype(F32)
    total[:MEMBERS] += acc
    out[:BLOCK] += dot_t(total[:BLOCK].astype(BF16), send_w[...])
    for row, copy in halos:
        if row:
            pl.when(reaches(lat, row))(copy.wait_send)
        else:
            copy.wait_send()
    for copy in list(copies.values()) + plane + [copy for _, copy in pairs]:
        copy.wait_send()


def collect(slot_of, receivers, picks, pre_grad, send_w, recv_w):
    hbm = pl.BlockSpec(memory_space=pl.ANY)
    dma = pltpu.SemaphoreType.DMA
    return pl.pallas_call(
        collect_kernel,
        out_shape=jax.ShapeDtypeStruct((NODES, D), F32),
        in_specs=[hbm] * 6,
        out_specs=pl.BlockSpec(memory_space=pltpu.VMEM),
        scratch_shapes=[
            pltpu.VMEM((SLOTS, D), BF16),
            pltpu.VMEM((2, 4, 4, 4, MEMBERS, D), BF16),
            pltpu.VMEM((4, 4, 4, MEMBERS, D), BF16),
            pltpu.VMEM((4, 4, 4, MEMBERS, D), BF16),
            pltpu.VMEM((12, 4, MEMBERS, D), BF16),
            pltpu.VMEM((15, MEMBERS, D), BF16),
            pltpu.VMEM((15, MEMBERS, D), BF16),
            pltpu.VMEM((14, BLOCK, D), BF16),
            pltpu.VMEM((14, BLOCK, D), BF16),
            pltpu.VMEM((NODES, D), F32),
            pltpu.VMEM((8, SLOTS), jnp.int32),
            pltpu.VMEM((1, SLOTS), jnp.int32),
            pltpu.VMEM((PACKED, GROUP * MEMBERS), BF16),
            pltpu.VMEM((D, D), BF16),
            pltpu.VMEM((D, D), BF16),
            dma((6,)), dma((8,)), dma((8,)), dma((4,)), dma((4,)),
            dma((12,)), dma((12,)), dma((15,)), dma((15,)),
        ],
        compiler_params=pltpu.CompilerParams(
            collective_id=1, has_side_effects=True, vmem_limit_bytes=VMEM_BYTES
        ),
        name="collect",
    )(slot_of, receivers, picks, pre_grad, send_w, recv_w)


def centered(weight):
    rows = weight[...].astype(F32)
    return (rows - mean(rows)).astype(BF16)


def layer_norm(hidden):
    center = hidden - mean(hidden)
    inv_std = lax.rsqrt(mean(center * center) + EPSILON)
    return center * inv_std, inv_std


def norm_back(grad_out, normed, inv_std):
    return inv_std * (grad_out - mean(grad_out) - normed * mean(grad_out * normed))


def layer_kernel(
    count, edge_gain, node_gain, slot_in, receivers_in, table_in, nodes_in, node_up_in, pre, edges, edge_up,
    out_in, self_in, node_in, aggr_in, node_out_in,
    node_new_out, edge_new, node_grad_out, edge_grad, pre_grad,
    pre_v, edges_v, up_v, new_v, grad_v, normed_v, slope_v, rstd_v, pre_grad_v, aggr, aggr_grad, out_c,
    slot_of, receivers, table, nodes, node_up, out_w, self_w, node_w, aggr_w, node_out, node_new, node_grad,
    load_sem, pre_sem, edges_sem, up_sem, new_sem, grad_sem, pre_grad_sem,
):
    def loaded(turn):
        at = turn_of(turn)
        return (
            pltpu.make_async_copy(pre.at[at], pre_v.at[at], pre_sem.at[turn]),
            pltpu.make_async_copy(edges.at[at], edges_v.at[at], edges_sem.at[turn]),
        )

    def raised(turn):
        at = turn_of(turn)
        return pltpu.make_async_copy(edge_up.at[at], up_v.at[at], up_sem.at[turn])

    sources = (
        (out_in, out_w), (slot_in, slot_of), (table_in, table), (receivers_in, receivers),
        (nodes_in, nodes), (node_up_in, node_up), (node_in, node_w), (aggr_in, aggr_w), (node_out_in, node_out),
        (self_in, self_w),
    )
    loads = [pltpu.make_async_copy(source, target, load_sem.at[at]) for at, (source, target) in enumerate(sources)]
    for copy in loads[:4]:
        copy.start()
    for turn in range(TURNS):
        for copy in loaded(turn):
            copy.start()
    for copy in loads[4:]:
        copy.start()
    for turn in range(TURNS):
        raised(turn).start()
    for copy in loads[:4]:
        copy.wait()

    out_c[...] = centered(out_w)
    node_row = lax.broadcasted_iota(jnp.int32, (NODES, WIDE), 0)
    slot_row = lax.broadcasted_iota(jnp.int32, (STEP, 1), 0)
    own_ids = [lane_ids(at * LANES, at * LANES + BLOCK) for at in range(3)]
    far_ids = [lane_ids(EXT + at * LANES, EXT + at * LANES + BLOCK) for at in range(PACKED // LANES)]
    aggr[...] = jnp.zeros_like(aggr)

    def live_of(step):
        return (slot_row + step * STEP < count[0, 0]).astype(F32)

    def stored(turn):
        at = turn_of(turn)
        return pltpu.make_async_copy(new_v.at[at], edge_new.at[at], new_sem.at[turn])

    def returned(turn):
        at = turn_of(turn)
        return (
            pltpu.make_async_copy(pre_grad_v.at[at], pre_grad.at[at], pre_grad_sem.at[turn]),
            pltpu.make_async_copy(grad_v.at[at], edge_grad.at[at], grad_sem.at[turn]),
        )

    def forward(turn, carry):
        for copy in loaded(turn):
            copy.wait()
        messages = []
        for step, at in enumerate(steps_of(turn)):
            before = pre_v[at] + dot(hot_rows(column(slot_of[0:1, at]), far_ids), table[...])
            gate = sigmoid(before)
            act = before * gate
            slope_v[at] = (gate + act * (1.0 - gate)).astype(BF16)
            center = dot(act.astype(BF16), out_c[...])
            rstd = live_of(turn * TURN + step) * lax.rsqrt(mean(center * center) + EPSILON)
            normed = center * rstd
            normed_v[at] = normed.astype(BF16)
            rstd_v[at] = jnp.broadcast_to(rstd, (STEP, LANES))
            message = (normed * edge_gain[...]).astype(BF16)
            new_v[at] = edges_v[at] + message
            messages.append(message)
        to_hot = onehot(jnp.broadcast_to(receivers[:, turn_of(turn)], (NODES, WIDE)) == node_row)
        aggr[...] += dot(to_hot, jnp.concatenate(messages, axis=0))
        stored(turn).start()
        return carry

    lax.fori_loop(0, TURNS, forward, 0)

    for copy in loads[4:]:
        copy.wait()
    node_rows = nodes[...]
    node_pre = dot(node_rows, node_w[...]) + dot(aggr[...].astype(BF16), aggr_w[...])
    gate = sigmoid(node_pre)
    act = node_pre * gate
    slope = gate + act * (1.0 - gate)
    normed, rstd = layer_norm(dot(act.astype(BF16), node_out[...]))
    node_new[...] = (node_rows.astype(F32) + normed * node_gain[...]).astype(BF16)
    up = node_up[...].astype(F32)
    hidden_grad = norm_back(up * node_gain[...], normed, rstd).astype(BF16)
    node_pre_grad = (dot_t(hidden_grad, node_out[...]) * slope).astype(BF16)
    node_grad[...] = up + dot_t(node_pre_grad, node_w[...])
    aggr_grad[...] = dot_t(node_pre_grad, aggr_w[...]).astype(BF16)
    outs = (
        pltpu.make_async_copy(node_new, node_new_out, load_sem.at[10]),
        pltpu.make_async_copy(node_grad, node_grad_out, load_sem.at[11]),
    )
    for copy in outs:
        copy.start()

    def backward(turn, carry):
        raised(turn).wait()
        for step, at in enumerate(steps_of(turn)):
            upstream = up_v[at].astype(F32)
            to_hot = hot_rows(column(receivers[:, at]), own_ids)
            grad = (upstream + dot(to_hot, aggr_grad[...])) * edge_gain[...]
            normed = normed_v[at].astype(F32)
            hidden_grad = (rstd_v[at][:, :1] * (grad - normed * mean(grad * normed))).astype(BF16)
            gone = dot_t(hidden_grad, out_c[...]).astype(BF16) * slope_v[at]
            pre_grad_v[at] = gone
            grad_v[at] = upstream + dot_t(gone, self_w[...])
        for copy in returned(turn):
            copy.start()
        return carry

    lax.fori_loop(0, TURNS, backward, 0)

    for copy in outs:
        copy.wait()
    for turn in range(TURNS):
        stored(turn).wait()
        for copy in returned(turn):
            copy.wait()


def layer(count, edge_gain, node_gain, *rows):
    vmem = pl.BlockSpec(memory_space=pltpu.VMEM)
    smem = pl.BlockSpec(memory_space=pltpu.SMEM)
    hbm = pl.BlockSpec(memory_space=pl.ANY)
    dma = pltpu.SemaphoreType.DMA
    return pl.pallas_call(
        layer_kernel,
        out_shape=(
            jax.ShapeDtypeStruct((NODES, D), BF16),
            jax.ShapeDtypeStruct((SLOTS, D), BF16),
            jax.ShapeDtypeStruct((NODES, D), F32),
            jax.ShapeDtypeStruct((SLOTS, D), F32),
            jax.ShapeDtypeStruct((SLOTS, D), BF16),
        ),
        in_specs=[smem, vmem, vmem] + [hbm] * len(rows),
        out_specs=(hbm,) * 5,
        scratch_shapes=[
            pltpu.VMEM((SLOTS, D), BF16),
            pltpu.VMEM((SLOTS, D), BF16),
            pltpu.VMEM((SLOTS, D), BF16),
            pltpu.VMEM((SLOTS, D), BF16),
            pltpu.VMEM((SLOTS, D), F32),
            pltpu.VMEM((SLOTS, D), BF16),
            pltpu.VMEM((SLOTS, D), BF16),
            pltpu.VMEM((SLOTS, LANES), F32),
            pltpu.VMEM((SLOTS, D), BF16),
            pltpu.VMEM((NODES, D), F32),
            pltpu.VMEM((NODES, D), BF16),
            pltpu.VMEM((D, D), BF16),
            pltpu.VMEM((8, SLOTS), jnp.int32),
            pltpu.VMEM((1, SLOTS), jnp.int32),
            pltpu.VMEM((PACKED, D), BF16),
            pltpu.VMEM((NODES, D), BF16),
            pltpu.VMEM((NODES, D), BF16),
        ]
        + [pltpu.VMEM((D, D), BF16)] * 5
        + [pltpu.VMEM((NODES, D), BF16), pltpu.VMEM((NODES, D), F32)]
        + [dma((12,))]
        + [dma((TURNS,))] * 6,
        compiler_params=pltpu.CompilerParams(vmem_limit_bytes=VMEM_BYTES),
        name="layer",
    )(count, edge_gain, node_gain, *rows)


def body(
    node_latents,
    edge_latents,
    senders,
    receivers,
    edge_count,
    edge_self_w,
    edge_send_w,
    edge_recv_w,
    edge_out_w,
    node_self_w,
    node_aggr_w,
    node_out_w,
    edge_gain,
    node_gain,
    node_upstream,
    edge_upstream,
):
    grid = node_latents.shape
    node_rows = node_latents.reshape(NODES, D)
    edges = edge_latents.reshape(SLOTS, D)
    to = receivers.reshape(1, SLOTS)
    pre, slot_of, picks, table = spread(
        node_latents, senders.reshape(1, SLOTS), to, node_rows, edges, edge_self_w, edge_send_w, edge_recv_w
    )
    node_new, edge_new, node_grad, edge_grad, pre_grad = layer(
        edge_count,
        edge_gain.reshape(1, D),
        node_gain.reshape(1, D),
        slot_of,
        to,
        table,
        node_rows,
        node_upstream.reshape(NODES, D),
        pre,
        edges,
        edge_upstream.reshape(SLOTS, D),
        edge_out_w,
        edge_self_w,
        node_self_w,
        node_aggr_w,
        node_out_w,
    )
    returned = collect(slot_of, to, picks, pre_grad, edge_send_w, edge_recv_w)
    return (
        node_new.reshape(grid),
        edge_new.reshape(edge_latents.shape),
        (node_grad + returned).reshape(grid),
        edge_grad.reshape(edge_latents.shape),
    )


def solution(mesh):
    tiles = P("lat", "lon", None, None)
    lists = P("lat", "lon", None)
    return jax.shard_map(
        body,
        mesh=mesh,
        in_specs=(tiles, tiles, lists, lists, P("lat", "lon")) + (P(),) * 9 + (tiles, tiles),
        out_specs=(tiles,) * 4,
        check_vma=False,
    )
```

```python
import jax
import jax.numpy as jnp
from jax import lax
from jax.experimental import pallas as pl
from jax.experimental.pallas import tpu as pltpu
from jax.sharding import PartitionSpec as P

MESH = pl.DeviceIdType.MESH
F32 = jnp.float32
BF16 = jnp.bfloat16
EPSILON = 1e-05

D = 512
BLOCK = 64
SLOTS = 3072
NODES = 384
EXT = 1280
OWNERS = 128
MEMBERS = 16
COARSE = OWNERS * MEMBERS
PER_OWNER = 8
PACKED = OWNERS * PER_OWNER
STEP = 512
STEPS = SLOTS // STEP
TURN = 2
TURNS = STEPS // TURN
WIDE = STEP * TURN
LANES = 128
GROUP = 16
GROUPS = OWNERS // GROUP
LONS = 32
SAME_CORE = 64
RIM = 14 * BLOCK
SIDES = 10 * BLOCK
VMEM_BYTES = 60 * 1024 * 1024


def dot(left, right):
    return jnp.dot(left, right, preferred_element_type=F32)


def dot_t(left, right):
    return lax.dot_general(left, right, (((1,), (1,)), ((), ())), preferred_element_type=F32)


def t_dot(left, right):
    return lax.dot_general(left, right, (((0,), (0,)), ((), ())), preferred_element_type=F32)


def onehot(mask):
    return jnp.where(mask, 1.0, 0.0).astype(BF16)


def mean(rows):
    return jnp.sum(rows, -1, keepdims=True) * (1.0 / D)


def sigmoid(pre):
    return 0.5 * jnp.tanh(0.5 * pre) + 0.5


def places():
    lat = lax.axis_index("lat")
    lon = lax.axis_index("lon")
    return lat, lon


def shifted(lat, lon, row, col):
    return {"lat": lax.rem(lat + row + 4, 4), "lon": lax.rem(lon + col + LONS, LONS)}


def rings(lat, lon):
    core, x, z = lat % 2, lon // 8, lon // 2 % 4
    y = lat // 2 * 2 + lon % 2
    near = z + core * (x - z)
    far = x + core * (z - x)

    def device(y_step, near_step, far_step):
        y_at = lax.rem(y + y_step, 4)
        x_at = lax.rem(x + far_step + core * (near_step - far_step), 4)
        z_at = lax.rem(z + near_step + core * (far_step - near_step), 4)
        return {"lat": y_at // 2 * 2 + core, "lon": x_at * 8 + z_at * 2 + y_at % 2}

    return core, y, near, far, device


PLANE = tuple((near, y) for near in (0, 1, 3, 2) for y in (0, 1, 3, 2) if near or y)


def greet(lat, lon, device):
    peers = [shifted(lat, lon, row, col) for row in (-1, 0, 1) for col in (-1, 0, 1) if row or col]
    peers += [device(y_step, near_step, 0) for near_step, y_step in PLANE]
    peers += [device(0, 0, step) for step in (1, 2, 3)]
    for peer in peers:
        pl.semaphore_signal(pltpu.get_barrier_semaphore(), inc=1, device_id=peer, device_id_type=MESH)
    return len(peers)


def reaches(lat, row):
    return jnp.logical_and(lat + row >= 0, lat + row < 4)


RIM_BASES = (0, 64, 128, 192, 256, 960, 1024, 1088, 1152, 1216, 320, 640, 576, 896)
CORE_BASES = (384, 448, 512, 704, 768, 832)
HALO = (
    ((0, -1), (None, 0), (12, 2)),
    ((0, 1), (None, 2), (10, 2)),
    ((-1, 0), (0, (0, 3)), (6, 3)),
    ((1, 0), (1, (0, 3)), (1, 3)),
    ((-1, -1), (0, (0, 1)), (9, 1)),
    ((-1, 1), (0, (2, 1)), (5, 1)),
    ((1, -1), (1, (0, 1)), (4, 1)),
    ((1, 1), (1, (2, 1)), (0, 1)),
)
BACK = (
    ((-1, 0), (1, 3), (3, 3)),
    ((1, 0), (6, 3), (0, 3)),
    ((0, -1), (10, 2), (8, 2)),
    ((0, 1), (12, 2), (6, 2)),
    ((-1, -1), (0, 1), (13, 1)),
    ((-1, 1), (4, 1), (12, 1)),
    ((1, -1), (5, 1), (11, 1)),
    ((1, 1), (9, 1), (10, 1)),
)


def place_of(owner):
    core = jnp.bitwise_and(jnp.right_shift(owner, 5), 1)
    y = jnp.right_shift(owner, 6) * 2 + jnp.bitwise_and(owner, 1)
    x = jnp.bitwise_and(jnp.right_shift(owner, 3), 3)
    z = jnp.bitwise_and(jnp.right_shift(owner, 1), 3)
    place = jnp.where(core == 0, x * 16 + z * 4, SAME_CORE + z * 16 + x * 4) + y
    return jnp.where(owner < 0, owner, place)


def rows_of(step, size=STEP):
    return pl.ds(pl.multiple_of(step * size, size), size)


def turn_of(turn):
    return rows_of(turn, WIDE)


def steps_of(turn):
    return [rows_of(turn * TURN + step) for step in range(TURN)]


def hot_rows(col, groups):
    return jnp.concatenate([onehot(col == ids) for ids in groups], axis=1)


def column(ids):
    return jnp.transpose(jnp.broadcast_to(ids, (LANES, STEP)))


def lane_ids(first, second):
    lane = lax.broadcasted_iota(jnp.int32, (STEP, LANES), 1)
    return lane + jnp.where(lane < BLOCK, first, second - BLOCK)


def row_ids(bases):
    row = lax.broadcasted_iota(jnp.int32, (len(bases) * BLOCK, 1), 0)
    block = jnp.right_shift(row, 6)
    start = jnp.zeros_like(row)
    for at, base in enumerate(bases):
        start = jnp.where(block == at, base - at * BLOCK, start)
    return row + start


def rank_slots(senders, slot_of, requests, picks):
    earlier = onehot(
        lax.broadcasted_iota(jnp.int32, (STEP, STEP), 0) < lax.broadcasted_iota(jnp.int32, (STEP, STEP), 1)
    )
    down = lax.broadcasted_iota(jnp.int32, (OWNERS, STEP), 0)
    requests[...] = jnp.zeros_like(requests)

    def rank_step(step, seen):
        at = rows_of(step)
        ids = senders[:, at]
        far = ids - EXT
        owner = place_of(jnp.right_shift(far, 4))
        flags = jnp.where(jnp.broadcast_to(owner, (OWNERS, STEP)) == down, 1.0, 0.0)
        flags_16 = flags.astype(BF16)
        before = dot(flags_16, earlier) + seen
        rank = jnp.sum(flags * before, 0, keepdims=True).astype(jnp.int32)
        slot_of[0:1, at] = jnp.where(far >= 0, EXT + owner * PER_OWNER + rank, ids)
        member = jnp.where(far >= 0, jnp.bitwise_and(far, MEMBERS - 1) + 1, 0).astype(F32)
        chosen = jnp.where(jnp.broadcast_to(rank, (OWNERS, STEP)) == down, jnp.broadcast_to(member, (OWNERS, STEP)), 0.0)
        requests[...] += dot_t(flags_16, chosen.astype(BF16))
        return seen + jnp.sum(flags, 1, keepdims=True)

    lax.fori_loop(0, STEPS, rank_step, jnp.zeros((OWNERS, 1), F32))
    wide = jnp.broadcast_to(requests[...][:, None, :], (OWNERS, PER_OWNER, LANES)).reshape(PACKED, LANES)
    at_row = jnp.bitwise_and(lax.broadcasted_iota(jnp.int32, (PACKED, LANES), 0), PER_OWNER - 1)
    at_lane = lax.broadcasted_iota(jnp.int32, (PACKED, LANES), 1)
    wanted = jnp.sum(jnp.where(at_row == at_lane, wide, 0.0), 1, keepdims=True).astype(jnp.int32)
    span = GROUP * MEMBERS
    rows_in = lax.broadcasted_iota(jnp.int32, (PACKED, span), 0)
    cols_in = lax.broadcasted_iota(jnp.int32, (PACKED, span), 1)
    same = jnp.bitwise_and(jnp.right_shift(rows_in, 3), GROUP - 1) == jnp.right_shift(cols_in, 4)
    named = wanted == jnp.bitwise_and(cols_in, MEMBERS - 1) + 1
    picks[...] = onehot(jnp.logical_and(same, named))


def spread_kernel(
    nodes, senders_in, receivers_in, node_rows_in, edges, self_w, send_w, recv_w,
    pre, slot_out, picks_out, table_out,
    coarse, rim, edges_v, pre_v, pre_out, weights_v, table, packed, requests, senders, receivers, node_rows, slot_of, picks,
    load_sem, out_sem, edges_sem, pre_sem, halo_send, halo_recv,
    plane_send, plane_recv, far_send, far_recv, pass_send, pass_recv, corner_send, corner_recv,
):
    lat, lon = places()
    core, y, near, far, device = rings(lat, lon)
    met = greet(lat, lon, device)
    loads = []
    sources = (
        (senders_in, senders), (receivers_in, receivers), (node_rows_in, node_rows),
        (recv_w, weights_v.at[0]), (send_w, weights_v.at[1]), (self_w, weights_v.at[2]),
    )
    for at, (source, target) in enumerate(sources):
        copy = pltpu.make_async_copy(source, target, load_sem.at[at])
        copy.start()
        loads.append(copy)
    for turn in range(TURNS):
        at = turn_of(turn)
        pltpu.make_async_copy(edges.at[at], edges_v.at[at], edges_sem.at[turn]).start()

    base = core * SAME_CORE
    mine = base + far * 16 + near * 4 + y
    first = nodes.at[0, 0, pl.ds(0, MEMBERS)]
    kept = pltpu.make_async_copy(first, coarse.at[mine], load_sem.at[6])
    kept.start()
    loads[0].wait()
    rank_slots(senders, slot_of, requests, picks)
    outs = [
        pltpu.make_async_copy(slot_of, slot_out, out_sem.at[0]),
        pltpu.make_async_copy(picks, picks_out, out_sem.at[1]),
    ]
    for copy in outs:
        copy.start()
    pl.semaphore_wait(pltpu.get_barrier_semaphore(), met)

    def remote(source, target, sems, at, peer):
        return pltpu.make_async_remote_copy(
            src_ref=source,
            dst_ref=target,
            send_sem=sems[0].at[at],
            recv_sem=sems[1].at[at],
            device_id=peer,
            device_id_type=MESH,
        )

    plane = {}
    for near_step, y_step in PLANE:
        copy = remote(
            first, coarse.at[mine], (plane_send, plane_recv), near_step * 4 + y_step, device(y_step, near_step, 0)
        )
        copy.start()
        plane[near_step, y_step] = copy
    @pl.when(lat == 0)
    def _():
        rim[0:5] = jnp.zeros((5, BLOCK, D), BF16)

    @pl.when(lat == 3)
    def _():
        rim[5:10] = jnp.zeros((5, BLOCK, D), BF16)

    for copy in plane.values():
        copy.wait_send()
    halos = []
    for at, ((row, col), (r, c), (to, size)) in enumerate(HALO):
        source = nodes.at[pl.ds(0, 2), c] if r is None else nodes.at[r, pl.ds(*c)]
        copy = remote(source, rim.at[pl.ds(to, size)], (halo_send, halo_recv), at, shifted(lat, lon, row, col))
        if row and col:
            sends, gets = lat == (2 if row < 0 else 1), lat == (1 if row < 0 else 2)
        elif row:
            sends, gets = reaches(lat, row), reaches(lat, -row)
        else:
            sends = gets = None
        copy.start() if sends is None else pl.when(sends)(copy.start)
        halos.append((sends, gets, copy))

    for copy in loads[1:]:
        copy.wait()
    table[0:NODES] = dot(node_rows[...], weights_v[0]).astype(BF16)
    table[NODES : 2 * NODES] = dot(node_rows[...], weights_v[1]).astype(BF16)
    core_ids = [lane_ids(CORE_BASES[at], CORE_BASES[at + 1]) for at in (0, 2, 4)]
    own_ids = [lane_ids(at * LANES, at * LANES + BLOCK) for at in range(3)]
    rim_ids = [lane_ids(RIM_BASES[at], RIM_BASES[at + 1]) for at in range(0, 14, 2)]

    def own_turn(turn, carry):
        whole = turn_of(turn)
        pltpu.make_async_copy(edges.at[whole], edges_v.at[whole], edges_sem.at[turn]).wait()
        for at in steps_of(turn):
            hot = jnp.concatenate(
                [hot_rows(column(receivers[:, at]), own_ids), hot_rows(column(slot_of[0:1, at]), core_ids)], axis=1
            )
            pre_v[at] = dot(edges_v[at], weights_v[2]) + dot(hot, table[: 2 * NODES])
        return carry

    def side_turn(turn, carry):
        for at in steps_of(turn):
            pre_v[at] += dot(hot_rows(column(slot_of[0:1, at]), rim_ids[5:]), table[SIDES:RIM])
        return carry

    def rim_turn(turn, carry):
        whole = turn_of(turn)
        for at in steps_of(turn):
            near_rows = dot(hot_rows(column(slot_of[0:1, at]), rim_ids[:5]), table[:SIDES])
            pre_out[at] = (pre_v[at] + near_rows).astype(BF16)
        pltpu.make_async_copy(pre_out.at[whole], pre.at[whole], pre_sem.at[turn]).start()
        return carry

    def piece(step):
        return coarse.at[pl.ds(base + far * 16 + lax.rem(near + 4 - step, 4) * 4, 4)]

    far_copies = {}

    def send_far(part):
        for y_step in range(4):
            if (part, y_step) in plane:
                plane[part, y_step].wait_recv()
        for step in (1, 3, 2):
            copy = remote(piece(part), piece(part), (far_send, far_recv), part * 3 + step - 1, device(0, 0, step))
            copy.start()
            far_copies[part, step] = copy

    partner = shifted(lat, lon, 1 - 2 * core, 0)
    passes = []

    def hand_over(step):
        if step:
            for part in range(4):
                far_copies[part, step].wait_recv()
        block = coarse.at[pl.ds(base + lax.rem(far + 4 - step, 4) * 16, 16)]
        copy = remote(block, block, (pass_send, pass_recv), step, partner)
        copy.start()
        passes.append(copy)

    def pack(group):
        at = pl.ds(pl.multiple_of(group * LANES, LANES), LANES)
        rows = dot(picks[at], coarse[pl.ds(group * GROUP, GROUP)].reshape(GROUP * MEMBERS, D)).astype(BF16)
        packed[at] = dot(rows, weights_v[1]).astype(BF16)

    lax.fori_loop(0, 1, own_turn, 0)
    kept.wait()
    send_far(0)
    for part in (1, 3, 2):
        send_far(part)
    hand_over(0)
    lax.fori_loop(1, TURNS, own_turn, 0)
    corners = []
    for _, _, copy in halos[:2]:
        copy.wait_recv()
    for at, (column_at, row_at) in enumerate(((11, 0), (13, 4))):
        copy = remote(
            rim.at[column_at - core], rim.at[row_at + 5 * core], (corner_send, corner_recv), at, partner
        )
        copy.start()
        corners.append(copy)
    table[SIDES:RIM] = dot(rim[10:14].reshape(4 * BLOCK, D), weights_v[1]).astype(BF16)
    lax.fori_loop(0, TURNS, side_turn, 0)
    for copy in corners:
        copy.wait_recv()
    for _, gets, copy in halos[2:]:
        pl.when(gets)(copy.wait_recv)
    table[:SIDES] = dot(rim[:10].reshape(SIDES, D), weights_v[1]).astype(BF16)
    hand_over(1)
    lax.fori_loop(0, 1, rim_turn, 0)
    hand_over(3)
    lax.fori_loop(1, 2, rim_turn, 0)
    hand_over(2)
    lax.fori_loop(2, TURNS, rim_turn, 0)
    for step in range(4):
        pack(core * 4 + step)
    for copy in passes:
        copy.wait_recv()
    for step in range(4):
        pack(4 - core * 4 + step)
    copy = pltpu.make_async_copy(packed, table_out, out_sem.at[2])
    copy.start()
    for turn in range(TURNS):
        at = turn_of(turn)
        pltpu.make_async_copy(pre_out.at[at], pre.at[at], pre_sem.at[turn]).wait()
    for copy in outs + [copy]:
        copy.wait()
    for sends, _, copy in halos:
        copy.wait_send() if sends is None else pl.when(sends)(copy.wait_send)
    for copy in list(far_copies.values()) + passes + corners:
        copy.wait_send()


def spread(nodes, senders, receivers, node_rows, edges, self_w, send_w, recv_w):
    hbm = pl.BlockSpec(memory_space=pl.ANY)
    dma = pltpu.SemaphoreType.DMA
    return pl.pallas_call(
        spread_kernel,
        out_shape=(
            jax.ShapeDtypeStruct((SLOTS, D), BF16),
            jax.ShapeDtypeStruct((8, SLOTS), jnp.int32),
            jax.ShapeDtypeStruct((PACKED, GROUP * MEMBERS), BF16),
            jax.ShapeDtypeStruct((PACKED, D), BF16),
        ),
        in_specs=[hbm] * 8,
        out_specs=(hbm,) * 4,
        scratch_shapes=[
            pltpu.VMEM((OWNERS, MEMBERS, D), BF16),
            pltpu.VMEM((14, BLOCK, D), BF16),
            pltpu.VMEM((SLOTS, D), BF16),
            pltpu.VMEM((SLOTS, D), F32),
            pltpu.VMEM((SLOTS, D), BF16),
            pltpu.VMEM((3, D, D), BF16),
            pltpu.VMEM((RIM, D), BF16),
            pltpu.VMEM((PACKED, D), BF16),
            pltpu.VMEM((OWNERS, LANES), F32),
            pltpu.VMEM((1, SLOTS), jnp.int32),
            pltpu.VMEM((1, SLOTS), jnp.int32),
            pltpu.VMEM((NODES, D), BF16),
            pltpu.VMEM((8, SLOTS), jnp.int32),
            pltpu.VMEM((PACKED, GROUP * MEMBERS), BF16),
            dma((7,)), dma((3,)), dma((TURNS,)), dma((TURNS,)), dma((8,)), dma((8,)),
            dma((16,)), dma((16,)), dma((12,)), dma((12,)), dma((4,)), dma((4,)), dma((2,)), dma((2,)),
        ],
        compiler_params=pltpu.CompilerParams(
            collective_id=0, has_side_effects=True, vmem_limit_bytes=VMEM_BYTES
        ),
        name="spread",
    )(nodes, senders, receivers, node_rows, edges, self_w, send_w, recv_w)


def collect_kernel(
    slot_in, receivers_in, picks_in, pre_grad, send_in, recv_in, out,
    pre_grad_v, far_grad, paired, summed, far_in, plane_sum, plane_in, rim, rim_in, total,
    slot_of, receivers, picks, send_w, recv_w,
    load_sem, halo_send, halo_recv, pair_send, pair_recv, far_send, far_recv, plane_send, plane_recv,
):
    lat, lon = places()
    core, y, near, far, device = rings(lat, lon)
    met = greet(lat, lon, device)
    partner = shifted(lat, lon, 1 - 2 * core, 0)
    loads = []
    sources = (
        (slot_in, slot_of), (pre_grad, pre_grad_v), (picks_in, picks),
        (receivers_in, receivers), (recv_in, recv_w), (send_in, send_w),
    )
    for at, (source, target) in enumerate(sources):
        copy = pltpu.make_async_copy(source, target, load_sem.at[at])
        copy.start()
        loads.append(copy)

    def remote(source, target, sems, at, peer):
        return pltpu.make_async_remote_copy(
            src_ref=source,
            dst_ref=target,
            send_sem=sems[0].at[at],
            recv_sem=sems[1].at[at],
            device_id=peer,
            device_id_type=MESH,
        )

    @pl.when(lat == 0)
    def _():
        rim_in[0:3] = jnp.zeros((3, BLOCK, D), BF16)
        rim_in[10:12] = jnp.zeros((2, BLOCK, D), BF16)

    @pl.when(lat == 3)
    def _():
        rim_in[3:6] = jnp.zeros((3, BLOCK, D), BF16)
        rim_in[12:14] = jnp.zeros((2, BLOCK, D), BF16)

    def summed_by(ids, rows):
        mask = jnp.broadcast_to(ids, (rows.shape[0], SLOTS)) == rows
        return dot(onehot(mask), pre_grad_v[...])

    def gathered(ids, bases):
        return summed_by(ids, row_ids(bases))

    half = PACKED // 2

    def far_rows(side):
        rows = lax.broadcasted_iota(jnp.int32, (half, 1), 0) + (EXT + side * half)
        got = summed_by(slot_of[0:1, :], rows).astype(BF16)
        for group in range(4):
            wanted = picks[pl.ds(pl.multiple_of(side * half + group * LANES, LANES), LANES)]
            block = t_dot(wanted, got[group * LANES : (group + 1) * LANES]).astype(BF16)
            far_grad[side, group] = block.reshape(4, 4, MEMBERS, D)

    for copy in loads[:3]:
        copy.wait()
    slots = slot_of[0:1, :]
    rim[0:5] = gathered(slots, RIM_BASES[0:5]).astype(BF16).reshape(5, BLOCK, D)
    rim[5:10] = gathered(slots, RIM_BASES[5:10]).astype(BF16).reshape(5, BLOCK, D)
    rim[10:14] = gathered(slots, RIM_BASES[10:14]).astype(BF16).reshape(4, BLOCK, D)
    pl.semaphore_wait(pltpu.get_barrier_semaphore(), met)
    halos = []
    for at, ((row, col), (start, size), (to, _)) in enumerate(BACK):
        copy = remote(
            rim.at[pl.ds(start, size)], rim_in.at[pl.ds(to, size)], (halo_send, halo_recv), at, shifted(lat, lon, row, col)
        )
        if row:
            pl.when(reaches(lat, row))(copy.start)
        else:
            copy.start()
        halos.append((row, copy))
    far_rows(1 - core)
    pairs = []
    for part in (1, 3, 2, 0):
        at = lax.rem(far + part, 4)
        copy = remote(far_grad.at[1 - core, :, at], paired.at[:, at], (pair_send, pair_recv), part, partner)
        copy.start()
        pairs.append((part, copy))
    far_rows(core)

    copies = {}
    for part, copy in pairs:
        copy.wait_recv()
        at = lax.rem(near + part, 4)
        for step in (1, 3, 2, 0):
            to = lax.rem(far + step, 4)
            summed[to, at] = (far_grad[core, to, at].astype(F32) + paired[to, at].astype(F32)).astype(BF16)
            if step:
                slot = part * 3 + step - 1
                copies[part, step] = remote(
                    summed.at[to, at], far_in.at[slot], (far_send, far_recv), slot, device(0, 0, step)
                )
                copies[part, step].start()

    for copy in loads[3:]:
        copy.wait()
    total[...] = gathered(slots, CORE_BASES)
    got = gathered(receivers[...], tuple(range(0, NODES, BLOCK))).astype(BF16)
    out[...] = dot_t(got, recv_w[...])

    plane = []
    for part in (1, 3, 2, 0):
        for step in (1, 3, 2):
            copies[part, step].wait_recv()
        at = lax.rem(near + part, 4)
        for y_step in (1, 3, 2, 0):
            y_at = lax.rem(y + y_step, 4)
            acc = summed[far, at, y_at].astype(F32)
            for step in range(3):
                acc += far_in[part * 3 + step, y_at].astype(F32)
            if part or y_step:
                slot = part * 4 + y_step - 1
                plane_sum[slot] = acc.astype(BF16)
                sent = remote(
                    plane_sum.at[slot], plane_in.at[slot], (plane_send, plane_recv), slot, device(y_step, part, 0)
                )
                sent.start()
                plane.append(sent)

    for row, copy in halos:
        if row:
            pl.when(reaches(lat, -row))(copy.wait_recv)
        else:
            copy.wait_recv()

    def add(at, block):
        total[at * BLOCK : (at + 1) * BLOCK] += rim_in[block].astype(F32)

    for block in range(6):
        add(block, block)
    for at, block in ((0, 6), (3, 7), (2, 8), (5, 9), (0, 10), (2, 11), (3, 12), (5, 13)):
        add(at, block)
    out[BLOCK:] += dot_t(total[BLOCK:].astype(BF16), send_w[...])

    for copy in plane:
        copy.wait_recv()
    for slot in range(15):
        acc += plane_in[slot].astype(F32)
    total[:MEMBERS] += acc
    out[:BLOCK] += dot_t(total[:BLOCK].astype(BF16), send_w[...])
    for row, copy in halos:
        if row:
            pl.when(reaches(lat, row))(copy.wait_send)
        else:
            copy.wait_send()
    for copy in list(copies.values()) + plane + [copy for _, copy in pairs]:
        copy.wait_send()


def collect(slot_of, receivers, picks, pre_grad, send_w, recv_w):
    hbm = pl.BlockSpec(memory_space=pl.ANY)
    dma = pltpu.SemaphoreType.DMA
    return pl.pallas_call(
        collect_kernel,
        out_shape=jax.ShapeDtypeStruct((NODES, D), F32),
        in_specs=[hbm] * 6,
        out_specs=pl.BlockSpec(memory_space=pltpu.VMEM),
        scratch_shapes=[
            pltpu.VMEM((SLOTS, D), BF16),
            pltpu.VMEM((2, 4, 4, 4, MEMBERS, D), BF16),
            pltpu.VMEM((4, 4, 4, MEMBERS, D), BF16),
            pltpu.VMEM((4, 4, 4, MEMBERS, D), BF16),
            pltpu.VMEM((12, 4, MEMBERS, D), BF16),
            pltpu.VMEM((15, MEMBERS, D), BF16),
            pltpu.VMEM((15, MEMBERS, D), BF16),
            pltpu.VMEM((14, BLOCK, D), BF16),
            pltpu.VMEM((14, BLOCK, D), BF16),
            pltpu.VMEM((NODES, D), F32),
            pltpu.VMEM((8, SLOTS), jnp.int32),
            pltpu.VMEM((1, SLOTS), jnp.int32),
            pltpu.VMEM((PACKED, GROUP * MEMBERS), BF16),
            pltpu.VMEM((D, D), BF16),
            pltpu.VMEM((D, D), BF16),
            dma((6,)), dma((8,)), dma((8,)), dma((4,)), dma((4,)),
            dma((12,)), dma((12,)), dma((15,)), dma((15,)),
        ],
        compiler_params=pltpu.CompilerParams(
            collective_id=1, has_side_effects=True, vmem_limit_bytes=VMEM_BYTES
        ),
        name="collect",
    )(slot_of, receivers, picks, pre_grad, send_w, recv_w)


def centered(weight):
    rows = weight[...].astype(F32)
    return (rows - mean(rows)).astype(BF16)


def layer_norm(hidden):
    center = hidden - mean(hidden)
    inv_std = lax.rsqrt(mean(center * center) + EPSILON)
    return center * inv_std, inv_std


def norm_back(grad_out, normed, inv_std):
    return inv_std * (grad_out - mean(grad_out) - normed * mean(grad_out * normed))


def layer_kernel(
    count, edge_gain, node_gain, slot_in, receivers_in, table_in, nodes_in, node_up_in, pre, edges, edge_up,
    out_in, self_in, node_in, aggr_in, node_out_in,
    node_new_out, edge_new, node_grad_out, edge_grad, pre_grad,
    pre_v, edges_v, up_v, new_v, grad_v, normed_v, slope_v, rstd_v, pre_grad_v, aggr, aggr_grad, out_c,
    slot_of, receivers, table, nodes, node_up, out_w, self_w, node_w, aggr_w, node_out, node_new, node_grad,
    load_sem, pre_sem, edges_sem, up_sem, new_sem, grad_sem, pre_grad_sem,
):
    def loaded(turn):
        at = turn_of(turn)
        return (
            pltpu.make_async_copy(pre.at[at], pre_v.at[at], pre_sem.at[turn]),
            pltpu.make_async_copy(edges.at[at], edges_v.at[at], edges_sem.at[turn]),
        )

    def raised(turn):
        at = turn_of(turn)
        return pltpu.make_async_copy(edge_up.at[at], up_v.at[at], up_sem.at[turn])

    sources = (
        (out_in, out_w), (slot_in, slot_of), (table_in, table), (receivers_in, receivers),
        (nodes_in, nodes), (node_up_in, node_up), (node_in, node_w), (aggr_in, aggr_w), (node_out_in, node_out),
        (self_in, self_w),
    )
    loads = [pltpu.make_async_copy(source, target, load_sem.at[at]) for at, (source, target) in enumerate(sources)]
    for copy in loads[:4]:
        copy.start()
    for turn in range(TURNS):
        for copy in loaded(turn):
            copy.start()
    for copy in loads[4:]:
        copy.start()
    for turn in range(TURNS):
        raised(turn).start()
    for copy in loads[:4]:
        copy.wait()

    out_c[...] = centered(out_w)
    node_row = lax.broadcasted_iota(jnp.int32, (NODES, WIDE), 0)
    slot_row = lax.broadcasted_iota(jnp.int32, (STEP, 1), 0)
    own_ids = [lane_ids(at * LANES, at * LANES + BLOCK) for at in range(3)]
    far_ids = [lane_ids(EXT + at * LANES, EXT + at * LANES + BLOCK) for at in range(PACKED // LANES)]
    aggr[...] = jnp.zeros_like(aggr)

    def live_of(step):
        return (slot_row + step * STEP < count[0, 0]).astype(F32)

    def stored(turn):
        at = turn_of(turn)
        return pltpu.make_async_copy(new_v.at[at], edge_new.at[at], new_sem.at[turn])

    def returned(turn):
        at = turn_of(turn)
        return (
            pltpu.make_async_copy(pre_grad_v.at[at], pre_grad.at[at], pre_grad_sem.at[turn]),
            pltpu.make_async_copy(grad_v.at[at], edge_grad.at[at], grad_sem.at[turn]),
        )

    def forward(turn, carry):
        for copy in loaded(turn):
            copy.wait()
        messages = []
        for step, at in enumerate(steps_of(turn)):
            before = pre_v[at] + dot(hot_rows(column(slot_of[0:1, at]), far_ids), table[...])
            gate = sigmoid(before)
            act = before * gate
            slope_v[at] = (gate + act * (1.0 - gate)).astype(BF16)
            center = dot(act.astype(BF16), out_c[...])
            rstd = live_of(turn * TURN + step) * lax.rsqrt(mean(center * center) + EPSILON)
            normed = center * rstd
            normed_v[at] = normed.astype(BF16)
            rstd_v[at] = jnp.broadcast_to(rstd, (STEP, LANES))
            message = (normed * edge_gain[...]).astype(BF16)
            new_v[at] = edges_v[at] + message
            messages.append(message)
        to_hot = onehot(jnp.broadcast_to(receivers[:, turn_of(turn)], (NODES, WIDE)) == node_row)
        aggr[...] += dot(to_hot, jnp.concatenate(messages, axis=0))
        stored(turn).start()
        return carry

    lax.fori_loop(0, TURNS, forward, 0)

    for copy in loads[4:]:
        copy.wait()
    node_rows = nodes[...]
    node_pre = dot(node_rows, node_w[...]) + dot(aggr[...].astype(BF16), aggr_w[...])
    gate = sigmoid(node_pre)
    act = node_pre * gate
    slope = gate + act * (1.0 - gate)
    normed, rstd = layer_norm(dot(act.astype(BF16), node_out[...]))
    node_new[...] = (node_rows.astype(F32) + normed * node_gain[...]).astype(BF16)
    up = node_up[...].astype(F32)
    hidden_grad = norm_back(up * node_gain[...], normed, rstd).astype(BF16)
    node_pre_grad = (dot_t(hidden_grad, node_out[...]) * slope).astype(BF16)
    node_grad[...] = up + dot_t(node_pre_grad, node_w[...])
    aggr_grad[...] = dot_t(node_pre_grad, aggr_w[...]).astype(BF16)
    outs = (
        pltpu.make_async_copy(node_new, node_new_out, load_sem.at[10]),
        pltpu.make_async_copy(node_grad, node_grad_out, load_sem.at[11]),
    )
    for copy in outs:
        copy.start()

    def backward(turn, carry):
        raised(turn).wait()
        for step, at in enumerate(steps_of(turn)):
            upstream = up_v[at].astype(F32)
            to_hot = hot_rows(column(receivers[:, at]), own_ids)
            grad = (upstream + dot(to_hot, aggr_grad[...])) * edge_gain[...]
            normed = normed_v[at].astype(F32)
            hidden_grad = (rstd_v[at][:, :1] * (grad - normed * mean(grad * normed))).astype(BF16)
            gone = dot_t(hidden_grad, out_c[...]).astype(BF16) * slope_v[at]
            pre_grad_v[at] = gone
            grad_v[at] = upstream + dot_t(gone, self_w[...])
        for copy in returned(turn):
            copy.start()
        return carry

    lax.fori_loop(0, TURNS, backward, 0)

    for copy in outs:
        copy.wait()
    for turn in range(TURNS):
        stored(turn).wait()
        for copy in returned(turn):
            copy.wait()


def layer(count, edge_gain, node_gain, *rows):
    vmem = pl.BlockSpec(memory_space=pltpu.VMEM)
    smem = pl.BlockSpec(memory_space=pltpu.SMEM)
    hbm = pl.BlockSpec(memory_space=pl.ANY)
    dma = pltpu.SemaphoreType.DMA
    return pl.pallas_call(
        layer_kernel,
        out_shape=(
            jax.ShapeDtypeStruct((NODES, D), BF16),
            jax.ShapeDtypeStruct((SLOTS, D), BF16),
            jax.ShapeDtypeStruct((NODES, D), F32),
            jax.ShapeDtypeStruct((SLOTS, D), F32),
            jax.ShapeDtypeStruct((SLOTS, D), BF16),
        ),
        in_specs=[smem, vmem, vmem] + [hbm] * len(rows),
        out_specs=(hbm,) * 5,
        scratch_shapes=[
            pltpu.VMEM((SLOTS, D), BF16),
            pltpu.VMEM((SLOTS, D), BF16),
            pltpu.VMEM((SLOTS, D), BF16),
            pltpu.VMEM((SLOTS, D), BF16),
            pltpu.VMEM((SLOTS, D), F32),
            pltpu.VMEM((SLOTS, D), BF16),
            pltpu.VMEM((SLOTS, D), BF16),
            pltpu.VMEM((SLOTS, LANES), F32),
            pltpu.VMEM((SLOTS, D), BF16),
            pltpu.VMEM((NODES, D), F32),
            pltpu.VMEM((NODES, D), BF16),
            pltpu.VMEM((D, D), BF16),
            pltpu.VMEM((8, SLOTS), jnp.int32),
            pltpu.VMEM((1, SLOTS), jnp.int32),
            pltpu.VMEM((PACKED, D), BF16),
            pltpu.VMEM((NODES, D), BF16),
            pltpu.VMEM((NODES, D), BF16),
        ]
        + [pltpu.VMEM((D, D), BF16)] * 5
        + [pltpu.VMEM((NODES, D), BF16), pltpu.VMEM((NODES, D), F32)]
        + [dma((12,))]
        + [dma((TURNS,))] * 6,
        compiler_params=pltpu.CompilerParams(vmem_limit_bytes=VMEM_BYTES),
        name="layer",
    )(count, edge_gain, node_gain, *rows)


def body(
    node_latents,
    edge_latents,
    senders,
    receivers,
    edge_count,
    edge_self_w,
    edge_send_w,
    edge_recv_w,
    edge_out_w,
    node_self_w,
    node_aggr_w,
    node_out_w,
    edge_gain,
    node_gain,
    node_upstream,
    edge_upstream,
):
    grid = node_latents.shape
    node_rows = node_latents.reshape(NODES, D)
    edges = edge_latents.reshape(SLOTS, D)
    to = receivers.reshape(1, SLOTS)
    pre, slot_of, picks, table = spread(
        node_latents, senders.reshape(1, SLOTS), to, node_rows, edges, edge_self_w, edge_send_w, edge_recv_w
    )
    node_new, edge_new, node_grad, edge_grad, pre_grad = layer(
        edge_count,
        edge_gain.reshape(1, D),
        node_gain.reshape(1, D),
        slot_of,
        to,
        table,
        node_rows,
        node_upstream.reshape(NODES, D),
        pre,
        edges,
        edge_upstream.reshape(SLOTS, D),
        edge_out_w,
        edge_self_w,
        node_self_w,
        node_aggr_w,
        node_out_w,
    )
    returned = collect(slot_of, to, picks, pre_grad, edge_send_w, edge_recv_w)
    return (
        node_new.reshape(grid),
        edge_new.reshape(edge_latents.shape),
        (node_grad + returned).reshape(grid),
        edge_grad.reshape(edge_latents.shape),
    )


def solution(mesh):
    tiles = P("lat", "lon", None, None)
    lists = P("lat", "lon", None)
    return jax.shard_map(
        body,
        mesh=mesh,
        in_specs=(tiles, tiles, lists, lists, P("lat", "lon")) + (P(),) * 9 + (tiles, tiles),
        out_specs=(tiles,) * 4,
        check_vma=False,
    )
```

```python
import jax
import jax.numpy as jnp
from jax import lax
from jax.experimental import pallas as pl
from jax.experimental.pallas import tpu as pltpu
from jax.sharding import PartitionSpec as P

MESH = pl.DeviceIdType.MESH
F32 = jnp.float32
BF16 = jnp.bfloat16
EPSILON = 1e-05

D = 512
BLOCK = 64
SLOTS = 3072
NODES = 384
EXT = 1280
OWNERS = 128
MEMBERS = 16
COARSE = OWNERS * MEMBERS
PER_OWNER = 8
PACKED = OWNERS * PER_OWNER
STEP = 512
STEPS = SLOTS // STEP
TURN = 2
TURNS = STEPS // TURN
WIDE = STEP * TURN
LANES = 128
GROUP = 16
GROUPS = OWNERS // GROUP
LONS = 32
SAME_CORE = 64
RIM = 14 * BLOCK
SIDES = 10 * BLOCK
VMEM_BYTES = 60 * 1024 * 1024


def dot(left, right):
    return jnp.dot(left, right, preferred_element_type=F32)


def dot_t(left, right):
    return lax.dot_general(left, right, (((1,), (1,)), ((), ())), preferred_element_type=F32)


def t_dot(left, right):
    return lax.dot_general(left, right, (((0,), (0,)), ((), ())), preferred_element_type=F32)


def onehot(mask):
    return jnp.where(mask, 1.0, 0.0).astype(BF16)


def mean(rows):
    return jnp.sum(rows, -1, keepdims=True) * (1.0 / D)


def sigmoid(pre):
    return 0.5 * jnp.tanh(0.5 * pre) + 0.5


def places():
    lat = lax.axis_index("lat")
    lon = lax.axis_index("lon")
    return lat, lon


def shifted(lat, lon, row, col):
    return {"lat": lax.rem(lat + row + 4, 4), "lon": lax.rem(lon + col + LONS, LONS)}


def rings(lat, lon):
    core, x, z = lat % 2, lon // 8, lon // 2 % 4
    y = lat // 2 * 2 + lon % 2
    near = z + core * (x - z)
    far = x + core * (z - x)

    def device(y_step, near_step, far_step):
        y_at = lax.rem(y + y_step, 4)
        x_at = lax.rem(x + far_step + core * (near_step - far_step), 4)
        z_at = lax.rem(z + near_step + core * (far_step - near_step), 4)
        return {"lat": y_at // 2 * 2 + core, "lon": x_at * 8 + z_at * 2 + y_at % 2}

    return core, y, near, far, device


PLANE = tuple((near, y) for near in (0, 1, 3, 2) for y in (0, 1, 3, 2) if near or y)


def greet(lat, lon, device):
    peers = [shifted(lat, lon, row, col) for row in (-1, 0, 1) for col in (-1, 0, 1) if row or col]
    peers += [device(y_step, near_step, 0) for near_step, y_step in PLANE]
    peers += [device(0, 0, step) for step in (1, 2, 3)]
    for peer in peers:
        pl.semaphore_signal(pltpu.get_barrier_semaphore(), inc=1, device_id=peer, device_id_type=MESH)
    return len(peers)


def reaches(lat, row):
    return jnp.logical_and(lat + row >= 0, lat + row < 4)


RIM_BASES = (0, 64, 128, 192, 256, 960, 1024, 1088, 1152, 1216, 320, 640, 576, 896)
CORE_BASES = (384, 448, 512, 704, 768, 832)
HALO = (
    ((0, -1), (None, 0), (12, 2)),
    ((0, 1), (None, 2), (10, 2)),
    ((-1, 0), (0, (0, 3)), (6, 3)),
    ((1, 0), (1, (0, 3)), (1, 3)),
    ((-1, -1), (0, (0, 1)), (9, 1)),
    ((-1, 1), (0, (2, 1)), (5, 1)),
    ((1, -1), (1, (0, 1)), (4, 1)),
    ((1, 1), (1, (2, 1)), (0, 1)),
)
BACK = (
    ((-1, 0), (1, 3), (3, 3)),
    ((1, 0), (6, 3), (0, 3)),
    ((0, -1), (10, 2), (8, 2)),
    ((0, 1), (12, 2), (6, 2)),
    ((-1, -1), (0, 1), (13, 1)),
    ((-1, 1), (4, 1), (12, 1)),
    ((1, -1), (5, 1), (11, 1)),
    ((1, 1), (9, 1), (10, 1)),
)


def place_of(owner):
    core = jnp.bitwise_and(jnp.right_shift(owner, 5), 1)
    y = jnp.right_shift(owner, 6) * 2 + jnp.bitwise_and(owner, 1)
    x = jnp.bitwise_and(jnp.right_shift(owner, 3), 3)
    z = jnp.bitwise_and(jnp.right_shift(owner, 1), 3)
    place = jnp.where(core == 0, x * 16 + z * 4, SAME_CORE + z * 16 + x * 4) + y
    return jnp.where(owner < 0, owner, place)


def rows_of(step, size=STEP):
    return pl.ds(pl.multiple_of(step * size, size), size)


def turn_of(turn):
    return rows_of(turn, WIDE)


def steps_of(turn):
    return [rows_of(turn * TURN + step) for step in range(TURN)]


def hot_rows(col, groups):
    return jnp.concatenate([onehot(col == ids) for ids in groups], axis=1)


def column(ids):
    return jnp.transpose(jnp.broadcast_to(ids, (LANES, STEP)))


def lane_ids(first, second):
    lane = lax.broadcasted_iota(jnp.int32, (STEP, LANES), 1)
    return lane + jnp.where(lane < BLOCK, first, second - BLOCK)


def row_ids(bases):
    row = lax.broadcasted_iota(jnp.int32, (len(bases) * BLOCK, 1), 0)
    block = jnp.right_shift(row, 6)
    start = jnp.zeros_like(row)
    for at, base in enumerate(bases):
        start = jnp.where(block == at, base - at * BLOCK, start)
    return row + start


def rank_slots(senders, slot_of, requests, picks):
    earlier = onehot(
        lax.broadcasted_iota(jnp.int32, (STEP, STEP), 0) < lax.broadcasted_iota(jnp.int32, (STEP, STEP), 1)
    )
    down = lax.broadcasted_iota(jnp.int32, (OWNERS, STEP), 0)
    requests[...] = jnp.zeros_like(requests)

    def rank_step(step, seen):
        at = rows_of(step)
        ids = senders[:, at]
        far = ids - EXT
        owner = place_of(jnp.right_shift(far, 4))
        flags = jnp.where(jnp.broadcast_to(owner, (OWNERS, STEP)) == down, 1.0, 0.0)
        flags_16 = flags.astype(BF16)
        before = dot(flags_16, earlier) + seen
        rank = jnp.sum(flags * before, 0, keepdims=True).astype(jnp.int32)
        slot_of[0:1, at] = jnp.where(far >= 0, EXT + owner * PER_OWNER + rank, ids)
        member = jnp.where(far >= 0, jnp.bitwise_and(far, MEMBERS - 1) + 1, 0).astype(F32)
        chosen = jnp.where(jnp.broadcast_to(rank, (OWNERS, STEP)) == down, jnp.broadcast_to(member, (OWNERS, STEP)), 0.0)
        requests[...] += dot_t(flags_16, chosen.astype(BF16))
        return seen + jnp.sum(flags, 1, keepdims=True)

    lax.fori_loop(0, STEPS, rank_step, jnp.zeros((OWNERS, 1), F32))
    wide = jnp.broadcast_to(requests[...][:, None, :], (OWNERS, PER_OWNER, LANES)).reshape(PACKED, LANES)
    at_row = jnp.bitwise_and(lax.broadcasted_iota(jnp.int32, (PACKED, LANES), 0), PER_OWNER - 1)
    at_lane = lax.broadcasted_iota(jnp.int32, (PACKED, LANES), 1)
    wanted = jnp.sum(jnp.where(at_row == at_lane, wide, 0.0), 1, keepdims=True).astype(jnp.int32)
    span = GROUP * MEMBERS
    rows_in = lax.broadcasted_iota(jnp.int32, (PACKED, span), 0)
    cols_in = lax.broadcasted_iota(jnp.int32, (PACKED, span), 1)
    same = jnp.bitwise_and(jnp.right_shift(rows_in, 3), GROUP - 1) == jnp.right_shift(cols_in, 4)
    named = wanted == jnp.bitwise_and(cols_in, MEMBERS - 1) + 1
    picks[...] = onehot(jnp.logical_and(same, named))


def spread_kernel(
    nodes, senders_in, receivers_in, node_rows_in, edges, self_w, send_w, recv_w,
    pre, slot_out, picks_out, table_out,
    coarse, rim, edges_v, pre_v, pre_out, weights_v, table, packed, requests, senders, receivers, node_rows, slot_of, picks,
    load_sem, out_sem, edges_sem, pre_sem, halo_send, halo_recv,
    plane_send, plane_recv, far_send, far_recv, pass_send, pass_recv, corner_send, corner_recv,
):
    lat, lon = places()
    core, y, near, far, device = rings(lat, lon)
    met = greet(lat, lon, device)
    loads = []
    sources = (
        (senders_in, senders), (receivers_in, receivers), (node_rows_in, node_rows),
        (recv_w, weights_v.at[0]), (send_w, weights_v.at[1]), (self_w, weights_v.at[2]),
    )
    for at, (source, target) in enumerate(sources):
        copy = pltpu.make_async_copy(source, target, load_sem.at[at])
        copy.start()
        loads.append(copy)

    base = core * SAME_CORE
    mine = base + far * 16 + near * 4 + y
    first = nodes.at[0, 0, pl.ds(0, MEMBERS)]
    kept = pltpu.make_async_copy(first, coarse.at[mine], load_sem.at[6])
    kept.start()
    pl.semaphore_wait(pltpu.get_barrier_semaphore(), met)

    def remote(source, target, sems, at, peer):
        return pltpu.make_async_remote_copy(
            src_ref=source,
            dst_ref=target,
            send_sem=sems[0].at[at],
            recv_sem=sems[1].at[at],
            device_id=peer,
            device_id_type=MESH,
        )

    plane = {}
    for near_step, y_step in PLANE:
        copy = remote(
            first, coarse.at[mine], (plane_send, plane_recv), near_step * 4 + y_step, device(y_step, near_step, 0)
        )
        copy.start()
        plane[near_step, y_step] = copy

    for turn in range(TURNS):
        at = turn_of(turn)
        pltpu.make_async_copy(edges.at[at], edges_v.at[at], edges_sem.at[turn]).start()

    loads[0].wait()
    rank_slots(senders, slot_of, requests, picks)
    outs = [
        pltpu.make_async_copy(slot_of, slot_out, out_sem.at[0]),
        pltpu.make_async_copy(picks, picks_out, out_sem.at[1]),
    ]
    for copy in outs:
        copy.start()
    @pl.when(lat == 0)
    def _():
        rim[0:5] = jnp.zeros((5, BLOCK, D), BF16)

    @pl.when(lat == 3)
    def _():
        rim[5:10] = jnp.zeros((5, BLOCK, D), BF16)

    for copy in plane.values():
        copy.wait_send()
    halos = []
    for at, ((row, col), (r, c), (to, size)) in enumerate(HALO):
        source = nodes.at[pl.ds(0, 2), c] if r is None else nodes.at[r, pl.ds(*c)]
        copy = remote(source, rim.at[pl.ds(to, size)], (halo_send, halo_recv), at, shifted(lat, lon, row, col))
        if row and col:
            sends, gets = lat == (2 if row < 0 else 1), lat == (1 if row < 0 else 2)
        elif row:
            sends, gets = reaches(lat, row), reaches(lat, -row)
        else:
            sends = gets = None
        copy.start() if sends is None else pl.when(sends)(copy.start)
        halos.append((sends, gets, copy))

    for copy in loads[1:]:
        copy.wait()
    table[0:NODES] = dot(node_rows[...], weights_v[0]).astype(BF16)
    table[NODES : 2 * NODES] = dot(node_rows[...], weights_v[1]).astype(BF16)
    core_ids = [lane_ids(CORE_BASES[at], CORE_BASES[at + 1]) for at in (0, 2, 4)]
    own_ids = [lane_ids(at * LANES, at * LANES + BLOCK) for at in range(3)]
    rim_ids = [lane_ids(RIM_BASES[at], RIM_BASES[at + 1]) for at in range(0, 14, 2)]

    def own_turn(turn, carry):
        whole = turn_of(turn)
        pltpu.make_async_copy(edges.at[whole], edges_v.at[whole], edges_sem.at[turn]).wait()
        for at in steps_of(turn):
            hot = jnp.concatenate(
                [hot_rows(column(receivers[:, at]), own_ids), hot_rows(column(slot_of[0:1, at]), core_ids)], axis=1
            )
            pre_v[at] = dot(edges_v[at], weights_v[2]) + dot(hot, table[: 2 * NODES])
        return carry

    def side_turn(turn, carry):
        for at in steps_of(turn):
            pre_v[at] += dot(hot_rows(column(slot_of[0:1, at]), rim_ids[5:]), table[SIDES:RIM])
        return carry

    def rim_turn(turn, carry):
        whole = turn_of(turn)
        for at in steps_of(turn):
            near_rows = dot(hot_rows(column(slot_of[0:1, at]), rim_ids[:5]), table[:SIDES])
            pre_out[at] = (pre_v[at] + near_rows).astype(BF16)
        pltpu.make_async_copy(pre_out.at[whole], pre.at[whole], pre_sem.at[turn]).start()
        return carry

    def piece(step):
        return coarse.at[pl.ds(base + far * 16 + lax.rem(near + 4 - step, 4) * 4, 4)]

    far_copies = {}

    def send_far(part):
        for y_step in range(4):
            if (part, y_step) in plane:
                plane[part, y_step].wait_recv()
        for step in (1, 3, 2):
            copy = remote(piece(part), piece(part), (far_send, far_recv), part * 3 + step - 1, device(0, 0, step))
            copy.start()
            far_copies[part, step] = copy

    partner = shifted(lat, lon, 1 - 2 * core, 0)
    passes = []

    def hand_over(step):
        if step:
            for part in range(4):
                far_copies[part, step].wait_recv()
        block = coarse.at[pl.ds(base + lax.rem(far + 4 - step, 4) * 16, 16)]
        copy = remote(block, block, (pass_send, pass_recv), step, partner)
        copy.start()
        passes.append(copy)

    def pack(group):
        at = pl.ds(pl.multiple_of(group * LANES, LANES), LANES)
        rows = dot(picks[at], coarse[pl.ds(group * GROUP, GROUP)].reshape(GROUP * MEMBERS, D)).astype(BF16)
        packed[at] = dot(rows, weights_v[1]).astype(BF16)

    lax.fori_loop(0, 1, own_turn, 0)
    kept.wait()
    send_far(0)
    for part in (1, 3, 2):
        send_far(part)
    hand_over(0)
    lax.fori_loop(1, TURNS, own_turn, 0)
    corners = []
    for _, _, copy in halos[:2]:
        copy.wait_recv()
    for at, (column_at, row_at) in enumerate(((11, 0), (13, 4))):
        copy = remote(
            rim.at[column_at - core], rim.at[row_at + 5 * core], (corner_send, corner_recv), at, partner
        )
        copy.start()
        corners.append(copy)
    table[SIDES:RIM] = dot(rim[10:14].reshape(4 * BLOCK, D), weights_v[1]).astype(BF16)
    lax.fori_loop(0, TURNS, side_turn, 0)
    for copy in corners:
        copy.wait_recv()
    for _, gets, copy in halos[2:]:
        pl.when(gets)(copy.wait_recv)
    table[:SIDES] = dot(rim[:10].reshape(SIDES, D), weights_v[1]).astype(BF16)
    hand_over(1)
    lax.fori_loop(0, 1, rim_turn, 0)
    hand_over(3)
    lax.fori_loop(1, 2, rim_turn, 0)
    hand_over(2)
    lax.fori_loop(2, TURNS, rim_turn, 0)
    for step in range(4):
        pack(core * 4 + step)
    for copy in passes:
        copy.wait_recv()
    for step in range(4):
        pack(4 - core * 4 + step)
    copy = pltpu.make_async_copy(packed, table_out, out_sem.at[2])
    copy.start()
    for turn in range(TURNS):
        at = turn_of(turn)
        pltpu.make_async_copy(pre_out.at[at], pre.at[at], pre_sem.at[turn]).wait()
    for copy in outs + [copy]:
        copy.wait()
    for sends, _, copy in halos:
        copy.wait_send() if sends is None else pl.when(sends)(copy.wait_send)
    for copy in list(far_copies.values()) + passes + corners:
        copy.wait_send()


def spread(nodes, senders, receivers, node_rows, edges, self_w, send_w, recv_w):
    hbm = pl.BlockSpec(memory_space=pl.ANY)
    dma = pltpu.SemaphoreType.DMA
    return pl.pallas_call(
        spread_kernel,
        out_shape=(
            jax.ShapeDtypeStruct((SLOTS, D), BF16),
            jax.ShapeDtypeStruct((8, SLOTS), jnp.int32),
            jax.ShapeDtypeStruct((PACKED, GROUP * MEMBERS), BF16),
            jax.ShapeDtypeStruct((PACKED, D), BF16),
        ),
        in_specs=[hbm] * 8,
        out_specs=(hbm,) * 4,
        scratch_shapes=[
            pltpu.VMEM((OWNERS, MEMBERS, D), BF16),
            pltpu.VMEM((14, BLOCK, D), BF16),
            pltpu.VMEM((SLOTS, D), BF16),
            pltpu.VMEM((SLOTS, D), F32),
            pltpu.VMEM((SLOTS, D), BF16),
            pltpu.VMEM((3, D, D), BF16),
            pltpu.VMEM((RIM, D), BF16),
            pltpu.VMEM((PACKED, D), BF16),
            pltpu.VMEM((OWNERS, LANES), F32),
            pltpu.VMEM((1, SLOTS), jnp.int32),
            pltpu.VMEM((1, SLOTS), jnp.int32),
            pltpu.VMEM((NODES, D), BF16),
            pltpu.VMEM((8, SLOTS), jnp.int32),
            pltpu.VMEM((PACKED, GROUP * MEMBERS), BF16),
            dma((7,)), dma((3,)), dma((TURNS,)), dma((TURNS,)), dma((8,)), dma((8,)),
            dma((16,)), dma((16,)), dma((12,)), dma((12,)), dma((4,)), dma((4,)), dma((2,)), dma((2,)),
        ],
        compiler_params=pltpu.CompilerParams(
            collective_id=0, has_side_effects=True, vmem_limit_bytes=VMEM_BYTES
        ),
        name="spread",
    )(nodes, senders, receivers, node_rows, edges, self_w, send_w, recv_w)


def collect_kernel(
    slot_in, receivers_in, picks_in, pre_grad, send_in, recv_in, returned,
    out, pre_grad_v, far_grad, paired, summed, far_in, plane_sum, plane_in, rim, rim_in, total,
    slot_of, receivers, picks, send_w, recv_w,
    load_sem, halo_send, halo_recv, pair_send, pair_recv, far_send, far_recv, plane_send, plane_recv,
):
    lat, lon = places()
    core, y, near, far, device = rings(lat, lon)
    met = greet(lat, lon, device)
    partner = shifted(lat, lon, 1 - 2 * core, 0)
    loads = []
    sources = (
        (slot_in, slot_of), (pre_grad, pre_grad_v), (picks_in, picks),
        (receivers_in, receivers), (recv_in, recv_w), (send_in, send_w),
    )
    for at, (source, target) in enumerate(sources):
        copy = pltpu.make_async_copy(source, target, load_sem.at[at])
        copy.start()
        loads.append(copy)

    def remote(source, target, sems, at, peer):
        return pltpu.make_async_remote_copy(
            src_ref=source,
            dst_ref=target,
            send_sem=sems[0].at[at],
            recv_sem=sems[1].at[at],
            device_id=peer,
            device_id_type=MESH,
        )

    @pl.when(lat == 0)
    def _():
        rim_in[0:3] = jnp.zeros((3, BLOCK, D), BF16)
        rim_in[10:12] = jnp.zeros((2, BLOCK, D), BF16)

    @pl.when(lat == 3)
    def _():
        rim_in[3:6] = jnp.zeros((3, BLOCK, D), BF16)
        rim_in[12:14] = jnp.zeros((2, BLOCK, D), BF16)

    def summed_by(ids, rows):
        mask = jnp.broadcast_to(ids, (rows.shape[0], SLOTS)) == rows
        return dot(onehot(mask), pre_grad_v[...])

    def gathered(ids, bases):
        return summed_by(ids, row_ids(bases))

    half = PACKED // 2

    def far_rows(side):
        rows = lax.broadcasted_iota(jnp.int32, (half, 1), 0) + (EXT + side * half)
        got = summed_by(slot_of[0:1, :], rows).astype(BF16)
        for group in range(4):
            wanted = picks[pl.ds(pl.multiple_of(side * half + group * LANES, LANES), LANES)]
            block = t_dot(wanted, got[group * LANES : (group + 1) * LANES]).astype(BF16)
            far_grad[side, group] = block.reshape(4, 4, MEMBERS, D)

    for copy in loads[:3]:
        copy.wait()
    slots = slot_of[0:1, :]
    rim[0:5] = gathered(slots, RIM_BASES[0:5]).astype(BF16).reshape(5, BLOCK, D)
    rim[5:10] = gathered(slots, RIM_BASES[5:10]).astype(BF16).reshape(5, BLOCK, D)
    rim[10:14] = gathered(slots, RIM_BASES[10:14]).astype(BF16).reshape(4, BLOCK, D)
    pl.semaphore_wait(pltpu.get_barrier_semaphore(), met)
    halos = []
    for at, ((row, col), (start, size), (to, _)) in enumerate(BACK):
        copy = remote(
            rim.at[pl.ds(start, size)], rim_in.at[pl.ds(to, size)], (halo_send, halo_recv), at, shifted(lat, lon, row, col)
        )
        if row:
            pl.when(reaches(lat, row))(copy.start)
        else:
            copy.start()
        halos.append((row, copy))
    far_rows(1 - core)
    pairs = []
    for part in (1, 3, 2, 0):
        at = lax.rem(far + part, 4)
        copy = remote(far_grad.at[1 - core, :, at], paired.at[:, at], (pair_send, pair_recv), part, partner)
        copy.start()
        pairs.append((part, copy))
    far_rows(core)

    copies = {}
    for part, copy in pairs:
        copy.wait_recv()
        at = lax.rem(near + part, 4)
        for step in (1, 3, 2, 0):
            to = lax.rem(far + step, 4)
            summed[to, at] = (far_grad[core, to, at].astype(F32) + paired[to, at].astype(F32)).astype(BF16)
            if step:
                slot = part * 3 + step - 1
                copies[part, step] = remote(
                    summed.at[to, at], far_in.at[slot], (far_send, far_recv), slot, device(0, 0, step)
                )
                copies[part, step].start()

    for copy in loads[3:]:
        copy.wait()
    total[...] = gathered(slots, CORE_BASES)
    got = gathered(receivers[...], tuple(range(0, NODES, BLOCK))).astype(BF16)
    out[...] = dot_t(got, recv_w[...])

    plane = []
    for part in (1, 3, 2, 0):
        for step in (1, 3, 2):
            copies[part, step].wait_recv()
        at = lax.rem(near + part, 4)
        for y_step in (1, 3, 2, 0):
            y_at = lax.rem(y + y_step, 4)
            acc = summed[far, at, y_at].astype(F32)
            for step in range(3):
                acc += far_in[part * 3 + step, y_at].astype(F32)
            if part or y_step:
                slot = part * 4 + y_step - 1
                plane_sum[slot] = acc.astype(BF16)
                sent = remote(
                    plane_sum.at[slot], plane_in.at[slot], (plane_send, plane_recv), slot, device(y_step, part, 0)
                )
                sent.start()
                plane.append(sent)

    for row, copy in halos:
        if row:
            pl.when(reaches(lat, -row))(copy.wait_recv)
        else:
            copy.wait_recv()

    def add(at, block):
        total[at * BLOCK : (at + 1) * BLOCK] += rim_in[block].astype(F32)

    for block in range(6):
        add(block, block)
    for at, block in ((0, 6), (3, 7), (2, 8), (5, 9), (0, 10), (2, 11), (3, 12), (5, 13)):
        add(at, block)
    out[BLOCK:] += dot_t(total[BLOCK:].astype(BF16), send_w[...])
    rest = pltpu.make_async_copy(out.at[pl.ds(BLOCK, NODES - BLOCK)], returned.at[pl.ds(BLOCK, NODES - BLOCK)], load_sem.at[6])
    rest.start()

    for copy in plane:
        copy.wait_recv()
    for slot in range(15):
        acc += plane_in[slot].astype(F32)
    total[:MEMBERS] += acc
    out[:BLOCK] += dot_t(total[:BLOCK].astype(BF16), send_w[...])
    head = pltpu.make_async_copy(out.at[pl.ds(0, BLOCK)], returned.at[pl.ds(0, BLOCK)], load_sem.at[7])
    head.start()
    for row, copy in halos:
        if row:
            pl.when(reaches(lat, row))(copy.wait_send)
        else:
            copy.wait_send()
    for copy in list(copies.values()) + plane + [copy for _, copy in pairs]:
        copy.wait_send()
    rest.wait()
    head.wait()


def collect(slot_of, receivers, picks, pre_grad, send_w, recv_w):
    hbm = pl.BlockSpec(memory_space=pl.ANY)
    dma = pltpu.SemaphoreType.DMA
    return pl.pallas_call(
        collect_kernel,
        out_shape=jax.ShapeDtypeStruct((NODES, D), F32),
        in_specs=[hbm] * 6,
        out_specs=hbm,
        scratch_shapes=[
            pltpu.VMEM((NODES, D), F32),
            pltpu.VMEM((SLOTS, D), BF16),
            pltpu.VMEM((2, 4, 4, 4, MEMBERS, D), BF16),
            pltpu.VMEM((4, 4, 4, MEMBERS, D), BF16),
            pltpu.VMEM((4, 4, 4, MEMBERS, D), BF16),
            pltpu.VMEM((12, 4, MEMBERS, D), BF16),
            pltpu.VMEM((15, MEMBERS, D), BF16),
            pltpu.VMEM((15, MEMBERS, D), BF16),
            pltpu.VMEM((14, BLOCK, D), BF16),
            pltpu.VMEM((14, BLOCK, D), BF16),
            pltpu.VMEM((NODES, D), F32),
            pltpu.VMEM((8, SLOTS), jnp.int32),
            pltpu.VMEM((1, SLOTS), jnp.int32),
            pltpu.VMEM((PACKED, GROUP * MEMBERS), BF16),
            pltpu.VMEM((D, D), BF16),
            pltpu.VMEM((D, D), BF16),
            dma((8,)), dma((8,)), dma((8,)), dma((4,)), dma((4,)),
            dma((12,)), dma((12,)), dma((15,)), dma((15,)),
        ],
        compiler_params=pltpu.CompilerParams(
            collective_id=1, has_side_effects=True, vmem_limit_bytes=VMEM_BYTES
        ),
        name="collect",
    )(slot_of, receivers, picks, pre_grad, send_w, recv_w)


def centered(weight):
    rows = weight[...].astype(F32)
    return (rows - mean(rows)).astype(BF16)


def layer_norm(hidden):
    center = hidden - mean(hidden)
    inv_std = lax.rsqrt(mean(center * center) + EPSILON)
    return center * inv_std, inv_std


def norm_back(grad_out, normed, inv_std):
    return inv_std * (grad_out - mean(grad_out) - normed * mean(grad_out * normed))


def layer_kernel(
    count, edge_gain, node_gain, slot_in, receivers_in, table_in, nodes_in, node_up_in, pre, edges, edge_up,
    out_in, self_in, node_in, aggr_in, node_out_in,
    node_new_out, edge_new, node_grad_out, edge_grad, pre_grad,
    pre_v, edges_v, up_v, new_v, grad_v, normed_v, slope_v, rstd_v, pre_grad_v, aggr, aggr_grad, out_c,
    slot_of, receivers, table, nodes, node_up, out_w, self_w, node_w, aggr_w, node_out, node_new, node_grad,
    load_sem, pre_sem, edges_sem, up_sem, new_sem, grad_sem, pre_grad_sem,
):
    def loaded(turn):
        at = turn_of(turn)
        return (
            pltpu.make_async_copy(pre.at[at], pre_v.at[at], pre_sem.at[turn]),
            pltpu.make_async_copy(edges.at[at], edges_v.at[at], edges_sem.at[turn]),
        )

    def raised(turn):
        at = turn_of(turn)
        return pltpu.make_async_copy(edge_up.at[at], up_v.at[at], up_sem.at[turn])

    sources = (
        (out_in, out_w), (slot_in, slot_of), (table_in, table), (receivers_in, receivers),
        (nodes_in, nodes), (node_up_in, node_up), (node_in, node_w), (aggr_in, aggr_w), (node_out_in, node_out),
        (self_in, self_w),
    )
    loads = [pltpu.make_async_copy(source, target, load_sem.at[at]) for at, (source, target) in enumerate(sources)]
    for copy in loads[:4]:
        copy.start()
    for turn in range(TURNS):
        for copy in loaded(turn):
            copy.start()
    for copy in loads[4:]:
        copy.start()
    for turn in range(TURNS):
        raised(turn).start()
    for copy in loads[:4]:
        copy.wait()

    out_c[...] = centered(out_w)
    node_row = lax.broadcasted_iota(jnp.int32, (NODES, WIDE), 0)
    slot_row = lax.broadcasted_iota(jnp.int32, (STEP, 1), 0)
    own_ids = [lane_ids(at * LANES, at * LANES + BLOCK) for at in range(3)]
    far_ids = [lane_ids(EXT + at * LANES, EXT + at * LANES + BLOCK) for at in range(PACKED // LANES)]
    aggr[...] = jnp.zeros_like(aggr)

    def live_of(step):
        return (slot_row + step * STEP < count[0, 0]).astype(F32)

    def stored(turn):
        at = turn_of(turn)
        return pltpu.make_async_copy(new_v.at[at], edge_new.at[at], new_sem.at[turn])

    def returned(turn):
        at = turn_of(turn)
        return (
            pltpu.make_async_copy(pre_grad_v.at[at], pre_grad.at[at], pre_grad_sem.at[turn]),
            pltpu.make_async_copy(grad_v.at[at], edge_grad.at[at], grad_sem.at[turn]),
        )

    def forward(turn, carry):
        for copy in loaded(turn):
            copy.wait()
        messages = []
        for step, at in enumerate(steps_of(turn)):
            before = pre_v[at] + dot(hot_rows(column(slot_of[0:1, at]), far_ids), table[...])
            gate = sigmoid(before)
            act = before * gate
            slope_v[at] = (gate + act * (1.0 - gate)).astype(BF16)
            center = dot(act.astype(BF16), out_c[...])
            rstd = live_of(turn * TURN + step) * lax.rsqrt(mean(center * center) + EPSILON)
            normed = center * rstd
            normed_v[at] = normed.astype(BF16)
            rstd_v[at] = jnp.broadcast_to(rstd, (STEP, LANES))
            message = (normed * edge_gain[...]).astype(BF16)
            new_v[at] = edges_v[at] + message
            messages.append(message)
        to_hot = onehot(jnp.broadcast_to(receivers[:, turn_of(turn)], (NODES, WIDE)) == node_row)
        aggr[...] += dot(to_hot, jnp.concatenate(messages, axis=0))
        stored(turn).start()
        return carry

    lax.fori_loop(0, TURNS, forward, 0)

    for copy in loads[4:]:
        copy.wait()
    node_rows = nodes[...]
    node_pre = dot(node_rows, node_w[...]) + dot(aggr[...].astype(BF16), aggr_w[...])
    gate = sigmoid(node_pre)
    act = node_pre * gate
    slope = gate + act * (1.0 - gate)
    normed, rstd = layer_norm(dot(act.astype(BF16), node_out[...]))
    node_new[...] = (node_rows.astype(F32) + normed * node_gain[...]).astype(BF16)
    up = node_up[...].astype(F32)
    hidden_grad = norm_back(up * node_gain[...], normed, rstd).astype(BF16)
    node_pre_grad = (dot_t(hidden_grad, node_out[...]) * slope).astype(BF16)
    node_grad[...] = up + dot_t(node_pre_grad, node_w[...])
    aggr_grad[...] = dot_t(node_pre_grad, aggr_w[...]).astype(BF16)
    outs = (
        pltpu.make_async_copy(node_new, node_new_out, load_sem.at[10]),
        pltpu.make_async_copy(node_grad, node_grad_out, load_sem.at[11]),
    )
    for copy in outs:
        copy.start()

    def backward(turn, carry):
        raised(turn).wait()
        for step, at in enumerate(steps_of(turn)):
            upstream = up_v[at].astype(F32)
            to_hot = hot_rows(column(receivers[:, at]), own_ids)
            grad = (upstream + dot(to_hot, aggr_grad[...])) * edge_gain[...]
            normed = normed_v[at].astype(F32)
            hidden_grad = (rstd_v[at][:, :1] * (grad - normed * mean(grad * normed))).astype(BF16)
            gone = dot_t(hidden_grad, out_c[...]).astype(BF16) * slope_v[at]
            pre_grad_v[at] = gone
            grad_v[at] = upstream + dot_t(gone, self_w[...])
        for copy in returned(turn):
            copy.start()
        return carry

    lax.fori_loop(0, TURNS, backward, 0)

    for copy in outs:
        copy.wait()
    for turn in range(TURNS):
        stored(turn).wait()
        for copy in returned(turn):
            copy.wait()


def layer(count, edge_gain, node_gain, *rows):
    vmem = pl.BlockSpec(memory_space=pltpu.VMEM)
    smem = pl.BlockSpec(memory_space=pltpu.SMEM)
    hbm = pl.BlockSpec(memory_space=pl.ANY)
    dma = pltpu.SemaphoreType.DMA
    return pl.pallas_call(
        layer_kernel,
        out_shape=(
            jax.ShapeDtypeStruct((NODES, D), BF16),
            jax.ShapeDtypeStruct((SLOTS, D), BF16),
            jax.ShapeDtypeStruct((NODES, D), F32),
            jax.ShapeDtypeStruct((SLOTS, D), F32),
            jax.ShapeDtypeStruct((SLOTS, D), BF16),
        ),
        in_specs=[smem, vmem, vmem] + [hbm] * len(rows),
        out_specs=(hbm,) * 5,
        scratch_shapes=[
            pltpu.VMEM((SLOTS, D), BF16),
            pltpu.VMEM((SLOTS, D), BF16),
            pltpu.VMEM((SLOTS, D), BF16),
            pltpu.VMEM((SLOTS, D), BF16),
            pltpu.VMEM((SLOTS, D), F32),
            pltpu.VMEM((SLOTS, D), BF16),
            pltpu.VMEM((SLOTS, D), BF16),
            pltpu.VMEM((SLOTS, LANES), F32),
            pltpu.VMEM((SLOTS, D), BF16),
            pltpu.VMEM((NODES, D), F32),
            pltpu.VMEM((NODES, D), BF16),
            pltpu.VMEM((D, D), BF16),
            pltpu.VMEM((8, SLOTS), jnp.int32),
            pltpu.VMEM((1, SLOTS), jnp.int32),
            pltpu.VMEM((PACKED, D), BF16),
            pltpu.VMEM((NODES, D), BF16),
            pltpu.VMEM((NODES, D), BF16),
        ]
        + [pltpu.VMEM((D, D), BF16)] * 5
        + [pltpu.VMEM((NODES, D), BF16), pltpu.VMEM((NODES, D), F32)]
        + [dma((12,))]
        + [dma((TURNS,))] * 6,
        compiler_params=pltpu.CompilerParams(vmem_limit_bytes=VMEM_BYTES),
        name="layer",
    )(count, edge_gain, node_gain, *rows)


def body(
    node_latents,
    edge_latents,
    senders,
    receivers,
    edge_count,
    edge_self_w,
    edge_send_w,
    edge_recv_w,
    edge_out_w,
    node_self_w,
    node_aggr_w,
    node_out_w,
    edge_gain,
    node_gain,
    node_upstream,
    edge_upstream,
):
    grid = node_latents.shape
    node_rows = node_latents.reshape(NODES, D)
    edges = edge_latents.reshape(SLOTS, D)
    to = receivers.reshape(1, SLOTS)
    pre, slot_of, picks, table = spread(
        node_latents, senders.reshape(1, SLOTS), to, node_rows, edges, edge_self_w, edge_send_w, edge_recv_w
    )
    node_new, edge_new, node_grad, edge_grad, pre_grad = layer(
        edge_count,
        edge_gain.reshape(1, D),
        node_gain.reshape(1, D),
        slot_of,
        to,
        table,
        node_rows,
        node_upstream.reshape(NODES, D),
        pre,
        edges,
        edge_upstream.reshape(SLOTS, D),
        edge_out_w,
        edge_self_w,
        node_self_w,
        node_aggr_w,
        node_out_w,
    )
    returned = collect(slot_of, to, picks, pre_grad, edge_send_w, edge_recv_w)
    return (
        node_new.reshape(grid),
        edge_new.reshape(edge_latents.shape),
        (node_grad + returned).reshape(grid),
        edge_grad.reshape(edge_latents.shape),
    )


def solution(mesh):
    tiles = P("lat", "lon", None, None)
    lists = P("lat", "lon", None)
    return jax.shard_map(
        body,
        mesh=mesh,
        in_specs=(tiles, tiles, lists, lists, P("lat", "lon")) + (P(),) * 9 + (tiles, tiles),
        out_specs=(tiles,) * 4,
        check_vma=False,
    )
```
